32 devices in a mesh: lon: 8 (over z, y), lat: 4 (over x, core).
Axes of the slice: x: 2, y: 2, z: 4, core: 2. Of those that a mesh axis runs over, the one named last changes fastest.
Arguments:
- forcing: float32 [256, 2048], P('lat', 'lon'), may hold values from -27 to 27
- surface_term: float32 [256, 2048], P('lat', 'lon'), may hold values from 0.001 to 0.025
- sea_cells: int32 [256, 2048], P('lat', 'lon'), may hold values from 0 to 1, as said below
- levels: int32 [256, 2048], P('lat', 'lon'), may hold values from 4 to 60
Outputs:
- solution: float32 [256, 2048], P('lat', 'lon')
- residual: float32 [256, 2048], P('lat', 'lon')
The draws below stay inside these ranges and needn't reach their ends.
Inputs may be any that keep to these rules, and one draw needn't show every extreme that they name: `sea_cells`: land (0) lies only at cells whose row and longitude index, counted from 0, are both even.
All inputs are finite; a program needn't handle non-finite values.
Results may differ from the reference program's by a relative error of at most 0.0003.
Values sent between devices are 32-bit elements; how exact they have to be, the bound alone decides.
No kernel may reach another device: no remote copies, remote signals or barrier semaphores. Data moves between devices by JAX's collectives and lax.ppermute only.
A program may use at most 64 MiB of HBM per device.

```python
import math
import jax
import jax.numpy as jnp

LEVELS = 3
SWEEPS = 2
BOTTOM_ITERS = 6
VLEV = 60
NX = 2048
NY = 256


LOG_THREE = math.log(3.0)


def draw_forcing(key, part):
    base = jax.random.fold_in(key, 101)
    keys = jax.random.split(base, 3)
    cols = jnp.arange(NX, dtype=jnp.float32)[None, :] / NX
    row_scale = jnp.exp(jax.random.uniform(keys[1], (NY, 1), jnp.float32, -1.15, 1.15))
    col_scale = jnp.exp(jax.random.uniform(keys[2], (1, NX), jnp.float32, -1.15, 1.15))
    rough = jnp.clip(jax.random.normal(keys[0], (NY, NX), jnp.float32), -4.0, 4.0)
    trend = jnp.exp(0.5 * LOG_THREE * (cols - 0.5))
    return 0.5 * rough * row_scale * col_scale * trend


def draw_surface_term(key, part):
    base = jax.random.fold_in(key, 202)
    keys = jax.random.split(base, 2)
    cols = jnp.arange(NX, dtype=jnp.float32)[None, :] / NX
    rows = jnp.arange(NY, dtype=jnp.float32)[:, None] / NY
    phases = jax.random.uniform(keys[1], (2,), jnp.float32, 0.0, 2.0 * math.pi)
    region = jnp.cos(6.0 * math.pi * cols + phases[0]) * jnp.cos(math.pi * rows + phases[1])
    single = jax.random.uniform(keys[0], (NY, NX), jnp.float32, -1.0, 1.0)
    return 0.006 * jnp.exp(0.8 * single + 0.6 * region)


def draw_sea_cells(key, part):
    base = jax.random.fold_in(key, 303)
    rows = jnp.arange(NY, dtype=jnp.int32)[:, None]
    cols = jnp.arange(NX, dtype=jnp.int32)[None, :]
    lattice = (rows % 2 == 0) & (cols % 2 == 0)
    picked = jax.random.randint(base, (NY, NX), 0, 5)
    land = lattice & (picked < 4)
    return jnp.where(land, 0, 1).astype(jnp.int32)


def place_ends(result, own_key, least, high):
    dims = result.shape
    place = [jax.random.randint(jax.random.fold_in(own_key, axis), (), 0, dims[axis]) for axis in range(len(dims))]
    result = result.at[tuple(place)].set(least)
    longest = dims.index(max(dims))
    place[longest] = (place[longest] + 1) % dims[longest]
    return result.at[tuple(place)].set(high)


def setup_inputs(seed: int = 0) -> dict:
    key_of = jax.random.split(jax.random.key(seed), 5)
    forcing = draw_forcing(jax.random.fold_in(key_of[4], 71), 0)
    surface_term = draw_surface_term(jax.random.fold_in(key_of[4], 71), 0)
    sea_cells = draw_sea_cells(jax.random.fold_in(key_of[4], 71), 0)
    levels = place_ends(jax.random.randint(key_of[3], (NY, NX), 4, VLEV + 1), jax.random.fold_in(key_of[3], 1), 4, VLEV).astype(jnp.int32)
    return dict(forcing=forcing, surface_term=surface_term, sea_cells=sea_cells, levels=levels)


DAMPING = 0.8
ROW_STEP = 150.0 / 8640.0
BAND_SOUTH = -50.0


def depth_of(levels, sea_mask):
    layers = levels.astype(jnp.float32)
    return sea_mask * ((layers + layers * (layers - 1.0) / 20.0) / 200.0)


def metric(first_row, row_count):
    row_index = first_row + jnp.arange(row_count, dtype=jnp.float32)[:, None]
    center = jnp.cos(jnp.deg2rad(BAND_SOUTH + ROW_STEP * (row_index + 0.5)))
    northern = jnp.cos(jnp.deg2rad(BAND_SOUTH + ROW_STEP * (row_index + 1.0)))
    return center, northern


def stencil(field, east_val, west_val, north_val, south_val, coeffs):
    return coeffs[4] * field - (coeffs[0] * east_val + coeffs[1] * west_val + coeffs[2] * north_val + coeffs[3] * south_val)


def coarsen(east_face, north_face, source_term, sea_mask):
    east_next = east_face[0::2, 1::2] + east_face[1::2, 1::2]
    north_next = north_face[1::2, 0::2] + north_face[1::2, 1::2]
    source_next = source_term[0::2, 0::2] + source_term[1::2, 0::2] + source_term[0::2, 1::2] + source_term[1::2, 1::2]
    mask_next = jnp.maximum(jnp.maximum(sea_mask[0::2, 0::2], sea_mask[1::2, 0::2]), jnp.maximum(sea_mask[0::2, 1::2], sea_mask[1::2, 1::2]))
    return east_next, north_next, source_next, mask_next


def restrict(field):
    return field[0::2, 0::2] + field[1::2, 0::2] + field[0::2, 1::2] + field[1::2, 1::2]


def prolong(field, sea_mask):
    return jnp.repeat(jnp.repeat(field, 2, axis=0), 2, axis=1) * sea_mask


def with_diagonal(east_face, west_face, north_face, south_face, source_term, sea_mask):
    diagonal = sea_mask * (source_term + east_face + west_face + north_face + south_face) + (1.0 - sea_mask)
    return (east_face, west_face, north_face, south_face, diagonal, 1.0 / diagonal)


def shifted(field):
    zero_row = jnp.zeros_like(field[:1])
    east_val = jnp.roll(field, -1, axis=1)
    west_val = jnp.roll(field, 1, axis=1)
    north_val = jnp.concatenate([field[1:], zero_row], axis=0)
    south_val = jnp.concatenate([zero_row, field[:-1]], axis=0)
    return east_val, west_val, north_val, south_val


def apply_op(field, coeffs):
    east_val, west_val, north_val, south_val = shifted(field)
    return stencil(field, east_val, west_val, north_val, south_val, coeffs)


def finish(east_face, north_face, source_term, sea_mask):
    west_face = jnp.roll(east_face, 1, axis=1)
    south_face = jnp.concatenate([jnp.zeros_like(north_face[:1]), north_face[:-1]], axis=0)
    return with_diagonal(east_face, west_face, north_face, south_face, source_term, sea_mask)


def smooth(field, source, coeffs):
    return field + DAMPING * coeffs[5] * (source - apply_op(field, coeffs))


def reference(forcing, surface_term, sea_cells, levels):
    sea_mask = sea_cells.astype(jnp.float32)
    depth = depth_of(levels, sea_mask)
    center, northern = metric(0.0, NY)
    east_depth, west_depth, north_depth, south_depth = shifted(depth)
    east_face = jnp.minimum(depth, east_depth) / center
    north_face = jnp.minimum(depth, north_depth) * northern
    source_term = surface_term * center * sea_mask
    coeff_list = []
    mask_list = []
    for level_index in range(LEVELS + 1):
        coeff_list.append(finish(east_face, north_face, source_term, sea_mask))
        mask_list.append(sea_mask)
        if level_index < LEVELS:
            east_face, north_face, source_term, sea_mask = coarsen(east_face, north_face, source_term, sea_mask)
    source = forcing * mask_list[0]
    first_source = source
    sources = []
    iterates = []
    for level_index in range(LEVELS):
        coeffs = coeff_list[level_index]
        field = DAMPING * coeffs[5] * source
        for sweep_index in range(SWEEPS - 1):
            field = smooth(field, source, coeffs)
        sources.append(source)
        iterates.append(field)
        source = restrict(source - apply_op(field, coeffs))
    coeffs = coeff_list[LEVELS]
    iterate = jnp.zeros_like(source)
    remain = source
    direction = source
    norm_now = jnp.sum(remain * remain)
    for sweep_index in range(BOTTOM_ITERS):
        image = apply_op(direction, coeffs)
        step_size = norm_now / jnp.sum(direction * image)
        iterate = iterate + step_size * direction
        remain = remain - step_size * image
        norm_next = jnp.sum(remain * remain)
        direction = remain + (norm_next / norm_now) * direction
        norm_now = norm_next
    correction = iterate
    for level_index in range(LEVELS - 1, -1, -1):
        coeffs = coeff_list[level_index]
        field = iterates[level_index] + prolong(correction, mask_list[level_index])
        for sweep_index in range(SWEEPS):
            field = smooth(field, sources[level_index], coeffs)
        correction = field
    residual = first_source - apply_op(correction, coeff_list[0])
    return correction, residual
```

```python
import functools

import jax
import jax.numpy as jnp
from jax import lax
from jax.experimental import pallas as pl
from jax.experimental.pallas import tpu as pltpu
from jax.sharding import PartitionSpec as P

LEVELS = 3
SWEEPS = 2
BOTTOM_ITERS = 6

DAMPING = 0.8
ROW_STEP = 150.0 / 8640.0
BAND_SOUTH = -50.0

HALO = 32
LANES = 128
TILE = 8
FIELDS = 3
VMEM = pltpu.VMEM


def iota(shape, dim):
    return lax.broadcasted_iota(jnp.int32, shape, dim)


def lane_shift(field, count):
    width = field.shape[1]
    return pltpu.roll(field, (-count) % width, 1)


def row_shift(field, count):
    height = field.shape[0]
    return pltpu.roll(field, (-count) % height, 0)


def operator(field, east_face, north_face, diagonal, stride):
    side = east_face * lane_shift(field, stride) + lane_shift(east_face * field, -stride)
    ends = north_face * row_shift(field, 1) + row_shift(north_face * field, -1)
    return diagonal * field - (side + ends)


def level_diagonal(east_face, north_face, source_term, stride):
    total = source_term + (
        (east_face + lane_shift(east_face, -stride)) + (north_face + row_shift(north_face, -1))
    )
    return jnp.where(source_term > 0.0, total, 1.0)


def descend(where_ref, own_ref, lat_near_ref, lat_far_ref, lon_near_ref, lon_far_ref, scale_ref,
            pack_ref, *rest):
    level_refs = [rest[5 * i : 5 * i + 5] for i in range(LEVELS)]
    mask_ref, grid_ref, fold_ref = rest[5 * LEVELS :]
    lon_index = where_ref[0]
    lon_odd = lax.rem(lon_index, 2)
    lat_odd = lax.rem(where_ref[1], 2)
    rows, cols = own_ref.shape[1], own_ref.shape[2]
    height = rows + 2 * HALO
    width = cols + LANES
    near_row = rows + pl.multiple_of(lat_odd * HALO, HALO)
    far_row = rows + pl.multiple_of((1 - lat_odd) * HALO, HALO)
    lane = iota((TILE, LANES), 1)
    slot = lane // HALO
    for part, (rows_at, count, near, far, body) in enumerate((
        (0, rows, lon_near_ref, lon_far_ref, own_ref),
        (near_row, HALO, None, None, lat_near_ref),
        (far_row, HALO, None, None, lat_far_ref),
    )):
        for f in range(FIELDS):
            if part == 0:
                grid_ref[f, pl.ds(0, rows), pl.ds(0, cols)] = body[f]
            else:
                grid_ref[f, pl.ds(rows_at, count), pl.ds(0, cols)] = body[:, f * cols : (f + 1) * cols]
        if part == 0:
            near_val, far_val = near[...], far[...]
        else:
            near_val = body[:, FIELDS * cols : FIELDS * cols + LANES]
            far_val = body[:, FIELDS * cols + LANES :]
        odd = jnp.broadcast_to(lon_odd, near_val.shape) > 0
        east_val = jnp.where(odd, far_val, near_val)
        west_val = jnp.where(odd, near_val, far_val)
        slots = iota(near_val.shape, 1) // HALO
        for f in range(FIELDS):
            both = jnp.where(
                slots == f, east_val, jnp.where(slots == (f + 3) % 4, west_val, 0.0)
            )
            grid_ref[f, pl.ds(rows_at, count), pl.ds(cols, LANES)] = lane_shift(both, f * HALO)

    depth = grid_ref[0]
    inverse_center = jnp.concatenate([scale_ref[0]] * (width // LANES), axis=1)
    northern = jnp.concatenate([scale_ref[1]] * (width // LANES), axis=1)
    east_face = jnp.minimum(depth, lane_shift(depth, 1)) * inverse_center
    north_face = jnp.minimum(depth, row_shift(depth, 1)) * northern
    source_term = grid_ref[1]
    source = grid_ref[2]
    mask_ref[...] = jnp.where(source_term > 0.0, 1.0, 0.0)
    for level in range(LEVELS):
        stride = 1 << level
        diagonal = level_diagonal(east_face, north_face, source_term, stride)
        inverse = DAMPING / diagonal
        field = inverse * source
        for _ in range(SWEEPS - 1):
            field = field + inverse * (source - operator(field, east_face, north_face, diagonal, stride))
        image = source - operator(field, east_face, north_face, diagonal, stride)
        east_ref, north_ref, diagonal_ref, source_ref, field_ref = level_refs[level]
        east_ref[...] = east_face
        north_ref[...] = north_face
        diagonal_ref[...] = diagonal
        source_ref[...] = source
        field_ref[...] = field
        half = height >> (level + 1)
        even = pl.ds(0, half, stride=2)
        odd_rows = pl.ds(1, half, stride=2)

        def put(slot_index, value):
            for c in range(width // LANES):
                fold_ref[slot_index, c, pl.ds(0, 2 * half), :] = value[:, c * LANES : (c + 1) * LANES]

        def get(slot_index, which):
            return jnp.concatenate(
                [fold_ref[slot_index, c, which, :] for c in range(width // LANES)], axis=1
            )

        put(0, east_face)
        put(1, north_face)
        put(2, source_term)
        put(3, image)
        east_sum = get(0, even) + get(0, odd_rows)
        east_face = lane_shift(east_sum, stride)
        north_odd = get(1, odd_rows)
        north_face = north_odd + lane_shift(north_odd, stride)
        term_sum = get(2, even) + get(2, odd_rows)
        source_term = term_sum + lane_shift(term_sum, stride)
        image_sum = get(3, even) + get(3, odd_rows)
        source = image_sum + lane_shift(image_sum, stride)

    stride = 1 << LEVELS
    bottom_width = cols // stride
    per_column = LANES // stride
    cell = lane % bottom_width
    pick = (cell % per_column) * stride
    packed = jnp.zeros((TILE, LANES), jnp.float32)
    turn = lax.rem(lane // bottom_width + (LANES // bottom_width) - lax.rem(lon_index, LANES // bottom_width),
                   LANES // bottom_width)
    for f, value in enumerate((source, east_face, north_face, source_term)):
        flat = jnp.zeros((TILE, LANES), jnp.float32)
        for c in range(cols // LANES):
            taken = jnp.take_along_axis(value[:TILE, c * LANES : (c + 1) * LANES], pick, axis=1)
            flat = jnp.where(cell // per_column == c, taken, flat)
        packed = jnp.where(turn == f, flat, packed)
    pack_ref[...] = packed


def total(value):
    height, width = value.shape
    parts = [
        value[r : r + TILE, c : c + LANES]
        for r in range(0, height, TILE)
        for c in range(0, width, LANES)
    ]
    while len(parts) > 1:
        parts = [parts[i] + parts[i + 1] if i + 1 < len(parts) else parts[i] for i in range(0, len(parts), 2)]
    return jnp.sum(jnp.sum(parts[0], axis=0, keepdims=True), axis=1, keepdims=True)


def ascend(lat_count, lon_count, where_ref, blocks_ref, *rest):
    level_refs = [rest[5 * i : 5 * i + 5] for i in range(LEVELS)]
    mask_ref, solution_ref, residual_ref, window_ref, fold_ref = rest[5 * LEVELS :]
    lon_index = where_ref[0]
    lat_index = where_ref[1]
    rows, cols = solution_ref.shape
    height = rows + 2 * HALO
    width = cols + LANES
    stride = 1 << LEVELS
    bottom_rows = rows // stride
    bottom_width = cols // stride
    group = LANES // bottom_width
    slot = iota((bottom_rows, LANES), 1) // bottom_width
    fields = []
    for f in range(4):
        strips = []
        for a in range(lat_count):
            pieces = []
            for c in range(lon_count // group):
                merged = None
                for j in range(group):
                    block = blocks_ref[(c * group + j) * lat_count + a]
                    merged = block if merged is None else jnp.where(slot == (f + j) % group, block, merged)
                pieces.append(lane_shift(merged, f * bottom_width))
            strips.append(jnp.concatenate(pieces, axis=1))
        fields.append(jnp.concatenate(strips, axis=0))
    source, east_face, north_face, source_term = fields
    diagonal = level_diagonal(east_face, north_face, source_term, 1)

    iterate = jnp.zeros_like(source)
    remain = source
    direction = source
    norm_now = total(remain * remain)
    for _ in range(BOTTOM_ITERS):
        image = operator(direction, east_face, north_face, diagonal, 1)
        step_size = norm_now / total(direction * image)
        iterate = iterate + step_size * direction
        remain = remain - step_size * image
        norm_next = total(remain * remain)
        direction = remain + (norm_next / norm_now) * direction
        norm_now = norm_next

    bottom_height = lat_count * bottom_rows
    zero_tile = jnp.zeros((TILE, lon_count * bottom_width), jnp.float32)
    window_ref[pl.ds(0, TILE), :] = zero_tile
    window_ref[pl.ds(TILE, bottom_height), :] = iterate
    window_ref[pl.ds(TILE + bottom_height, TILE), :] = zero_tile
    start = pl.multiple_of(lat_index * bottom_rows, TILE)
    strip = window_ref[pl.ds(start, 3 * TILE), :]
    margin = LANES // 2 // stride
    whole_width = lon_count * bottom_width
    shift = lax.rem(margin - lon_index * bottom_width + whole_width, whole_width)
    strip = pltpu.roll(strip, shift, 1)[:, :LANES]
    south, own, north = strip[:TILE], strip[TILE : 2 * TILE], strip[2 * TILE :]
    halo_rows = HALO // stride
    row = iota((TILE, LANES), 0)
    lower = jnp.where(row < halo_rows, north, south)
    lane = iota((TILE, LANES), 1)
    parts = []
    for c in range(width // LANES):
        if c < cols // LANES:
            pick = margin + (c * LANES + lane) // stride
        else:
            pick = jnp.where(
                lane < LANES // 2, margin + bottom_width + lane // stride, (lane - LANES // 2) // stride
            )
        parts.append(jnp.concatenate(
            [jnp.take_along_axis(own, pick, axis=1), jnp.take_along_axis(lower, pick, axis=1)], axis=0
        ))
    correction = jnp.concatenate(parts, axis=1)

    for level in range(LEVELS - 1, -1, -1):
        stride = 1 << level
        east_ref, north_ref, diagonal_ref, source_ref, field_ref = level_refs[level]
        half = height >> (level + 1)
        for c in range(width // LANES):
            piece = correction[:, c * LANES : (c + 1) * LANES]
            fold_ref[c, pl.ds(0, half, stride=2), :] = piece
            fold_ref[c, pl.ds(1, half, stride=2), :] = piece
        spread = jnp.concatenate([fold_ref[c, pl.ds(0, 2 * half), :] for c in range(width // LANES)], axis=1)
        if level < LEVELS - 1:
            lanes = iota(spread.shape, 1)
            spread = jnp.where(lax.rem(lanes // stride, 2) == 0, spread, lane_shift(spread, -stride))
        east_face, north_face, diagonal = east_ref[...], north_ref[...], diagonal_ref[...]
        source = source_ref[...]
        field = field_ref[...]
        if level == 0:
            spread = mask_ref[...] * spread
        field = field + spread
        inverse = DAMPING / diagonal
        for _ in range(SWEEPS):
            field = field + inverse * (source - operator(field, east_face, north_face, diagonal, stride))
        correction = field
    solution_ref[...] = correction[:rows, :cols]
    final = source - operator(correction, east_face, north_face, diagonal, 1)
    residual_ref[...] = final[:rows, :cols]


def metric(first_row, row_count):
    row_index = first_row + jnp.arange(row_count, dtype=jnp.float32)[:, None]
    center = jnp.cos(jnp.deg2rad(BAND_SOUTH + ROW_STEP * (row_index + 0.5)))
    northern = jnp.cos(jnp.deg2rad(BAND_SOUTH + ROW_STEP * (row_index + 1.0)))
    return center, northern


def swap_pairs(count, first, periodic):
    pairs = []
    for i in range(first, count, 2):
        j = i + 1
        if j < count or periodic:
            pairs += [(i, j % count), (j % count, i)]
    return pairs


def on_device(lat_count, lon_count, forcing, surface_term, sea_cells, levels):
    rows, cols = forcing.shape
    height, width = rows + 2 * HALO, cols + LANES
    lon_index = lax.axis_index("lon").astype(jnp.int32)
    lat_index = lax.axis_index("lat").astype(jnp.int32)
    where = jnp.stack([lon_index, lat_index])
    lon_odd, lat_odd = lon_index % 2, lat_index % 2
    sea_mask = sea_cells.astype(jnp.float32)
    layers = levels.astype(jnp.float32)
    depth = sea_mask * ((layers + layers * (layers - 1.0) / 20.0) / 200.0)
    first_row = (lat_index * rows).astype(jnp.float32)
    center, _ = metric(first_row, rows)
    own = jnp.stack([depth, surface_term * center * sea_mask, forcing * sea_mask])

    edge = own[:, :, :HALO]
    blank = jnp.zeros((rows, HALO), jnp.float32)
    west_edge = jnp.concatenate([edge[0], edge[1], edge[2], blank], axis=1)
    edge = own[:, :, cols - HALO :]
    east_edge = jnp.concatenate([edge[1], edge[2], blank, edge[0]], axis=1)
    odd = lon_odd == 1
    lon_near = lax.ppermute(jnp.where(odd, west_edge, east_edge), "lon", swap_pairs(lon_count, 0, True))
    lon_far = lax.ppermute(jnp.where(odd, east_edge, west_edge), "lon", swap_pairs(lon_count, 1, True))

    wide = jnp.concatenate([own[0], own[1], own[2], lon_near, lon_far], axis=1)
    odd = lat_odd == 1
    south_edge, north_edge = wide[:HALO], wide[rows - HALO :]
    lat_near = lax.ppermute(jnp.where(odd, south_edge, north_edge), "lat", swap_pairs(lat_count, 0, False))
    lat_far = lax.ppermute(jnp.where(odd, north_edge, south_edge), "lat", swap_pairs(lat_count, 1, False))

    row = jnp.arange(height)
    row = jnp.where(row < rows + HALO, row, row - height).astype(jnp.float32)[:, None] + first_row
    wide_center = jnp.cos(jnp.deg2rad(BAND_SOUTH + ROW_STEP * (row + 0.5)))
    wide_northern = jnp.cos(jnp.deg2rad(BAND_SOUTH + ROW_STEP * (row + 1.0)))
    scale = jnp.broadcast_to(jnp.stack([1.0 / wide_center, wide_northern]), (2, height, LANES))

    smem = pl.BlockSpec(memory_space=pltpu.SMEM)
    vmem = pl.BlockSpec(memory_space=pltpu.VMEM)
    f32 = jnp.float32
    level_shapes = []
    for level in range(LEVELS):
        level_shapes += [jax.ShapeDtypeStruct((height >> level, width), f32)] * 5
    held = pl.pallas_call(
        descend,
        out_shape=[jax.ShapeDtypeStruct((TILE, LANES), f32)]
        + level_shapes
        + [jax.ShapeDtypeStruct((height, width), f32)],
        in_specs=[smem] + [vmem] * 6,
        out_specs=[vmem] * (2 + len(level_shapes)),
        scratch_shapes=[
            pltpu.VMEM((FIELDS, height, width), f32),
            pltpu.VMEM((4, width // LANES, height, LANES), f32),
        ],
        compiler_params=pltpu.CompilerParams(vmem_limit_bytes=40 * 1024 * 1024),
        name="descend",
    )(where, own, lat_near, lat_far, lon_near, lon_far, scale)
    packed, held = held[0], held[1:]

    count = lat_count * lon_count
    blocks = lax.all_to_all(
        jnp.broadcast_to(packed[None], (count, TILE, LANES)), ("lon", "lat"), 0, 0, tiled=True
    )

    return pl.pallas_call(
        functools.partial(ascend, lat_count, lon_count),
        out_shape=[jax.ShapeDtypeStruct((rows, cols), f32)] * 2,
        in_specs=[smem] + [vmem] * (1 + len(held)),
        out_specs=[vmem] * 2,
        scratch_shapes=[
            pltpu.VMEM((lat_count * (rows >> LEVELS) + 2 * TILE, lon_count * (cols >> LEVELS)), f32),
            pltpu.VMEM((width // LANES, height, LANES), f32),
        ],
        compiler_params=pltpu.CompilerParams(vmem_limit_bytes=40 * 1024 * 1024),
        name="ascend",
    )(where, blocks, *held)


def solution(mesh):
    body = functools.partial(on_device, mesh.shape["lat"], mesh.shape["lon"])
    return jax.shard_map(
        body,
        mesh=mesh,
        in_specs=(P("lat", "lon"),) * 4,
        out_specs=(P("lat", "lon"),) * 2,
        check_vma=False,
    )
```

```python
import functools

import jax
import jax.numpy as jnp
from jax import lax
from jax.experimental import pallas as pl
from jax.experimental.pallas import tpu as pltpu
from jax.sharding import PartitionSpec as P

LEVELS = 3
SWEEPS = 2
BOTTOM_ITERS = 6

DAMPING = 0.8
ROW_STEP = 150.0 / 8640.0
BAND_SOUTH = -50.0

HALO = 32
LANES = 128
TILE = 8
FIELDS = 3
VMEM_LIMIT = 40 * 1024 * 1024


def iota(shape, dim):
    return lax.broadcasted_iota(jnp.int32, shape, dim)


def lane_shift(field, count):
    return pltpu.roll(field, (-count) % field.shape[1], 1)


def north_of(tiles, t):
    if t + 1 < len(tiles):
        return tiles[t + 1]
    return pltpu.roll(tiles[0], TILE - 1, 0)


def south_of(tiles, t):
    if t > 0:
        return tiles[t - 1]
    return pltpu.roll(tiles[-1], 1, 0)


def neighbour_sum(field, east_face, north_face, stride):
    upward = [north_face[t] * field[t] for t in range(len(field))]
    return [
        (east_face[t] * lane_shift(field[t], stride) + lane_shift(east_face[t] * field[t], -stride))
        + (north_face[t] * north_of(field, t) + south_of(upward, t))
        for t in range(len(field))
    ]


def sweep(field, source, inverse, east_face, north_face, stride):
    around = neighbour_sum(field, east_face, north_face, stride)
    return [
        (1.0 - DAMPING) * field[t] + inverse[t] * (source[t] + around[t]) for t in range(len(field))
    ]


def remainder(field, source, diagonal, east_face, north_face, stride):
    around = neighbour_sum(field, east_face, north_face, stride)
    return [source[t] - diagonal[t] * field[t] + around[t] for t in range(len(field))]


def tiles_of(ref):
    return [ref[t] for t in range(ref.shape[0])]


def keep(ref, tiles):
    for t, value in enumerate(tiles):
        ref[t] = value


def prepare(where_ref, forcing_ref, surface_ref, sea_ref, levels_ref,
            own_ref, lon_near_ref, lon_far_ref, lat_near_ref, lat_far_ref, scale_ref,
            forcing_buf, surface_buf, sea_buf, levels_buf, sems):
    copies = [
        pltpu.make_async_copy(source, target, sems.at[i])
        for i, (source, target) in enumerate((
            (levels_ref, levels_buf), (sea_ref, sea_buf), (surface_ref, surface_buf), (forcing_ref, forcing_buf),
        ))
    ]
    for copy in copies:
        copy.start()
    rows, cols = forcing_buf.shape
    lon_odd = lax.rem(where_ref[0], 2)
    lat_odd = lax.rem(where_ref[1], 2)
    first_row = where_ref[1] * rows
    count = scale_ref.shape[1]
    height = count * TILE
    for t in range(count):
        row = iota((TILE, LANES), 0) * count + t
        row = jnp.where(row < rows + HALO, row, row - height) + first_row
        row = row.astype(jnp.float32)
        scale_ref[0, t] = 1.0 / jnp.cos(jnp.deg2rad(BAND_SOUTH + ROW_STEP * (row + 0.5)))
        scale_ref[1, t] = jnp.cos(jnp.deg2rad(BAND_SOUTH + ROW_STEP * (row + 1.0)))
    row = (iota((rows, LANES), 0) + first_row).astype(jnp.float32)
    center = jnp.cos(jnp.deg2rad(BAND_SOUTH + ROW_STEP * (row + 0.5)))
    center = jnp.concatenate([center] * (cols // LANES), axis=1)
    for copy in copies:
        copy.wait()
    sea_mask = sea_buf[...].astype(jnp.float32)
    layers = levels_buf[...].astype(jnp.float32)
    depth = sea_mask * ((layers + layers * (layers - 1.0) / 20.0) / 200.0)
    fields = (depth, surface_buf[...] * center * sea_mask, forcing_buf[...] * sea_mask)
    slot = iota((rows, LANES), 1) // HALO
    last = LANES // HALO - 1
    west_edge = jnp.zeros((rows, LANES), jnp.float32)
    east_edge = jnp.zeros((rows, LANES), jnp.float32)
    for f, value in enumerate(fields):
        own_ref[f] = value
        west_edge = jnp.where(slot == f, lane_shift(value[:, :LANES], -f * HALO), west_edge)
        east_edge = jnp.where(
            slot == (f + last) % (last + 1), lane_shift(value[:, cols - LANES :], -f * HALO), east_edge
        )
    odd = jnp.broadcast_to(lon_odd, (rows, LANES)) > 0
    lon_near_ref[...] = jnp.where(odd, west_edge, east_edge)
    lon_far_ref[...] = jnp.where(odd, east_edge, west_edge)
    odd = jnp.broadcast_to(lat_odd, (HALO, cols)) > 0
    for f, value in enumerate(fields):
        south_edge, north_edge = value[:HALO], value[rows - HALO :]
        part = slice(f * cols, (f + 1) * cols)
        lat_near_ref[:, part] = jnp.where(odd, south_edge, north_edge)
        lat_far_ref[:, part] = jnp.where(odd, north_edge, south_edge)


def descend(where_ref, own_ref, lon_near_ref, lon_far_ref, lat_near_ref, lat_far_ref,
            corner_near_ref, corner_far_ref, scale_ref, pack_ref, *rest):
    level_refs = [rest[5 * i : 5 * i + 5] for i in range(LEVELS)]
    diagonal_ref, grid_ref = rest[5 * LEVELS :]
    lon_index = where_ref[0]
    lon_odd = lax.rem(lon_index, 2)
    lat_odd = lax.rem(where_ref[1], 2)
    rows, cols = own_ref.shape[1], own_ref.shape[2]
    count, width = diagonal_ref.shape[0], diagonal_ref.shape[2]
    own_columns = cols // LANES
    columns = width // LANES
    near_row = rows + pl.multiple_of(lat_odd * HALO, HALO)
    far_row = rows + pl.multiple_of((1 - lat_odd) * HALO, HALO)
    last = LANES // HALO - 1
    parts = (
        (0, lon_near_ref[...], lon_far_ref[...], [own_ref.at[f] for f in range(FIELDS)]),
        (near_row, corner_near_ref[:, :LANES], corner_near_ref[:, LANES:],
         [lat_near_ref.at[:, pl.ds(f * cols, cols)] for f in range(FIELDS)]),
        (far_row, corner_far_ref[:, :LANES], corner_far_ref[:, LANES:],
         [lat_far_ref.at[:, pl.ds(f * cols, cols)] for f in range(FIELDS)]),
    )
    for first, near_val, far_val, bodies in parts:
        size = near_val.shape[0]
        odd = jnp.broadcast_to(lon_odd, near_val.shape) > 0
        east_val = jnp.where(odd, far_val, near_val)
        west_val = jnp.where(odd, near_val, far_val)
        slot = iota(near_val.shape, 1) // HALO
        for f, body in enumerate(bodies):
            both = jnp.where(
                slot == f, east_val, jnp.where(slot == (f + last) % (last + 1), west_val, 0.0)
            )
            for c in range(own_columns):
                grid_ref[f, c, pl.ds(first, size), :] = body[:, c * LANES : (c + 1) * LANES]
            grid_ref[f, own_columns, pl.ds(first, size), :] = lane_shift(both, f * HALO)

    def load(f):
        return [
            jnp.concatenate(
                [grid_ref[f, c, pl.ds(t, TILE, stride=count), :] for c in range(columns)], axis=1
            )
            for t in range(count)
        ]

    depth = load(0)
    source_term = load(1)
    source = load(2)
    across = [jnp.concatenate([scale_ref[0, t]] * columns, axis=1) for t in range(count)]
    along = [jnp.concatenate([scale_ref[1, t]] * columns, axis=1) for t in range(count)]
    east_face = [jnp.minimum(depth[t], lane_shift(depth[t], 1)) * across[t] for t in range(count)]
    north_face = [jnp.minimum(depth[t], north_of(depth, t)) * along[t] for t in range(count)]
    for level in range(LEVELS):
        stride = 1 << level
        inverse, diagonal = [], []
        for t in range(count >> level):
            total = source_term[t] + (
                (east_face[t] + lane_shift(east_face[t], -stride))
                + (north_face[t] + south_of(north_face, t))
            )
            diagonal.append(jnp.where(source_term[t] > 0.0, total, 1.0))
            inverse.append(DAMPING / diagonal[t])
        field = [inverse[t] * source[t] for t in range(count >> level)]
        for _ in range(SWEEPS - 1):
            field = sweep(field, source, inverse, east_face, north_face, stride)
        image = remainder(field, source, diagonal, east_face, north_face, stride)
        for ref, value in zip(level_refs[level], (east_face, north_face, inverse, source, field)):
            keep(ref, value)
        if level == 0:
            keep(diagonal_ref, diagonal)

        def coarse(tiles):
            sums = [tiles[t] + tiles[t + 1] for t in range(0, len(tiles), 2)]
            return [value + lane_shift(value, stride) for value in sums]

        east_face = [
            lane_shift(east_face[t] + east_face[t + 1], stride) for t in range(0, len(east_face), 2)
        ]
        north_face = [
            north_face[t] + lane_shift(north_face[t], stride) for t in range(1, len(north_face), 2)
        ]
        source_term = coarse(source_term)
        source = coarse(image)

    stride = 1 << LEVELS
    bottom_width = cols // stride
    group = LANES // bottom_width
    per_column = LANES // stride
    tiles = len(source)
    lane = iota((TILE, LANES), 1)
    cell = lane % bottom_width
    pick = (cell % per_column) * stride
    turn = lax.rem(lane // bottom_width + group - lax.rem(lon_index, group), group)
    for t in range(tiles):
        packed = jnp.zeros((TILE, LANES), jnp.float32)
        for f, value in enumerate((source[t], east_face[t], north_face[t], source_term[t])):
            flat = jnp.zeros((TILE, LANES), jnp.float32)
            for c in range(own_columns):
                taken = jnp.take_along_axis(value[:, c * LANES : (c + 1) * LANES], pick, axis=1)
                flat = jnp.where(cell // per_column == c, taken, flat)
            packed = jnp.where(turn == f, flat, packed)
        own_rows = pack_ref.shape[0] // tiles
        pack_ref[pl.ds(t, own_rows, stride=tiles), :] = packed[:own_rows]


def total_of(tiles):
    parts = list(tiles)
    while len(parts) > 1:
        parts = [
            parts[i] + parts[i + 1] if i + 1 < len(parts) else parts[i] for i in range(0, len(parts), 2)
        ]
    value = parts[0]
    value = sum(value[:, c : c + LANES] for c in range(0, value.shape[1], LANES))
    return jnp.sum(jnp.sum(value, axis=0, keepdims=True), axis=1, keepdims=True)


def conjugate(source, east_face, north_face, source_term):
    height = source.shape[0]

    def split(value):
        return [value[r : r + TILE] for r in range(0, height, TILE)]

    def up(value):
        return pltpu.roll(value, height - 1, 0)

    def down(value):
        return pltpu.roll(value, 1, 0)

    diagonal = source_term + (
        (east_face + lane_shift(east_face, -1)) + (north_face + down(north_face))
    )
    iterate = jnp.zeros_like(source)
    remain = source
    direction = source
    for _ in range(BOTTOM_ITERS):
        image = diagonal * direction - (
            (east_face * lane_shift(direction, 1) + lane_shift(east_face * direction, -1))
            + (north_face * up(direction) + down(north_face * direction))
        )
        norm = total_of(split(remain * remain))
        energy = total_of(split(direction * image))
        cross = total_of(split(remain * image))
        square = total_of(split(image * image))
        step_size = norm / energy
        iterate = iterate + step_size * direction
        remain = remain - step_size * image
        norm_next = norm - step_size * (2.0 * cross - step_size * square)
        direction = remain + (norm_next / norm) * direction
    return iterate


def ascend(lat_count, lon_count, where_ref, blocks_ref, *rest):
    level_refs = [rest[5 * i : 5 * i + 5] for i in range(LEVELS)]
    diagonal_ref, solution_ref, residual_ref, window_ref, turn_ref, order_ref = rest[5 * LEVELS :]
    lon_index = where_ref[0]
    lat_index = where_ref[1]
    rows, cols = solution_ref.shape
    count, width = diagonal_ref.shape[0], diagonal_ref.shape[2]
    own_columns = cols // LANES
    columns = width // LANES
    stride = 1 << LEVELS
    bottom_rows = rows // stride
    bottom_width = cols // stride
    group = LANES // bottom_width
    slot = iota((bottom_rows, LANES), 1) // bottom_width
    fields = []
    for f in range(4):
        strips = []
        for a in range(lat_count):
            pieces = []
            for c in range(lon_count // group):
                merged = None
                for j in range(group):
                    block = blocks_ref[(c * group + j) * lat_count + a]
                    merged = block if merged is None else jnp.where(slot == (f + j) % group, block, merged)
                pieces.append(lane_shift(merged, f * bottom_width))
            strips.append(jnp.concatenate(pieces, axis=1))
        fields.append(jnp.concatenate(strips, axis=0))
    iterate = conjugate(*fields)

    bottom_height = lat_count * bottom_rows
    whole_width = lon_count * bottom_width
    pad = 2 * TILE
    window_ref[pl.ds(0, pad), :] = jnp.zeros((pad, LANES), jnp.float32)
    window_ref[pl.ds(pad + bottom_height, pad), :] = jnp.zeros((pad, LANES), jnp.float32)
    margin = LANES // 2 // stride
    shift = lax.rem(margin - lon_index * bottom_width + whole_width, whole_width)
    window_ref[pl.ds(pad, bottom_height), :] = pltpu.roll(iterate, shift, 1)[:, :LANES]
    start = pl.multiple_of(lat_index * bottom_rows, TILE)
    strip = window_ref[pl.ds(start, 5 * TILE), :]
    turn_ref[...] = strip
    tiles = count >> LEVELS
    sublane = iota((TILE, LANES), 0)
    ahead = (rows + HALO) // stride // tiles
    lane = iota((TILE, LANES), 1)
    correction = []
    for t in range(tiles):
        upper = turn_ref[pl.ds(pad + t, TILE, stride=tiles), :]
        lower = turn_ref[pl.ds(pad + t - tiles * TILE, TILE, stride=tiles), :]
        value = jnp.where(sublane < ahead, upper, lower)
        parts = []
        for c in range(columns):
            if c < own_columns:
                pick = margin + (c * LANES + lane) // stride
            else:
                pick = jnp.where(
                    lane < LANES // 2, margin + bottom_width + lane // stride, (lane - LANES // 2) // stride
                )
            parts.append(jnp.take_along_axis(value, pick, axis=1))
        correction.append(jnp.concatenate(parts, axis=1))

    lane = iota((TILE, width), 1)
    for level in range(LEVELS - 1, -1, -1):
        stride = 1 << level
        east_face, north_face, inverse, source, field = map(tiles_of, level_refs[level])
        if level < LEVELS - 1:
            first = lax.rem(lane // stride, 2) == 0
            correction = [jnp.where(first, value, lane_shift(value, -stride)) for value in correction]
        spread = [correction[t // 2] for t in range(count >> level)]
        if level == 0:
            sea = [east_face[t] + north_face[t] > 0.0 for t in range(count)]
            spread = [jnp.where(sea[t], spread[t], 0.0) for t in range(count)]
        field = [field[t] + spread[t] for t in range(count >> level)]
        for _ in range(SWEEPS):
            field = sweep(field, source, inverse, east_face, north_face, stride)
        correction = field
    final = remainder(correction, source, tiles_of(diagonal_ref), east_face, north_face, 1)
    own_sublanes = rows // count
    for k, (ref, value) in enumerate(((solution_ref, correction), (residual_ref, final))):
        for c in range(own_columns):
            part = slice(c * LANES, (c + 1) * LANES)
            for t in range(count):
                order_ref[k, c, pl.ds(t, own_sublanes, stride=count), :] = value[t][:own_sublanes, part]
            ref[:, part] = order_ref[k, c]


def swap_pairs(count, first, periodic):
    pairs = []
    for i in range(first, count, 2):
        j = i + 1
        if j < count or periodic:
            pairs += [(i, j % count), (j % count, i)]
    return pairs


def on_device(lat_count, lon_count, forcing, surface_term, sea_cells, levels):
    rows, cols = forcing.shape
    height, width = rows + 2 * HALO, cols + LANES
    count = height // TILE
    f32 = jnp.float32
    smem = pl.BlockSpec(memory_space=pltpu.SMEM)
    vmem = pl.BlockSpec(memory_space=pltpu.VMEM)
    hbm = pl.BlockSpec(memory_space=pltpu.HBM)
    params = pltpu.CompilerParams(vmem_limit_bytes=VMEM_LIMIT)
    lon_index = lax.axis_index("lon").astype(jnp.int32)
    lat_index = lax.axis_index("lat").astype(jnp.int32)
    where = jnp.stack([lon_index, lat_index])

    own, lon_near, lon_far, lat_near, lat_far, scale = pl.pallas_call(
        prepare,
        out_shape=[
            jax.ShapeDtypeStruct((FIELDS, rows, cols), f32),
            jax.ShapeDtypeStruct((rows, LANES), f32),
            jax.ShapeDtypeStruct((rows, LANES), f32),
            jax.ShapeDtypeStruct((HALO, FIELDS * cols), f32),
            jax.ShapeDtypeStruct((HALO, FIELDS * cols), f32),
            jax.ShapeDtypeStruct((2, count, TILE, LANES), f32),
        ],
        in_specs=[smem] + [hbm] * 4,
        out_specs=[vmem] * 6,
        scratch_shapes=[
            pltpu.VMEM((rows, cols), f32),
            pltpu.VMEM((rows, cols), f32),
            pltpu.VMEM((rows, cols), jnp.int32),
            pltpu.VMEM((rows, cols), jnp.int32),
            pltpu.SemaphoreType.DMA((4,)),
        ],
        compiler_params=params,
        name="prepare",
    )(where, *(pltpu.with_memory_space_constraint(x, pltpu.HBM) for x in (forcing, surface_term, sea_cells, levels)))

    far_pairs, near_pairs = swap_pairs(lon_count, 1, True), swap_pairs(lon_count, 0, True)
    north_pairs, south_pairs = swap_pairs(lat_count, 0, False), swap_pairs(lat_count, 1, False)
    lon_far = lax.ppermute(lon_far, "lon", far_pairs)
    lon_near = lax.ppermute(lon_near, "lon", near_pairs)
    lat_far = lax.ppermute(lat_far, "lat", south_pairs)
    lat_near = lax.ppermute(lat_near, "lat", north_pairs)
    sides = jnp.concatenate([lon_near, lon_far], axis=1)
    odd = lat_index % 2 == 1
    south_edge, north_edge = sides[:HALO], sides[rows - HALO :]
    corner_far = lax.ppermute(jnp.where(odd, north_edge, south_edge), "lat", south_pairs)
    corner_near = lax.ppermute(jnp.where(odd, south_edge, north_edge), "lat", north_pairs)

    level_shapes = []
    for level in range(LEVELS):
        level_shapes += [jax.ShapeDtypeStruct((count >> level, TILE, width), f32)] * 5
    held = pl.pallas_call(
        descend,
        out_shape=[jax.ShapeDtypeStruct((rows >> LEVELS, LANES), f32)]
        + level_shapes
        + [jax.ShapeDtypeStruct((count, TILE, width), f32)],
        in_specs=[smem] + [vmem] * 8,
        out_specs=[vmem] * (2 + len(level_shapes)),
        scratch_shapes=[pltpu.VMEM((FIELDS, width // LANES, height, LANES), f32)],
        compiler_params=params,
        name="descend",
    )(where, own, lon_near, lon_far, lat_near, lat_far, corner_near, corner_far, scale)
    packed, held = held[0], held[1:]

    blocks = lax.all_to_all(
        jnp.broadcast_to(packed[None], (lat_count * lon_count,) + packed.shape), ("lon", "lat"), 0, 0, tiled=True
    )

    return pl.pallas_call(
        functools.partial(ascend, lat_count, lon_count),
        out_shape=[jax.ShapeDtypeStruct((rows, cols), f32)] * 2,
        in_specs=[smem] + [vmem] * (1 + len(held)),
        out_specs=[vmem] * 2,
        scratch_shapes=[
            pltpu.VMEM((lat_count * (rows >> LEVELS) + 4 * TILE, LANES), f32),
            pltpu.VMEM((5 * TILE, LANES), f32),
            pltpu.VMEM((2, cols // LANES, rows, LANES), f32),
        ],
        compiler_params=params,
        name="ascend",
    )(where, blocks, *held)


def solution(mesh):
    body = functools.partial(on_device, mesh.shape["lat"], mesh.shape["lon"])
    return jax.shard_map(
        body,
        mesh=mesh,
        in_specs=(P("lat", "lon"),) * 4,
        out_specs=(P("lat", "lon"),) * 2,
        check_vma=False,
    )
```

```python
import functools

import jax
import jax.numpy as jnp
from jax import lax
from jax.experimental import pallas as pl
from jax.experimental.pallas import tpu as pltpu
from jax.sharding import PartitionSpec as P

LEVELS = 3
SWEEPS = 2
BOTTOM_ITERS = 6

DAMPING = 0.8
ROW_STEP = 150.0 / 8640.0
BAND_SOUTH = -50.0

HALO = 32
LANES = 128
TILE = 8
FIELDS = 3
SHIFT = 2
VMEM_LIMIT = 8 * 1024 * 1024


def iota(shape, dim):
    return lax.broadcasted_iota(jnp.int32, shape, dim)


def lane_shift(field, count):
    return pltpu.roll(field, (-count) % field.shape[1], 1)


def north_of(tiles, t):
    if t + 1 < len(tiles):
        return tiles[t + 1]
    return pltpu.roll(tiles[0], TILE - 1, 0)


def south_of(tiles, t):
    if t > 0:
        return tiles[t - 1]
    return pltpu.roll(tiles[-1], 1, 0)


def neighbour_sum(field, east_face, north_face, stride):
    upward = [north_face[t] * field[t] for t in range(len(field))]
    return [
        (east_face[t] * lane_shift(field[t], stride) + lane_shift(east_face[t] * field[t], -stride))
        + (north_face[t] * north_of(field, t) + south_of(upward, t))
        for t in range(len(field))
    ]


def sweep(field, source, inverse, east_face, north_face, stride):
    around = neighbour_sum(field, east_face, north_face, stride)
    return [
        (1.0 - DAMPING) * field[t] + inverse[t] * (source[t] + around[t]) for t in range(len(field))
    ]


def remainder(field, source, diagonal, east_face, north_face, stride):
    around = neighbour_sum(field, east_face, north_face, stride)
    return [source[t] - diagonal[t] * field[t] + around[t] for t in range(len(field))]


def tiles_of(ref):
    return [ref[t] for t in range(ref.shape[0])]


def keep(ref, tiles):
    for t, value in enumerate(tiles):
        ref[t] = value


def metric(row):
    center = jnp.cos(jnp.deg2rad(BAND_SOUTH + ROW_STEP * (row + 0.5)))
    northern = jnp.cos(jnp.deg2rad(BAND_SOUTH + ROW_STEP * (row + 1.0)))
    return center, northern


def prepare(where_ref, forcing_ref, surface_ref, sea_ref, levels_ref,
            own_ref, east_edge_ref, west_edge_ref, lat_near_ref, lat_far_ref, diagonal_edge_ref,
            forcing_buf, surface_buf, sea_buf, levels_buf, sems):
    copies = [
        pltpu.make_async_copy(source, target, sems.at[i])
        for i, (source, target) in enumerate((
            (levels_ref, levels_buf), (sea_ref, sea_buf), (surface_ref, surface_buf), (forcing_ref, forcing_buf),
        ))
    ]
    for copy in copies:
        copy.start()
    rows, cols = forcing_buf.shape
    lat_odd = lax.rem(where_ref[1], 2)
    first_row = where_ref[1] * rows
    row = (iota((rows, LANES), 0) + first_row).astype(jnp.float32)
    center = jnp.cos(jnp.deg2rad(BAND_SOUTH + ROW_STEP * (row + 0.5)))
    center = jnp.concatenate([center] * (cols // LANES), axis=1)
    for copy in copies:
        copy.wait()
    sea_mask = sea_buf[...].astype(jnp.float32)
    layers = levels_buf[...].astype(jnp.float32)
    depth = sea_mask * ((layers + layers * (layers - 1.0) / 20.0) / 200.0)
    fields = (depth, surface_buf[...] * center * sea_mask, forcing_buf[...] * sea_mask)
    slot = iota((rows, LANES), 1) // HALO
    slots = LANES // HALO
    west_edge = jnp.zeros((rows, LANES), jnp.float32)
    east_edge = jnp.zeros((rows, LANES), jnp.float32)
    for f, value in enumerate(fields):
        own_ref[f] = value
        west_edge = jnp.where(slot == f, lane_shift(value[:, :LANES], -f * HALO), west_edge)
        east_edge = jnp.where(
            slot == (f + slots - 1) % slots, lane_shift(value[:, cols - LANES :], -f * HALO), east_edge
        )
    east_edge_ref[...] = east_edge
    west_edge_ref[...] = west_edge
    odd = jnp.broadcast_to(lat_odd, (HALO, cols)) > 0
    for f, value in enumerate(fields):
        south_edge, north_edge = value[:HALO], value[rows - HALO :]
        part = slice(f * cols, (f + 1) * cols)
        lat_near_ref[:, part] = jnp.where(odd, south_edge, north_edge)
        lat_far_ref[:, part] = jnp.where(odd, north_edge, south_edge)
    odd = odd[:, :LANES]
    part = slice(FIELDS * cols, FIELDS * cols + LANES)
    lat_near_ref[:, part] = jnp.where(odd, west_edge[:HALO], west_edge[rows - HALO :])
    lat_far_ref[:, part] = jnp.where(odd, west_edge[rows - HALO :], west_edge[:HALO])
    diagonal_edge_ref[...] = jnp.where(odd, east_edge[rows - HALO :], east_edge[:HALO])


def faces(depth, across, along):
    count = len(depth)
    east_face = [jnp.minimum(depth[t], lane_shift(depth[t], 1)) * across[t] for t in range(count)]
    north_face = [jnp.minimum(depth[t], north_of(depth, t)) * along[t] for t in range(count)]
    return east_face, north_face


def level_down(level, east_face, north_face, source_term, source):
    stride = 1 << level
    count = len(source)
    inverse, diagonal = [], []
    for t in range(count):
        total = source_term[t] + (
            (east_face[t] + lane_shift(east_face[t], -stride))
            + (north_face[t] + south_of(north_face, t))
        )
        diagonal.append(jnp.where(source_term[t] > 0.0, total, 1.0))
        inverse.append(DAMPING / diagonal[t])
    field = [inverse[t] * source[t] for t in range(count)]
    for _ in range(SWEEPS - 1):
        field = sweep(field, source, inverse, east_face, north_face, stride)
    image = remainder(field, source, diagonal, east_face, north_face, stride)
    kept = (east_face, north_face, inverse, source, field, diagonal)

    def coarse(tiles):
        sums = [tiles[t] + tiles[t + 1] for t in range(0, count, 2)]
        return [value + lane_shift(value, stride) for value in sums]

    east_next = [lane_shift(east_face[t] + east_face[t + 1], stride) for t in range(0, count, 2)]
    north_next = [north_face[t] + lane_shift(north_face[t], stride) for t in range(1, count, 2)]
    return kept, (east_next, north_next, coarse(source_term), coarse(image))


def lay_out(lat_count, where_ref, own_ref, lat_near_ref, lat_far_ref, west_ref, west_far_ref, east_ref, scale_ref, grid_ref):
    rows, cols = own_ref.shape[1], own_ref.shape[2]
    columns, height = grid_ref.shape[1], grid_ref.shape[2]
    count = height // TILE
    own_columns = cols // LANES
    lat_odd = lax.rem(where_ref[1], 2)
    near_row = rows + pl.multiple_of(lat_odd * HALO, HALO)
    far_row = rows + pl.multiple_of((1 - lat_odd) * HALO, HALO)
    edge = FIELDS * cols + LANES
    parts = (
        (0, 0, west_ref, [own_ref.at[f] for f in range(FIELDS)]),
        (near_row, rows, lat_near_ref.at[:, pl.ds(edge, LANES)],
         [lat_near_ref.at[:, pl.ds(f * cols, cols)] for f in range(FIELDS)]),
        (far_row, rows + HALO, west_far_ref, [lat_far_ref.at[:, pl.ds(f * cols, cols)] for f in range(FIELDS)]),
    )
    last = LANES // HALO - 1
    for first, at, side_ref, bodies in parts:
        west = side_ref[...]
        slot = iota(west.shape, 1) // HALO
        lat_index = where_ref[1]
        outside = jnp.broadcast_to((lat_index == 0) | (lat_index == lat_count - 1), west.shape)
        for f, body in enumerate(bodies):
            for c in range(own_columns):
                value = body[:, c * LANES : (c + 1) * LANES]
                if first is far_row:
                    value = jnp.where(outside, 0.0, value)
                grid_ref[f, c, pl.ds(first, west.shape[0]), :] = value
            side = jnp.where(slot == (f + last) % (last + 1), west, 0.0)
            if east_ref is not None:
                side = jnp.where(slot == f, east_ref[pl.ds(at, west.shape[0]), :], side)
            if first is far_row:
                side = jnp.where(outside, 0.0, side)
            grid_ref[f, own_columns, pl.ds(first, west.shape[0]), :] = lane_shift(side, f * HALO)

    def load(f):
        return [
            jnp.concatenate(
                [grid_ref[f, c, pl.ds(t, TILE, stride=count), :] for c in range(columns)], axis=1
            )
            for t in range(count)
        ]

    depth, source_term, source = load(0), load(1), load(2)
    across = [jnp.concatenate([scale_ref[0, t]] * columns, axis=1) for t in range(count)]
    along = [jnp.concatenate([scale_ref[1, t]] * columns, axis=1) for t in range(count)]
    return faces(depth, across, along) + (source_term, source)


def hold(lat_count, where_ref, own_ref, lat_near_ref, lat_far_ref, west_ref, west_far_ref, east_ref, scale_ref, *rest):
    level_refs = [rest[5 * i : 5 * i + 5] for i in range(LEVELS)]
    diagonal_ref, grid_ref = rest[5 * LEVELS :]
    state = lay_out(lat_count, where_ref, own_ref, lat_near_ref, lat_far_ref, west_ref, west_far_ref, east_ref, scale_ref,
                    grid_ref)
    for level in range(LEVELS):
        kept, state = level_down(level, *state)
        for ref, tiles in zip(level_refs[level], kept):
            keep(ref, tiles)
        if level == 0:
            keep(diagonal_ref, kept[-1])


def descend(lat_count, where_ref, own_ref, lat_near_ref, lat_far_ref, west_ref, west_far_ref, scale_ref, pack_ref, grid_ref):
    lon_index = where_ref[0]
    cols = own_ref.shape[2]
    own_columns = cols // LANES
    columns = grid_ref.shape[1]
    state = lay_out(lat_count, where_ref, own_ref, lat_near_ref, lat_far_ref, west_ref, west_far_ref, None, scale_ref,
                    grid_ref)
    for level in range(LEVELS):
        _, state = level_down(level, *state)

    east_face, north_face, source_term, source = state
    stride = 1 << LEVELS
    bottom_width = cols // stride
    group = LANES // bottom_width
    per_column = LANES // stride
    tiles = len(source)
    lane = iota((TILE, LANES), 1)
    cell = lane % bottom_width - SHIFT
    column = jnp.where(cell < 0, own_columns, cell // per_column)
    pick = jnp.where(cell < 0, LANES + cell * stride, (cell % per_column) * stride)
    turn = lax.rem(lane // bottom_width + group - lax.rem(lon_index, group), group)
    own_rows = pack_ref.shape[1] // tiles
    for t in range(tiles):
        packed = jnp.zeros((TILE, LANES), jnp.float32)
        for f, value in enumerate((source[t], east_face[t], north_face[t], source_term[t])):
            flat = jnp.zeros((TILE, LANES), jnp.float32)
            for c in range(columns):
                taken = jnp.take_along_axis(value[:, c * LANES : (c + 1) * LANES], pick, axis=1)
                flat = jnp.where(column == c, taken, flat)
            packed = jnp.where(turn == f, flat, packed)
        for k in range(pack_ref.shape[0]):
            pack_ref[k, pl.ds(t, own_rows, stride=tiles), :] = packed[:own_rows]


def total_of(tiles):
    parts = list(tiles)
    while len(parts) > 1:
        parts = [
            parts[i] + parts[i + 1] if i + 1 < len(parts) else parts[i] for i in range(0, len(parts), 2)
        ]
    value = parts[0]
    value = sum(value[:, c : c + LANES] for c in range(0, value.shape[1], LANES))
    return jnp.sum(jnp.sum(value, axis=0, keepdims=True), axis=1, keepdims=True)


def conjugate(source, east_face, north_face, source_term):
    height = source.shape[0]

    def split(value):
        return [value[r : r + TILE] for r in range(0, height, TILE)]

    def up(value):
        return pltpu.roll(value, height - 1, 0)

    def down(value):
        return pltpu.roll(value, 1, 0)

    diagonal = source_term + (
        (east_face + lane_shift(east_face, -1)) + (north_face + down(north_face))
    )
    iterate = jnp.zeros_like(source)
    remain = source
    direction = source
    for _ in range(BOTTOM_ITERS):
        image = diagonal * direction - (
            (east_face * lane_shift(direction, 1) + lane_shift(east_face * direction, -1))
            + (north_face * up(direction) + down(north_face * direction))
        )
        norm = total_of(split(remain * remain))
        energy = total_of(split(direction * image))
        cross = total_of(split(remain * image))
        square = total_of(split(image * image))
        step_size = norm / energy
        iterate = iterate + step_size * direction
        remain = remain - step_size * image
        norm_next = norm - step_size * (2.0 * cross - step_size * square)
        direction = remain + (norm_next / norm) * direction
    return iterate


def ascend(lat_count, lon_count, where_ref, blocks_ref, *rest):
    level_refs = [rest[5 * i : 5 * i + 5] for i in range(LEVELS)]
    diagonal_ref, solution_ref, residual_ref, window_ref, turn_ref, order_ref = rest[5 * LEVELS :]
    lon_index = where_ref[0]
    lat_index = where_ref[1]
    rows, cols = solution_ref.shape
    count, width = diagonal_ref.shape[0], diagonal_ref.shape[2]
    own_columns = cols // LANES
    columns = width // LANES
    stride = 1 << LEVELS
    bottom_rows = rows // stride
    bottom_width = cols // stride
    group = LANES // bottom_width
    slot = iota((bottom_rows, LANES), 1) // bottom_width
    fields = []
    for f in range(4):
        strips = []
        for a in range(lat_count):
            pieces = []
            for c in range(lon_count // group):
                merged = None
                for j in range(group):
                    block = blocks_ref[(c * group + j) * lat_count + a]
                    merged = block if merged is None else jnp.where(slot == (f + j) % group, block, merged)
                pieces.append(lane_shift(merged, f * bottom_width))
            strips.append(jnp.concatenate(pieces, axis=1))
        fields.append(jnp.concatenate(strips, axis=0))
    iterate = conjugate(*fields)

    bottom_height = lat_count * bottom_rows
    whole_width = lon_count * bottom_width
    pad = 2 * TILE
    window_ref[pl.ds(0, pad), :] = jnp.zeros((pad, LANES), jnp.float32)
    window_ref[pl.ds(pad + bottom_height, pad), :] = jnp.zeros((pad, LANES), jnp.float32)
    half = LANES // 2
    margin = half // stride
    shift = lax.rem(margin - SHIFT - lon_index * bottom_width + whole_width, whole_width)
    window_ref[pl.ds(pad, bottom_height), :] = pltpu.roll(iterate, shift, 1)[:, :LANES]
    start = pl.multiple_of(lat_index * bottom_rows, TILE)
    turn_ref[...] = window_ref[pl.ds(start, 5 * TILE), :]
    tiles = count >> LEVELS
    lane = iota((TILE, LANES), 1)
    ahead = (rows + HALO) // stride // tiles
    sublane = iota((TILE, LANES), 0)
    correction = []
    for t in range(tiles):
        upper = turn_ref[pl.ds(pad + t, TILE, stride=tiles), :]
        lower = turn_ref[pl.ds(pad + t - tiles * TILE, TILE, stride=tiles), :]
        value = jnp.where(sublane < ahead, upper, lower)
        parts = []
        for c in range(columns):
            if c < own_columns:
                pick = margin + (c * LANES + lane) // stride
            else:
                pick = jnp.where(lane < half, margin + bottom_width + lane // stride, (lane - half) // stride)
            parts.append(jnp.take_along_axis(value, pick, axis=1))
        correction.append(jnp.concatenate(parts, axis=1))

    lane = iota((TILE, width), 1)
    for level in range(LEVELS - 1, -1, -1):
        stride = 1 << level
        east_face, north_face, inverse, source, field = map(tiles_of, level_refs[level])
        if level < LEVELS - 1:
            first = lax.rem(lane // stride, 2) == 0
            correction = [jnp.where(first, value, lane_shift(value, -stride)) for value in correction]
        spread = [correction[t // 2] for t in range(count >> level)]
        if level == 0:
            sea = [east_face[t] + north_face[t] > 0.0 for t in range(count)]
            spread = [jnp.where(sea[t], spread[t], 0.0) for t in range(count)]
        field = [field[t] + spread[t] for t in range(count >> level)]
        for _ in range(SWEEPS):
            field = sweep(field, source, inverse, east_face, north_face, stride)
        correction = field
    final = remainder(correction, source, tiles_of(diagonal_ref), east_face, north_face, 1)
    own_sublanes = rows // count
    for k, (ref, value) in enumerate(((solution_ref, correction), (residual_ref, final))):
        for c in range(own_columns):
            part = slice(c * LANES, (c + 1) * LANES)
            for t in range(count):
                order_ref[k, c, pl.ds(t, own_sublanes, stride=count), :] = value[t][:own_sublanes, part]
            ref[:, part] = order_ref[k, c]


def swap_pairs(count, first):
    pairs = []
    for i in range(first, count, 2):
        j = (i + 1) % count
        pairs += [(i, j), (j, i)]
    return pairs


def on_device(lat_count, lon_count, forcing, surface_term, sea_cells, levels):
    rows, cols = forcing.shape
    height, width = rows + 2 * HALO, cols + LANES
    count = height // TILE
    f32 = jnp.float32
    smem = pl.BlockSpec(memory_space=pltpu.SMEM)
    vmem = pl.BlockSpec(memory_space=pltpu.VMEM)
    hbm = pl.BlockSpec(memory_space=pltpu.HBM)
    params = pltpu.CompilerParams(vmem_limit_bytes=VMEM_LIMIT)
    lon_index = lax.axis_index("lon").astype(jnp.int32)
    lat_index = lax.axis_index("lat").astype(jnp.int32)
    where = jnp.stack([lon_index, lat_index])
    inputs = [
        pltpu.with_memory_space_constraint(x, pltpu.HBM) for x in (forcing, surface_term, sea_cells, levels)
    ]
    own, east_edge, west_edge, lat_near, lat_far, diagonal_edge = pl.pallas_call(
        prepare,
        out_shape=[
            jax.ShapeDtypeStruct((FIELDS, rows, cols), f32),
            jax.ShapeDtypeStruct((rows, LANES), f32),
            jax.ShapeDtypeStruct((rows, LANES), f32),
            jax.ShapeDtypeStruct((HALO, FIELDS * cols + LANES), f32),
            jax.ShapeDtypeStruct((HALO, FIELDS * cols + LANES), f32),
            jax.ShapeDtypeStruct((HALO, LANES), f32),
        ],
        in_specs=[smem] + [hbm] * 4,
        out_specs=[vmem] * 6,
        scratch_shapes=[
            pltpu.VMEM((rows, cols), f32),
            pltpu.VMEM((rows, cols), f32),
            pltpu.VMEM((rows, cols), jnp.int32),
            pltpu.VMEM((rows, cols), jnp.int32),
            pltpu.SemaphoreType.DMA((4,)),
        ],
        compiler_params=params,
        name="prepare",
    )(where, *inputs)

    eastward = [(i, (i + 1) % lon_count) for i in range(lon_count)]
    westward = [(target, source) for source, target in eastward]
    near_pairs, far_pairs = swap_pairs(lat_count, 0), swap_pairs(lat_count, 1)
    across_pairs = [
        (i * lat_count + a, (i + 1) % lon_count * lat_count + b) for i in range(lon_count) for a, b in far_pairs
    ]
    west_halo = lax.ppermute(east_edge, "lon", eastward)
    lat_far = lax.ppermute(lat_far, "lat", far_pairs)
    west_far = lax.ppermute(diagonal_edge, ("lon", "lat"), across_pairs)
    odd = lat_index % 2 == 1
    lat_near = lax.ppermute(
        jnp.concatenate([lat_near, jnp.where(odd, west_halo[:HALO], west_halo[rows - HALO :])], axis=1),
        "lat",
        near_pairs,
    )
    edge = FIELDS * cols
    east_halo = lax.ppermute(
        jnp.concatenate([west_edge, lat_near[:, edge : edge + LANES], lat_far[:, edge : edge + LANES]], axis=0),
        "lon",
        westward,
    )

    row = jnp.arange(TILE)[None, :] * count + jnp.arange(count)[:, None]
    row = jnp.where(row < rows + HALO, row, row - height).astype(f32) + (lat_index * rows).astype(f32)
    center, northern = metric(row)
    scale = jnp.broadcast_to(jnp.stack([1.0 / center, northern])[..., None], (2, count, TILE, LANES))

    devices = lat_count * lon_count
    grid = pltpu.VMEM((FIELDS, width // LANES, height, LANES), f32)
    packed = pl.pallas_call(
        functools.partial(descend, lat_count),
        out_shape=jax.ShapeDtypeStruct((devices, rows >> LEVELS, LANES), f32),
        in_specs=[smem] + [vmem] * 6,
        out_specs=vmem,
        scratch_shapes=[grid],
        compiler_params=params,
        name="descend",
    )(where, own, lat_near, lat_far, west_halo, west_far, scale)
    blocks = lax.all_to_all(packed, ("lon", "lat"), 0, 0, tiled=True)

    level_shapes = []
    for level in range(LEVELS):
        level_shapes += [jax.ShapeDtypeStruct((count >> level, TILE, width), f32)] * 5
    held = pl.pallas_call(
        functools.partial(hold, lat_count),
        out_shape=level_shapes + [jax.ShapeDtypeStruct((count, TILE, width), f32)],
        in_specs=[smem] + [vmem] * 7,
        out_specs=[vmem] * (1 + len(level_shapes)),
        scratch_shapes=[grid],
        compiler_params=params,
        cost_estimate=pl.CostEstimate(flops=0, bytes_accessed=60 * 1024 * 1024, transcendentals=0),
        name="hold",
    )(where, own, lat_near, lat_far, west_halo, west_far, east_halo, scale)

    return pl.pallas_call(
        functools.partial(ascend, lat_count, lon_count),
        out_shape=[jax.ShapeDtypeStruct((rows, cols), f32)] * 2,
        in_specs=[smem] + [vmem] * (1 + len(held)),
        out_specs=[vmem] * 2,
        scratch_shapes=[
            pltpu.VMEM((lat_count * (rows >> LEVELS) + 4 * TILE, LANES), f32),
            pltpu.VMEM((5 * TILE, LANES), f32),
            pltpu.VMEM((2, cols // LANES, rows, LANES), f32),
        ],
        compiler_params=params,
        name="ascend",
    )(where, blocks, *held)


def solution(mesh):
    body = functools.partial(on_device, mesh.shape["lat"], mesh.shape["lon"])
    return jax.shard_map(
        body,
        mesh=mesh,
        in_specs=(P("lat", "lon"),) * 4,
        out_specs=(P("lat", "lon"),) * 2,
        check_vma=False,
    )
```

```python
import functools

import jax
import jax.numpy as jnp
from jax import lax
from jax.experimental import pallas as pl
from jax.experimental.pallas import tpu as pltpu
from jax.sharding import PartitionSpec as P

LEVELS = 3
SWEEPS = 2
BOTTOM_ITERS = 6

DAMPING = 0.8
ROW_STEP = 150.0 / 8640.0
BAND_SOUTH = -50.0

HALO = 32
LANES = 128
TILE = 8
FIELDS = 3
SHIFT = 2
VMEM_LIMIT = 8 * 1024 * 1024


def iota(shape, dim):
    return lax.broadcasted_iota(jnp.int32, shape, dim)


def lane_shift(field, count):
    return pltpu.roll(field, (-count) % field.shape[1], 1)


def north_of(tiles, t):
    if t + 1 < len(tiles):
        return tiles[t + 1]
    return pltpu.roll(tiles[0], TILE - 1, 0)


def south_of(tiles, t):
    if t > 0:
        return tiles[t - 1]
    return pltpu.roll(tiles[-1], 1, 0)


def neighbour_sum(field, east_face, north_face, stride):
    upward = [north_face[t] * field[t] for t in range(len(field))]
    return [
        (east_face[t] * lane_shift(field[t], stride) + lane_shift(east_face[t] * field[t], -stride))
        + (north_face[t] * north_of(field, t) + south_of(upward, t))
        for t in range(len(field))
    ]


def sweep(field, source, inverse, east_face, north_face, stride):
    around = neighbour_sum(field, east_face, north_face, stride)
    return [
        (1.0 - DAMPING) * field[t] + inverse[t] * (source[t] + around[t]) for t in range(len(field))
    ]


def remainder(field, source, diagonal, east_face, north_face, stride):
    around = neighbour_sum(field, east_face, north_face, stride)
    return [source[t] - diagonal[t] * field[t] + around[t] for t in range(len(field))]


def tiles_of(ref):
    return [ref[t] for t in range(ref.shape[0])]


def keep(ref, tiles):
    for t, value in enumerate(tiles):
        ref[t] = value


def metric(row):
    center = jnp.cos(jnp.deg2rad(BAND_SOUTH + ROW_STEP * (row + 0.5)))
    northern = jnp.cos(jnp.deg2rad(BAND_SOUTH + ROW_STEP * (row + 1.0)))
    return center, northern


def prepare(forcing_ref, surface_ref, sea_ref, levels_ref,
            own_ref, east_edge_ref, west_edge_ref,
            forcing_buf, surface_buf, sea_buf, levels_buf, sems):
    copies = [
        pltpu.make_async_copy(source, target, sems.at[i])
        for i, (source, target) in enumerate((
            (levels_ref, levels_buf), (sea_ref, sea_buf), (surface_ref, surface_buf), (forcing_ref, forcing_buf),
        ))
    ]
    for copy in copies:
        copy.start()
    rows, cols = forcing_buf.shape
    first_row = lax.axis_index("lat") * rows
    row = (iota((rows, LANES), 0) + first_row).astype(jnp.float32)
    center = jnp.cos(jnp.deg2rad(BAND_SOUTH + ROW_STEP * (row + 0.5)))
    center = jnp.concatenate([center] * (cols // LANES), axis=1)
    for copy in copies:
        copy.wait()
    sea_mask = sea_buf[...].astype(jnp.float32)
    layers = levels_buf[...].astype(jnp.float32)
    depth = sea_mask * ((layers + layers * (layers - 1.0) / 20.0) / 200.0)
    fields = (depth, surface_buf[...] * center * sea_mask, forcing_buf[...] * sea_mask)
    slot = iota((rows, LANES), 1) // HALO
    slots = LANES // HALO
    west_edge = jnp.zeros((rows, LANES), jnp.float32)
    east_edge = jnp.zeros((rows, LANES), jnp.float32)
    for f, value in enumerate(fields):
        own_ref[f] = value
        west_edge = jnp.where(slot == f, lane_shift(value[:, :LANES], -f * HALO), west_edge)
        east_edge = jnp.where(
            slot == (f + slots - 1) % slots, lane_shift(value[:, cols - LANES :], -f * HALO), east_edge
        )
    east_edge_ref[...] = east_edge
    west_edge_ref[...] = west_edge


def prepare_corner(east_edge_ref, diagonal_edge_ref):
    rows = east_edge_ref.shape[0]
    odd = jnp.broadcast_to(lax.rem(lax.axis_index("lat"), 2), diagonal_edge_ref.shape) > 0
    diagonal_edge_ref[...] = jnp.where(odd, east_edge_ref[pl.ds(rows - HALO, HALO), :], east_edge_ref[pl.ds(0, HALO), :])


def prepare_rows(own_ref, west_edge_ref, lat_near_ref, lat_far_ref):
    rows, cols = own_ref.shape[1:]
    south, north = pl.ds(0, HALO), pl.ds(rows - HALO, HALO)
    odd = jnp.broadcast_to(lax.rem(lax.axis_index("lat"), 2), (HALO, cols)) > 0
    for f in range(FIELDS):
        south_edge, north_edge = own_ref[f, south, :], own_ref[f, north, :]
        part = slice(f * cols, (f + 1) * cols)
        lat_near_ref[:, part] = jnp.where(odd, south_edge, north_edge)
        lat_far_ref[:, part] = jnp.where(odd, north_edge, south_edge)
    odd = odd[:, :LANES]
    south_edge, north_edge = west_edge_ref[south, :], west_edge_ref[north, :]
    part = slice(FIELDS * cols, FIELDS * cols + LANES)
    lat_near_ref[:, part] = jnp.where(odd, south_edge, north_edge)
    lat_far_ref[:, part] = jnp.where(odd, north_edge, south_edge)


def faces(depth, across, along):
    count = len(depth)
    east_face = [jnp.minimum(depth[t], lane_shift(depth[t], 1)) * across[t] for t in range(count)]
    north_face = [jnp.minimum(depth[t], north_of(depth, t)) * along[t] for t in range(count)]
    return east_face, north_face


def level_down(level, east_face, north_face, source_term, source):
    stride = 1 << level
    count = len(source)
    inverse, diagonal = [], []
    for t in range(count):
        total = source_term[t] + (
            (east_face[t] + lane_shift(east_face[t], -stride))
            + (north_face[t] + south_of(north_face, t))
        )
        diagonal.append(jnp.where(source_term[t] > 0.0, total, 1.0))
        inverse.append(DAMPING / diagonal[t])
    field = [inverse[t] * source[t] for t in range(count)]
    for _ in range(SWEEPS - 1):
        field = sweep(field, source, inverse, east_face, north_face, stride)
    image = remainder(field, source, diagonal, east_face, north_face, stride)
    kept = (east_face, north_face, inverse, source, field, diagonal)

    def coarse(tiles):
        sums = [tiles[t] + tiles[t + 1] for t in range(0, count, 2)]
        return [value + lane_shift(value, stride) for value in sums]

    east_next = [lane_shift(east_face[t] + east_face[t + 1], stride) for t in range(0, count, 2)]
    north_next = [north_face[t] + lane_shift(north_face[t], stride) for t in range(1, count, 2)]
    return kept, (east_next, north_next, coarse(source_term), coarse(image))


def lay_out(lat_count, own_ref, lat_near_ref, lat_far_ref, west_ref, west_far_ref, east_ref, scale_ref, grid_ref):
    rows, cols = own_ref.shape[1], own_ref.shape[2]
    columns, height = grid_ref.shape[1], grid_ref.shape[2]
    count = height // TILE
    own_columns = cols // LANES
    lat_odd = lax.rem(lax.axis_index("lat"), 2)
    near_row = rows + pl.multiple_of(lat_odd * HALO, HALO)
    far_row = rows + pl.multiple_of((1 - lat_odd) * HALO, HALO)
    edge = FIELDS * cols + LANES
    parts = (
        (0, 0, west_ref, [own_ref.at[f] for f in range(FIELDS)]),
        (near_row, rows, lat_near_ref.at[:, pl.ds(edge, LANES)],
         [lat_near_ref.at[:, pl.ds(f * cols, cols)] for f in range(FIELDS)]),
        (far_row, rows + HALO, west_far_ref, [lat_far_ref.at[:, pl.ds(f * cols, cols)] for f in range(FIELDS)]),
    )
    last = LANES // HALO - 1
    for first, at, side_ref, bodies in parts:
        west = side_ref[...]
        slot = iota(west.shape, 1) // HALO
        lat_index = lax.axis_index("lat")
        outside = jnp.broadcast_to((lat_index == 0) | (lat_index == lat_count - 1), west.shape)
        for f, body in enumerate(bodies):
            for c in range(own_columns):
                value = body[:, c * LANES : (c + 1) * LANES]
                if first is far_row:
                    value = jnp.where(outside, 0.0, value)
                grid_ref[f, c, pl.ds(first, west.shape[0]), :] = value
            side = jnp.where(slot == (f + last) % (last + 1), west, 0.0)
            if east_ref is not None:
                side = jnp.where(slot == f, east_ref[pl.ds(at, west.shape[0]), :], side)
            if first is far_row:
                side = jnp.where(outside, 0.0, side)
            grid_ref[f, own_columns, pl.ds(first, west.shape[0]), :] = lane_shift(side, f * HALO)

    def load(f):
        return [
            jnp.concatenate(
                [grid_ref[f, c, pl.ds(t, TILE, stride=count), :] for c in range(columns)], axis=1
            )
            for t in range(count)
        ]

    depth, source_term, source = load(0), load(1), load(2)
    across = [jnp.concatenate([scale_ref[0, t]] * columns, axis=1) for t in range(count)]
    along = [jnp.concatenate([scale_ref[1, t]] * columns, axis=1) for t in range(count)]
    return faces(depth, across, along) + (source_term, source)


def hold(lat_count, own_ref, lat_near_ref, lat_far_ref, west_ref, west_far_ref, east_ref, scale_ref, *rest):
    level_refs = [rest[5 * i : 5 * i + 5] for i in range(LEVELS)]
    diagonal_ref, grid_ref = rest[5 * LEVELS :]
    state = lay_out(lat_count, own_ref, lat_near_ref, lat_far_ref, west_ref, west_far_ref, east_ref, scale_ref,
                    grid_ref)
    for level in range(LEVELS):
        kept, state = level_down(level, *state)
        for ref, tiles in zip(level_refs[level], kept):
            keep(ref, tiles)
        if level == 0:
            keep(diagonal_ref, kept[-1])


def descend(lat_count, own_ref, lat_near_ref, lat_far_ref, west_ref, west_far_ref, west_edge_ref, scale_ref,
            pack_ref, edge_ref, grid_ref):
    rows = own_ref.shape[1]
    edge = slice(FIELDS * own_ref.shape[2], FIELDS * own_ref.shape[2] + LANES)
    edge_ref[pl.ds(0, rows), :] = west_edge_ref[...]
    edge_ref[pl.ds(rows, HALO), :] = lat_near_ref[:, edge]
    edge_ref[pl.ds(rows + HALO, HALO), :] = lat_far_ref[:, edge]
    lon_index = lax.axis_index("lon")
    cols = own_ref.shape[2]
    own_columns = cols // LANES
    columns = grid_ref.shape[1]
    state = lay_out(lat_count, own_ref, lat_near_ref, lat_far_ref, west_ref, west_far_ref, None, scale_ref,
                    grid_ref)
    for level in range(LEVELS):
        _, state = level_down(level, *state)

    east_face, north_face, source_term, source = state
    stride = 1 << LEVELS
    bottom_width = cols // stride
    group = LANES // bottom_width
    per_column = LANES // stride
    tiles = len(source)
    lane = iota((TILE, LANES), 1)
    cell = lane % bottom_width - SHIFT
    column = jnp.where(cell < 0, own_columns, cell // per_column)
    pick = jnp.where(cell < 0, LANES + cell * stride, (cell % per_column) * stride)
    turn = lax.rem(lane // bottom_width + group - lax.rem(lon_index, group), group)
    own_rows = pack_ref.shape[1] // tiles
    for t in range(tiles):
        packed = jnp.zeros((TILE, LANES), jnp.float32)
        for f, value in enumerate((source[t], east_face[t], north_face[t], source_term[t])):
            flat = jnp.zeros((TILE, LANES), jnp.float32)
            for c in range(columns):
                taken = jnp.take_along_axis(value[:, c * LANES : (c + 1) * LANES], pick, axis=1)
                flat = jnp.where(column == c, taken, flat)
            packed = jnp.where(turn == f, flat, packed)
        for k in range(pack_ref.shape[0]):
            pack_ref[k, pl.ds(t, own_rows, stride=tiles), :] = packed[:own_rows]


def total_of(tiles):
    parts = list(tiles)
    while len(parts) > 1:
        parts = [
            parts[i] + parts[i + 1] if i + 1 < len(parts) else parts[i] for i in range(0, len(parts), 2)
        ]
    value = parts[0]
    value = sum(value[:, c : c + LANES] for c in range(0, value.shape[1], LANES))
    return jnp.sum(jnp.sum(value, axis=0, keepdims=True), axis=1, keepdims=True)


def conjugate(source, east_face, north_face, source_term):
    height = source.shape[0]

    def split(value):
        return [value[r : r + TILE] for r in range(0, height, TILE)]

    def up(value):
        return pltpu.roll(value, height - 1, 0)

    def down(value):
        return pltpu.roll(value, 1, 0)

    diagonal = source_term + (
        (east_face + lane_shift(east_face, -1)) + (north_face + down(north_face))
    )
    iterate = jnp.zeros_like(source)
    remain = source
    direction = source
    for _ in range(BOTTOM_ITERS):
        image = diagonal * direction - (
            (east_face * lane_shift(direction, 1) + lane_shift(east_face * direction, -1))
            + (north_face * up(direction) + down(north_face * direction))
        )
        norm = total_of(split(remain * remain))
        energy = total_of(split(direction * image))
        cross = total_of(split(remain * image))
        square = total_of(split(image * image))
        step_size = norm / energy
        iterate = iterate + step_size * direction
        remain = remain - step_size * image
        norm_next = norm - step_size * (2.0 * cross - step_size * square)
        direction = remain + (norm_next / norm) * direction
    return iterate


def ascend(lat_count, lon_count, blocks_ref, *rest):
    level_refs = [rest[5 * i : 5 * i + 5] for i in range(LEVELS)]
    diagonal_ref, solution_ref, residual_ref, window_ref, turn_ref, order_ref, sems = rest[5 * LEVELS :]
    lon_index = lax.axis_index("lon")
    lat_index = lax.axis_index("lat")
    rows, cols = solution_ref.shape
    count, width = diagonal_ref.shape[0], diagonal_ref.shape[2]
    own_columns = cols // LANES
    columns = width // LANES
    stride = 1 << LEVELS
    bottom_rows = rows // stride
    bottom_width = cols // stride
    group = LANES // bottom_width
    slot = iota((bottom_rows, LANES), 1) // bottom_width
    fields = []
    for f in range(4):
        strips = []
        for a in range(lat_count):
            pieces = []
            for c in range(lon_count // group):
                merged = None
                for j in range(group):
                    block = blocks_ref[(c * group + j) * lat_count + a]
                    merged = block if merged is None else jnp.where(slot == (f + j) % group, block, merged)
                pieces.append(lane_shift(merged, f * bottom_width))
            strips.append(jnp.concatenate(pieces, axis=1))
        fields.append(jnp.concatenate(strips, axis=0))
    iterate = conjugate(*fields)

    bottom_height = lat_count * bottom_rows
    whole_width = lon_count * bottom_width
    pad = 2 * TILE
    window_ref[pl.ds(0, pad), :] = jnp.zeros((pad, LANES), jnp.float32)
    window_ref[pl.ds(pad + bottom_height, pad), :] = jnp.zeros((pad, LANES), jnp.float32)
    half = LANES // 2
    margin = half // stride
    shift = lax.rem(margin - SHIFT - lon_index * bottom_width + whole_width, whole_width)
    window_ref[pl.ds(pad, bottom_height), :] = pltpu.roll(iterate, shift, 1)[:, :LANES]
    start = pl.multiple_of(lat_index * bottom_rows, TILE)
    turn_ref[...] = window_ref[pl.ds(start, 5 * TILE), :]
    tiles = count >> LEVELS
    lane = iota((TILE, LANES), 1)
    ahead = (rows + HALO) // stride // tiles
    sublane = iota((TILE, LANES), 0)
    correction = []
    for t in range(tiles):
        upper = turn_ref[pl.ds(pad + t, TILE, stride=tiles), :]
        lower = turn_ref[pl.ds(pad + t - tiles * TILE, TILE, stride=tiles), :]
        value = jnp.where(sublane < ahead, upper, lower)
        parts = []
        for c in range(columns):
            if c < own_columns:
                pick = margin + (c * LANES + lane) // stride
            else:
                pick = jnp.where(lane < half, margin + bottom_width + lane // stride, (lane - half) // stride)
            parts.append(jnp.take_along_axis(value, pick, axis=1))
        correction.append(jnp.concatenate(parts, axis=1))

    lane = iota((TILE, width), 1)
    for level in range(LEVELS - 1, -1, -1):
        stride = 1 << level
        east_face, north_face, inverse, source, field = map(tiles_of, level_refs[level])
        if level < LEVELS - 1:
            first = lax.rem(lane // stride, 2) == 0
            correction = [jnp.where(first, value, lane_shift(value, -stride)) for value in correction]
        spread = [correction[t // 2] for t in range(count >> level)]
        if level == 0:
            sea = [east_face[t] + north_face[t] > 0.0 for t in range(count)]
            spread = [jnp.where(sea[t], spread[t], 0.0) for t in range(count)]
        field = [field[t] + spread[t] for t in range(count >> level)]
        for _ in range(SWEEPS):
            field = sweep(field, source, inverse, east_face, north_face, stride)
        correction = field
    own_sublanes = rows // count

    def send_out(k, ref, tiles):
        copies = []
        for c in range(own_columns):
            part = slice(c * LANES, (c + 1) * LANES)
            for t in range(count):
                order_ref[k, c, pl.ds(t, own_sublanes, stride=count), :] = tiles[t][:own_sublanes, part]
            copies.append(pltpu.make_async_copy(order_ref.at[k, c], ref.at[:, part], sems.at[k, c]))
            copies[-1].start()
        return copies

    copies = send_out(0, solution_ref, correction)
    final = remainder(correction, source, tiles_of(diagonal_ref), east_face, north_face, 1)
    copies += send_out(1, residual_ref, final)
    for copy in copies:
        copy.wait()


def swap_pairs(count, first):
    pairs = []
    for i in range(first, count, 2):
        j = (i + 1) % count
        pairs += [(i, j), (j, i)]
    return pairs


def on_device(lat_count, lon_count, forcing, surface_term, sea_cells, levels):
    rows, cols = forcing.shape
    height, width = rows + 2 * HALO, cols + LANES
    count = height // TILE
    f32 = jnp.float32
    vmem = pl.BlockSpec(memory_space=pltpu.VMEM)
    hbm = pl.BlockSpec(memory_space=pltpu.HBM)
    params = pltpu.CompilerParams(vmem_limit_bytes=VMEM_LIMIT)
    lat_index = lax.axis_index("lat").astype(jnp.int32)
    inputs = [
        pltpu.with_memory_space_constraint(x, pltpu.HBM) for x in (forcing, surface_term, sea_cells, levels)
    ]
    own, east_edge, west_edge = pl.pallas_call(
        prepare,
        out_shape=[
            jax.ShapeDtypeStruct((FIELDS, rows, cols), f32),
            jax.ShapeDtypeStruct((rows, LANES), f32),
            jax.ShapeDtypeStruct((rows, LANES), f32),
        ],
        in_specs=[hbm] * 4,
        out_specs=[vmem] * 3,
        scratch_shapes=[
            pltpu.VMEM((rows, cols), f32),
            pltpu.VMEM((rows, cols), f32),
            pltpu.VMEM((rows, cols), jnp.int32),
            pltpu.VMEM((rows, cols), jnp.int32),
            pltpu.SemaphoreType.DMA((4,)),
        ],
        compiler_params=params,
        name="prepare",
    )(*inputs)

    diagonal_edge = pl.pallas_call(
        prepare_corner,
        out_shape=jax.ShapeDtypeStruct((HALO, LANES), f32),
        in_specs=[vmem],
        out_specs=vmem,
        compiler_params=params,
        name="prepare_corner",
    )(east_edge)
    lat_near, lat_far = pl.pallas_call(
        prepare_rows,
        out_shape=[jax.ShapeDtypeStruct((HALO, FIELDS * cols + LANES), f32)] * 2,
        in_specs=[vmem] * 2,
        out_specs=[vmem] * 2,
        compiler_params=params,
        name="prepare_rows",
    )(own, west_edge)

    eastward = [(i, (i + 1) % lon_count) for i in range(lon_count)]
    westward = [(target, source) for source, target in eastward]
    near_pairs, far_pairs = swap_pairs(lat_count, 0), swap_pairs(lat_count, 1)
    across_pairs = [
        (i * lat_count + a, (i + 1) % lon_count * lat_count + b) for i in range(lon_count) for a, b in far_pairs
    ]
    west_halo = lax.ppermute(east_edge, "lon", eastward)
    lat_far = lax.ppermute(lat_far, "lat", far_pairs)
    west_far = lax.ppermute(diagonal_edge, ("lon", "lat"), across_pairs)
    odd = lat_index % 2 == 1
    lat_near = lax.ppermute(
        jnp.concatenate([lat_near, jnp.where(odd, west_halo[:HALO], west_halo[rows - HALO :])], axis=1),
        "lat",
        near_pairs,
    )

    row = jnp.arange(TILE)[None, :] * count + jnp.arange(count)[:, None]
    row = jnp.where(row < rows + HALO, row, row - height).astype(f32) + (lat_index * rows).astype(f32)
    center, northern = metric(row)
    scale = jnp.broadcast_to(jnp.stack([1.0 / center, northern])[..., None], (2, count, TILE, LANES))

    devices = lat_count * lon_count
    grid = pltpu.VMEM((FIELDS, width // LANES, height, LANES), f32)
    packed, edges = pl.pallas_call(
        functools.partial(descend, lat_count),
        out_shape=[
            jax.ShapeDtypeStruct((devices, rows >> LEVELS, LANES), f32),
            jax.ShapeDtypeStruct((height, LANES), f32),
        ],
        in_specs=[vmem] * 7,
        out_specs=[vmem] * 2,
        scratch_shapes=[grid],
        compiler_params=params,
        name="descend",
    )(own, lat_near, lat_far, west_halo, west_far, west_edge, scale)
    east_halo = lax.ppermute(edges, "lon", westward)
    blocks = lax.all_to_all(packed, ("lon", "lat"), 0, 0, tiled=True)

    level_shapes = []
    for level in range(LEVELS):
        level_shapes += [jax.ShapeDtypeStruct((count >> level, TILE, width), f32)] * 5
    held = pl.pallas_call(
        functools.partial(hold, lat_count),
        out_shape=level_shapes + [jax.ShapeDtypeStruct((count, TILE, width), f32)],
        in_specs=[vmem] * 7,
        out_specs=[vmem] * (1 + len(level_shapes)),
        scratch_shapes=[grid],
        compiler_params=params,
        cost_estimate=pl.CostEstimate(flops=0, bytes_accessed=60 * 1024 * 1024, transcendentals=0),
        name="hold",
    )(own, lat_near, lat_far, west_halo, west_far, east_halo, scale)

    return pl.pallas_call(
        functools.partial(ascend, lat_count, lon_count),
        out_shape=[jax.ShapeDtypeStruct((rows, cols), f32)] * 2,
        in_specs=[vmem] * (1 + len(held)),
        out_specs=[hbm] * 2,
        scratch_shapes=[
            pltpu.VMEM((lat_count * (rows >> LEVELS) + 4 * TILE, LANES), f32),
            pltpu.VMEM((5 * TILE, LANES), f32),
            pltpu.VMEM((2, cols // LANES, rows, LANES), f32),
            pltpu.SemaphoreType.DMA((2, cols // LANES)),
        ],
        compiler_params=params,
        name="ascend",
    )(blocks, *held)


def solution(mesh):
    body = functools.partial(on_device, mesh.shape["lat"], mesh.shape["lon"])
    return jax.shard_map(
        body,
        mesh=mesh,
        in_specs=(P("lat", "lon"),) * 4,
        out_specs=(P("lat", "lon"),) * 2,
        check_vma=False,
    )
```

```python
import functools

import jax
import jax.numpy as jnp
from jax import lax
from jax.experimental import pallas as pl
from jax.experimental.pallas import tpu as pltpu
from jax.sharding import PartitionSpec as P

LEVELS = 3
SWEEPS = 2
BOTTOM_ITERS = 6

DAMPING = 0.8
ROW_STEP = 150.0 / 8640.0
BAND_SOUTH = -50.0

HALO = 32
LANES = 128
TILE = 8
FIELDS = 3
SHIFT = 2
VMEM_LIMIT = 8 * 1024 * 1024


def iota(shape, dim):
    return lax.broadcasted_iota(jnp.int32, shape, dim)


def lane_shift(field, count):
    return pltpu.roll(field, (-count) % field.shape[1], 1)


def north_of(tiles, t):
    if t + 1 < len(tiles):
        return tiles[t + 1]
    return pltpu.roll(tiles[0], TILE - 1, 0)


def south_of(tiles, t):
    if t > 0:
        return tiles[t - 1]
    return pltpu.roll(tiles[-1], 1, 0)


def neighbour_sum(field, east_face, north_face, stride):
    upward = [north_face[t] * field[t] for t in range(len(field))]
    return [
        (east_face[t] * lane_shift(field[t], stride) + lane_shift(east_face[t] * field[t], -stride))
        + (north_face[t] * north_of(field, t) + south_of(upward, t))
        for t in range(len(field))
    ]


def sweep(field, source, inverse, east_face, north_face, stride):
    around = neighbour_sum(field, east_face, north_face, stride)
    return [
        (1.0 - DAMPING) * field[t] + inverse[t] * (source[t] + around[t]) for t in range(len(field))
    ]


def remainder(field, source, diagonal, east_face, north_face, stride):
    around = neighbour_sum(field, east_face, north_face, stride)
    return [source[t] - diagonal[t] * field[t] + around[t] for t in range(len(field))]


def tiles_of(ref):
    return [ref[t] for t in range(ref.shape[0])]


def keep(ref, tiles):
    for t, value in enumerate(tiles):
        ref[t] = value


def metric(row):
    center = jnp.cos(jnp.deg2rad(BAND_SOUTH + ROW_STEP * (row + 0.5)))
    northern = jnp.cos(jnp.deg2rad(BAND_SOUTH + ROW_STEP * (row + 1.0)))
    return center, northern


def prepare(forcing_ref, surface_ref, sea_ref, levels_ref,
            own_ref, east_edge_ref, west_edge_ref,
            forcing_buf, surface_buf, sea_buf, levels_buf, sems):
    copies = [
        pltpu.make_async_copy(source, target, sems.at[i])
        for i, (source, target) in enumerate((
            (levels_ref, levels_buf), (sea_ref, sea_buf), (surface_ref, surface_buf), (forcing_ref, forcing_buf),
        ))
    ]
    for copy in copies:
        copy.start()
    rows, cols = forcing_buf.shape
    first_row = lax.axis_index("lat") * rows
    row = (iota((rows, LANES), 0) + first_row).astype(jnp.float32)
    center = jnp.cos(jnp.deg2rad(BAND_SOUTH + ROW_STEP * (row + 0.5)))
    center = jnp.concatenate([center] * (cols // LANES), axis=1)
    for copy in copies:
        copy.wait()
    sea_mask = sea_buf[...].astype(jnp.float32)
    layers = levels_buf[...].astype(jnp.float32)
    depth = sea_mask * ((layers + layers * (layers - 1.0) / 20.0) / 200.0)
    fields = (depth, surface_buf[...] * center * sea_mask, forcing_buf[...] * sea_mask)
    slot = iota((rows, LANES), 1) // HALO
    slots = LANES // HALO
    west_edge = jnp.zeros((rows, LANES), jnp.float32)
    east_edge = jnp.zeros((rows, LANES), jnp.float32)
    for f, value in enumerate(fields):
        own_ref[f] = value
        west_edge = jnp.where(slot == f, lane_shift(value[:, :LANES], -f * HALO), west_edge)
        east_edge = jnp.where(
            slot == (f + slots - 1) % slots, lane_shift(value[:, cols - LANES :], -f * HALO), east_edge
        )
    east_edge_ref[...] = east_edge
    west_edge_ref[...] = west_edge


def prepare_corner(east_edge_ref, rows_ref, diagonal_edge_ref):
    rows = east_edge_ref.shape[0]
    odd = jnp.broadcast_to(lax.rem(lax.axis_index("lat"), 2), diagonal_edge_ref.shape) > 0
    diagonal_edge_ref[...] = jnp.where(odd, east_edge_ref[pl.ds(rows - HALO, HALO), :], east_edge_ref[pl.ds(0, HALO), :])


def prepare_rows(own_ref, west_edge_ref, lat_near_ref, lat_far_ref):
    rows, cols = own_ref.shape[1:]
    south, north = pl.ds(0, HALO), pl.ds(rows - HALO, HALO)
    odd = jnp.broadcast_to(lax.rem(lax.axis_index("lat"), 2), (HALO, cols)) > 0
    for f in range(FIELDS):
        south_edge, north_edge = own_ref[f, south, :], own_ref[f, north, :]
        part = slice(f * cols, (f + 1) * cols)
        lat_near_ref[:, part] = jnp.where(odd, south_edge, north_edge)
        lat_far_ref[:, part] = jnp.where(odd, north_edge, south_edge)
    odd = odd[:, :LANES]
    south_edge, north_edge = west_edge_ref[south, :], west_edge_ref[north, :]
    part = slice(FIELDS * cols, FIELDS * cols + LANES)
    lat_near_ref[:, part] = jnp.where(odd, south_edge, north_edge)
    lat_far_ref[:, part] = jnp.where(odd, north_edge, south_edge)


def faces(depth, across, along):
    count = len(depth)
    east_face = [jnp.minimum(depth[t], lane_shift(depth[t], 1)) * across[t] for t in range(count)]
    north_face = [jnp.minimum(depth[t], north_of(depth, t)) * along[t] for t in range(count)]
    return east_face, north_face


def level_down(level, east_face, north_face, source_term, source):
    stride = 1 << level
    count = len(source)
    inverse, diagonal = [], []
    for t in range(count):
        total = source_term[t] + (
            (east_face[t] + lane_shift(east_face[t], -stride))
            + (north_face[t] + south_of(north_face, t))
        )
        diagonal.append(jnp.where(source_term[t] > 0.0, total, 1.0))
        inverse.append(DAMPING / diagonal[t])
    field = [inverse[t] * source[t] for t in range(count)]
    for _ in range(SWEEPS - 1):
        field = sweep(field, source, inverse, east_face, north_face, stride)
    image = remainder(field, source, diagonal, east_face, north_face, stride)
    kept = (east_face, north_face, inverse, source, field, diagonal)

    def coarse(tiles):
        sums = [tiles[t] + tiles[t + 1] for t in range(0, count, 2)]
        return [value + lane_shift(value, stride) for value in sums]

    east_next = [lane_shift(east_face[t] + east_face[t + 1], stride) for t in range(0, count, 2)]
    north_next = [north_face[t] + lane_shift(north_face[t], stride) for t in range(1, count, 2)]
    return kept, (east_next, north_next, coarse(source_term), coarse(image))


def lay_out(lat_count, own_ref, lat_near_ref, lat_far_ref, west_ref, west_far_ref, east_ref, scale_ref, grid_ref):
    rows, cols = own_ref.shape[1], own_ref.shape[2]
    columns, height = grid_ref.shape[1], grid_ref.shape[2]
    count = height // TILE
    own_columns = cols // LANES
    lat_odd = lax.rem(lax.axis_index("lat"), 2)
    near_row = rows + pl.multiple_of(lat_odd * HALO, HALO)
    far_row = rows + pl.multiple_of((1 - lat_odd) * HALO, HALO)
    edge = FIELDS * cols + LANES
    parts = (
        (0, 0, west_ref, [own_ref.at[f] for f in range(FIELDS)]),
        (near_row, rows, lat_near_ref.at[:, pl.ds(edge, LANES)],
         [lat_near_ref.at[:, pl.ds(f * cols, cols)] for f in range(FIELDS)]),
        (far_row, rows + HALO, west_far_ref, [lat_far_ref.at[:, pl.ds(f * cols, cols)] for f in range(FIELDS)]),
    )
    last = LANES // HALO - 1
    for first, at, side_ref, bodies in parts:
        west = side_ref[...]
        slot = iota(west.shape, 1) // HALO
        lat_index = lax.axis_index("lat")
        outside = jnp.broadcast_to((lat_index == 0) | (lat_index == lat_count - 1), west.shape)
        for f, body in enumerate(bodies):
            for c in range(own_columns):
                value = body[:, c * LANES : (c + 1) * LANES]
                if first is far_row:
                    value = jnp.where(outside, 0.0, value)
                grid_ref[f, c, pl.ds(first, west.shape[0]), :] = value
            side = jnp.where(slot == (f + last) % (last + 1), west, 0.0)
            if east_ref is not None:
                side = jnp.where(slot == f, east_ref[pl.ds(at, west.shape[0]), :], side)
            if first is far_row:
                side = jnp.where(outside, 0.0, side)
            grid_ref[f, own_columns, pl.ds(first, west.shape[0]), :] = lane_shift(side, f * HALO)

    def load(f):
        return [
            jnp.concatenate(
                [grid_ref[f, c, pl.ds(t, TILE, stride=count), :] for c in range(columns)], axis=1
            )
            for t in range(count)
        ]

    depth, source_term, source = load(0), load(1), load(2)
    across = [jnp.concatenate([scale_ref[0, t]] * columns, axis=1) for t in range(count)]
    along = [jnp.concatenate([scale_ref[1, t]] * columns, axis=1) for t in range(count)]
    return faces(depth, across, along) + (source_term, source)


def hold(lat_count, own_ref, lat_near_ref, lat_far_ref, west_ref, west_far_ref, east_ref, scale_ref, *rest):
    level_refs = [rest[5 * i : 5 * i + 5] for i in range(LEVELS)]
    diagonal_ref, grid_ref = rest[5 * LEVELS :]
    state = lay_out(lat_count, own_ref, lat_near_ref, lat_far_ref, west_ref, west_far_ref, east_ref, scale_ref,
                    grid_ref)
    for level in range(LEVELS):
        kept, state = level_down(level, *state)
        for ref, tiles in zip(level_refs[level], kept):
            keep(ref, tiles)
        if level == 0:
            keep(diagonal_ref, kept[-1])


def descend(lat_count, own_ref, lat_near_ref, lat_far_ref, west_ref, west_far_ref, west_edge_ref, scale_ref,
            pack_ref, edge_ref, grid_ref):
    rows = own_ref.shape[1]
    edge = slice(FIELDS * own_ref.shape[2], FIELDS * own_ref.shape[2] + LANES)
    edge_ref[pl.ds(0, rows), :] = west_edge_ref[...]
    edge_ref[pl.ds(rows, HALO), :] = lat_near_ref[:, edge]
    edge_ref[pl.ds(rows + HALO, HALO), :] = lat_far_ref[:, edge]
    lon_index = lax.axis_index("lon")
    cols = own_ref.shape[2]
    own_columns = cols // LANES
    columns = grid_ref.shape[1]
    state = lay_out(lat_count, own_ref, lat_near_ref, lat_far_ref, west_ref, west_far_ref, None, scale_ref,
                    grid_ref)
    for level in range(LEVELS):
        _, state = level_down(level, *state)

    east_face, north_face, source_term, source = state
    stride = 1 << LEVELS
    bottom_width = cols // stride
    group = LANES // bottom_width
    per_column = LANES // stride
    tiles = len(source)
    lane = iota((TILE, LANES), 1)
    cell = lane % bottom_width - SHIFT
    column = jnp.where(cell < 0, own_columns, cell // per_column)
    pick = jnp.where(cell < 0, LANES + cell * stride, (cell % per_column) * stride)
    turn = lax.rem(lane // bottom_width + group - lax.rem(lon_index, group), group)
    own_rows = pack_ref.shape[1] // tiles
    for t in range(tiles):
        packed = jnp.zeros((TILE, LANES), jnp.float32)
        for f, value in enumerate((source[t], east_face[t], north_face[t], source_term[t])):
            flat = jnp.zeros((TILE, LANES), jnp.float32)
            for c in range(columns):
                taken = jnp.take_along_axis(value[:, c * LANES : (c + 1) * LANES], pick, axis=1)
                flat = jnp.where(column == c, taken, flat)
            packed = jnp.where(turn == f, flat, packed)
        for k in range(pack_ref.shape[0]):
            pack_ref[k, pl.ds(t, own_rows, stride=tiles), :] = packed[:own_rows]


def total_of(tiles):
    parts = list(tiles)
    while len(parts) > 1:
        parts = [
            parts[i] + parts[i + 1] if i + 1 < len(parts) else parts[i] for i in range(0, len(parts), 2)
        ]
    value = parts[0]
    value = sum(value[:, c : c + LANES] for c in range(0, value.shape[1], LANES))
    return jnp.sum(jnp.sum(value, axis=0, keepdims=True), axis=1, keepdims=True)


def conjugate(source, east_face, north_face, source_term):
    height = source.shape[0]

    def split(value):
        return [value[r : r + TILE] for r in range(0, height, TILE)]

    def up(value):
        return pltpu.roll(value, height - 1, 0)

    def down(value):
        return pltpu.roll(value, 1, 0)

    west_face = lane_shift(east_face, -1)
    south_face = down(north_face)
    diagonal = source_term + ((east_face + west_face) + (north_face + south_face))

    def apply(value):
        return diagonal * value - (
            (east_face * lane_shift(value, 1) + west_face * lane_shift(value, -1))
            + (north_face * up(value) + south_face * down(value))
        )

    iterate = jnp.zeros_like(source)
    remain = source
    image_r = apply(source)
    direction = image_d = second = step_size = norm = None
    for step in range(BOTTOM_ITERS):
        norm_now = total_of(split(remain * remain))
        energy = total_of(split(remain * image_r))
        last = step == BOTTOM_ITERS - 1
        ahead = None if last else apply(image_r)
        if step == 0:
            step_size = norm_now / energy
            direction, image_d, second = remain, image_r, ahead
        else:
            ratio = norm_now / norm
            step_size = norm_now / (energy - ratio * (norm_now / step_size))
            direction = remain + ratio * direction
            if not last:
                image_d = image_r + ratio * image_d
                second = ahead + ratio * second
        norm = norm_now
        iterate = iterate + step_size * direction
        if not last:
            remain = remain - step_size * image_d
            image_r = image_r - step_size * second
    return iterate


def ascend(lat_count, lon_count, blocks_ref, *rest):
    level_refs = [rest[5 * i : 5 * i + 5] for i in range(LEVELS)]
    diagonal_ref, solution_ref, residual_ref, window_ref, order_ref, sems = rest[5 * LEVELS :]
    lon_index = lax.axis_index("lon")
    lat_index = lax.axis_index("lat")
    rows, cols = solution_ref.shape
    count, width = diagonal_ref.shape[0], diagonal_ref.shape[2]
    own_columns = cols // LANES
    columns = width // LANES
    stride = 1 << LEVELS
    bottom_rows = rows // stride
    bottom_width = cols // stride
    group = LANES // bottom_width
    slot = iota((bottom_rows, LANES), 1) // bottom_width
    fields = []
    for f in range(4):
        strips = []
        for a in range(lat_count):
            pieces = []
            for c in range(lon_count // group):
                merged = None
                for j in range(group):
                    block = blocks_ref[(c * group + j) * lat_count + a]
                    merged = block if merged is None else jnp.where(slot == (f + j) % group, block, merged)
                pieces.append(lane_shift(merged, f * bottom_width))
            strips.append(jnp.concatenate(pieces, axis=1))
        fields.append(jnp.concatenate(strips, axis=0))
    iterate = conjugate(*fields)

    bottom_height = lat_count * bottom_rows
    whole_width = lon_count * bottom_width
    pad = 2 * TILE
    window_ref[pl.ds(0, pad), :] = jnp.zeros((pad, LANES), jnp.float32)
    window_ref[pl.ds(pad + bottom_height, pad), :] = jnp.zeros((pad, LANES), jnp.float32)
    half = LANES // 2
    margin = half // stride
    shift = lax.rem(margin - SHIFT - lon_index * bottom_width + whole_width, whole_width)
    window_ref[pl.ds(pad, bottom_height), :] = pltpu.roll(iterate, shift, 1)[:, :LANES]
    start = pl.multiple_of(lat_index * bottom_rows, TILE)
    tiles = count >> LEVELS
    lane = iota((TILE, LANES), 1)
    ahead = (rows + HALO) // stride // tiles
    sublane = iota((TILE, LANES), 0)
    correction = []
    for t in range(tiles):
        upper = window_ref[pl.ds(start + pad + t, TILE, stride=tiles), :]
        lower = window_ref[pl.ds(start + pad + t - tiles * TILE, TILE, stride=tiles), :]
        value = jnp.where(sublane < ahead, upper, lower)
        parts = []
        for c in range(columns):
            if c < own_columns:
                pick = margin + (c * LANES + lane) // stride
            else:
                pick = jnp.where(lane < half, margin + bottom_width + lane // stride, (lane - half) // stride)
            parts.append(jnp.take_along_axis(value, pick, axis=1))
        correction.append(jnp.concatenate(parts, axis=1))

    lane = iota((TILE, width), 1)
    for level in range(LEVELS - 1, -1, -1):
        stride = 1 << level
        east_face, north_face, inverse, source, field = map(tiles_of, level_refs[level])
        if level < LEVELS - 1:
            first = lax.rem(lane // stride, 2) == 0
            correction = [jnp.where(first, value, lane_shift(value, -stride)) for value in correction]
        spread = [correction[t // 2] for t in range(count >> level)]
        if level == 0:
            sea = [east_face[t] + north_face[t] > 0.0 for t in range(count)]
            spread = [jnp.where(sea[t], spread[t], 0.0) for t in range(count)]
        field = [field[t] + spread[t] for t in range(count >> level)]
        for _ in range(SWEEPS):
            field = sweep(field, source, inverse, east_face, north_face, stride)
        correction = field
    own_sublanes = rows // count

    def send_out(k, ref, tiles):
        copies = []
        for c in range(own_columns):
            part = slice(c * LANES, (c + 1) * LANES)
            for t in range(count):
                order_ref[k, c, pl.ds(t, own_sublanes, stride=count), :] = tiles[t][:own_sublanes, part]
            copies.append(pltpu.make_async_copy(order_ref.at[k, c], ref.at[:, part], sems.at[k, c]))
            copies[-1].start()
        return copies

    copies = send_out(0, solution_ref, correction)
    final = remainder(correction, source, tiles_of(diagonal_ref), east_face, north_face, 1)
    copies += send_out(1, residual_ref, final)
    for copy in copies:
        copy.wait()


def near_pairs(lat_count):
    return [(a, a ^ 1) for a in range(lat_count)]


def far_pairs(lon_count, lat_count, east):
    pairs = []
    for i in range(lon_count):
        for a in range(lat_count):
            b = a + 1 if a % 2 else a - 1
            j = (i + east) % lon_count
            if b < 0 or b == lat_count:
                b, j = a, i ^ 1
            pairs.append((i * lat_count + a, j * lat_count + b))
    return pairs


def on_device(lat_count, lon_count, forcing, surface_term, sea_cells, levels):
    rows, cols = forcing.shape
    height, width = rows + 2 * HALO, cols + LANES
    count = height // TILE
    f32 = jnp.float32
    vmem = pl.BlockSpec(memory_space=pltpu.VMEM)
    hbm = pl.BlockSpec(memory_space=pltpu.HBM)
    params = pltpu.CompilerParams(vmem_limit_bytes=VMEM_LIMIT)
    lat_index = lax.axis_index("lat").astype(jnp.int32)
    inputs = [
        pltpu.with_memory_space_constraint(x, pltpu.HBM) for x in (forcing, surface_term, sea_cells, levels)
    ]
    own, east_edge, west_edge = pl.pallas_call(
        prepare,
        out_shape=[
            jax.ShapeDtypeStruct((FIELDS, rows, cols), f32),
            jax.ShapeDtypeStruct((rows, LANES), f32),
            jax.ShapeDtypeStruct((rows, LANES), f32),
        ],
        in_specs=[hbm] * 4,
        out_specs=[vmem] * 3,
        scratch_shapes=[
            pltpu.VMEM((rows, cols), f32),
            pltpu.VMEM((rows, cols), f32),
            pltpu.VMEM((rows, cols), jnp.int32),
            pltpu.VMEM((rows, cols), jnp.int32),
            pltpu.SemaphoreType.DMA((4,)),
        ],
        compiler_params=params,
        name="prepare",
    )(*inputs)

    lat_near, lat_far = pl.pallas_call(
        prepare_rows,
        out_shape=[jax.ShapeDtypeStruct((HALO, FIELDS * cols + LANES), f32)] * 2,
        in_specs=[vmem] * 2,
        out_specs=[vmem] * 2,
        compiler_params=params,
        name="prepare_rows",
    )(own, west_edge)

    diagonal_edge = pl.pallas_call(
        prepare_corner,
        out_shape=jax.ShapeDtypeStruct((HALO, LANES), f32),
        in_specs=[vmem] * 2,
        out_specs=vmem,
        compiler_params=params,
        name="prepare_corner",
    )(east_edge, lat_far)
    eastward = [(i, (i + 1) % lon_count) for i in range(lon_count)]
    westward = [(target, source) for source, target in eastward]
    west_halo = lax.ppermute(east_edge, "lon", eastward)
    lat_far = lax.ppermute(lat_far, ("lon", "lat"), far_pairs(lon_count, lat_count, 0))
    west_far = lax.ppermute(diagonal_edge, ("lon", "lat"), far_pairs(lon_count, lat_count, 1))
    odd = lat_index % 2 == 1
    lat_near = lax.ppermute(
        jnp.concatenate([lat_near, jnp.where(odd, west_halo[:HALO], west_halo[rows - HALO :])], axis=1),
        "lat",
        near_pairs(lat_count),
    )

    row = jnp.arange(TILE)[None, :] * count + jnp.arange(count)[:, None]
    row = jnp.where(row < rows + HALO, row, row - height).astype(f32) + (lat_index * rows).astype(f32)
    center, northern = metric(row)
    scale = jnp.broadcast_to(jnp.stack([1.0 / center, northern])[..., None], (2, count, TILE, LANES))

    devices = lat_count * lon_count
    grid = pltpu.VMEM((FIELDS, width // LANES, height, LANES), f32)
    packed, edges = pl.pallas_call(
        functools.partial(descend, lat_count),
        out_shape=[
            jax.ShapeDtypeStruct((devices, rows >> LEVELS, LANES), f32),
            jax.ShapeDtypeStruct((height, LANES), f32),
        ],
        in_specs=[vmem] * 7,
        out_specs=[vmem] * 2,
        scratch_shapes=[grid],
        compiler_params=params,
        name="descend",
    )(own, lat_near, lat_far, west_halo, west_far, west_edge, scale)
    east_halo = lax.ppermute(edges, "lon", westward)
    blocks = lax.all_to_all(packed, ("lon", "lat"), 0, 0, tiled=True)

    level_shapes = []
    for level in range(LEVELS):
        level_shapes += [jax.ShapeDtypeStruct((count >> level, TILE, width), f32)] * 5
    held = pl.pallas_call(
        functools.partial(hold, lat_count),
        out_shape=level_shapes + [jax.ShapeDtypeStruct((count, TILE, width), f32)],
        in_specs=[vmem] * 7,
        out_specs=[vmem] * (1 + len(level_shapes)),
        scratch_shapes=[grid],
        compiler_params=params,
        cost_estimate=pl.CostEstimate(flops=0, bytes_accessed=60 * 1024 * 1024, transcendentals=0),
        name="hold",
    )(own, lat_near, lat_far, west_halo, west_far, east_halo, scale)

    return pl.pallas_call(
        functools.partial(ascend, lat_count, lon_count),
        out_shape=[jax.ShapeDtypeStruct((rows, cols), f32)] * 2,
        in_specs=[vmem] * (1 + len(held)),
        out_specs=[hbm] * 2,
        scratch_shapes=[
            pltpu.VMEM((lat_count * (rows >> LEVELS) + 4 * TILE, LANES), f32),
            pltpu.VMEM((2, cols // LANES, rows, LANES), f32),
            pltpu.SemaphoreType.DMA((2, cols // LANES)),
        ],
        compiler_params=params,
        name="ascend",
    )(blocks, *held)


def solution(mesh):
    body = functools.partial(on_device, mesh.shape["lat"], mesh.shape["lon"])
    return jax.shard_map(
        body,
        mesh=mesh,
        in_specs=(P("lat", "lon"),) * 4,
        out_specs=(P("lat", "lon"),) * 2,
        check_vma=False,
    )
```

```python
import functools

import jax
import jax.numpy as jnp
from jax import lax
from jax.experimental import pallas as pl
from jax.experimental.pallas import tpu as pltpu
from jax.sharding import PartitionSpec as P

LEVELS = 3
SWEEPS = 2
BOTTOM_ITERS = 6

DAMPING = 0.8
ROW_STEP = 150.0 / 8640.0
BAND_SOUTH = -50.0

HALO = 32
REACH = 16
LANES = 128
TILE = 8
FIELDS = 3
KEPT = 6
SHIFT = 2
VMEM_LIMIT = 8 * 1024 * 1024


def iota(shape, dim):
    return lax.broadcasted_iota(jnp.int32, shape, dim)


def lane_shift(field, count):
    return pltpu.roll(field, (-count) % field.shape[1], 1)


def north_of(tiles, t):
    if t + 1 < len(tiles):
        return tiles[t + 1]
    return pltpu.roll(tiles[0], TILE - 1, 0)


def south_of(tiles, t):
    if t > 0:
        return tiles[t - 1]
    return pltpu.roll(tiles[-1], 1, 0)


def neighbour_sum(field, faces, stride):
    east_face, west_face, north_face = faces
    upward = [north_face[t] * field[t] for t in range(len(field))]
    return [
        (east_face[t] * lane_shift(field[t], stride) + west_face[t] * lane_shift(field[t], -stride))
        + (north_face[t] * north_of(field, t) + south_of(upward, t))
        for t in range(len(field))
    ]


def sweep(field, source, inverse, faces, stride):
    around = neighbour_sum(field, faces, stride)
    return [
        (1.0 - DAMPING) * field[t] + inverse[t] * (source[t] + around[t]) for t in range(len(field))
    ]


def remainder(field, source, diagonal, faces, stride):
    around = neighbour_sum(field, faces, stride)
    return [source[t] - diagonal[t] * field[t] + around[t] for t in range(len(field))]


def tiles_of(ref):
    return [ref[t] for t in range(ref.shape[0])]


def keep(ref, tiles):
    for t, value in enumerate(tiles):
        ref[t] = value


def metric(row):
    center = jnp.cos(jnp.deg2rad(BAND_SOUTH + ROW_STEP * (row + 0.5)))
    northern = jnp.cos(jnp.deg2rad(BAND_SOUTH + ROW_STEP * (row + 1.0)))
    return center, northern


def prepare(forcing_ref, surface_ref, sea_ref, levels_ref,
            own_ref, east_edge_ref, west_edge_ref,
            forcing_buf, surface_buf, sea_buf, levels_buf, sems):
    copies = [
        pltpu.make_async_copy(source, target, sems.at[i])
        for i, (source, target) in enumerate((
            (levels_ref, levels_buf), (sea_ref, sea_buf), (surface_ref, surface_buf), (forcing_ref, forcing_buf),
        ))
    ]
    for copy in copies:
        copy.start()
    rows, cols = forcing_buf.shape
    first_row = lax.axis_index("lat") * rows
    row = (iota((rows, LANES), 0) + first_row).astype(jnp.float32)
    center = jnp.cos(jnp.deg2rad(BAND_SOUTH + ROW_STEP * (row + 0.5)))
    center = jnp.concatenate([center] * (cols // LANES), axis=1)
    for copy in copies:
        copy.wait()
    sea_mask = sea_buf[...].astype(jnp.float32)
    layers = levels_buf[...].astype(jnp.float32)
    depth = sea_mask * ((layers + layers * (layers - 1.0) / 20.0) / 200.0)
    fields = (depth, surface_buf[...] * center * sea_mask, forcing_buf[...] * sea_mask)
    slot = iota((rows, LANES), 1) // HALO
    slots = LANES // HALO
    west_edge = jnp.zeros((rows, LANES), jnp.float32)
    east_edge = jnp.zeros((rows, LANES), jnp.float32)
    for f, value in enumerate(fields):
        own_ref[f] = value
        west_edge = jnp.where(slot == f, lane_shift(value[:, :LANES], -f * HALO), west_edge)
        east_edge = jnp.where(
            slot == (f + slots - 1) % slots, lane_shift(value[:, cols - LANES :], -f * HALO), east_edge
        )
    east_edge_ref[...] = east_edge
    west_edge_ref[...] = west_edge


def prepare_corner(east_edge_ref, rows_ref, diagonal_edge_ref):
    rows = east_edge_ref.shape[0]
    odd = jnp.broadcast_to(lax.rem(lax.axis_index("lat"), 2), diagonal_edge_ref.shape) > 0
    diagonal_edge_ref[...] = jnp.where(odd, east_edge_ref[pl.ds(rows - HALO, HALO), :], east_edge_ref[pl.ds(0, HALO), :])


def prepare_rows(own_ref, west_edge_ref, lat_near_ref, lat_far_ref):
    rows, cols = own_ref.shape[1:]
    south, north = pl.ds(0, HALO), pl.ds(rows - HALO, HALO)
    odd = jnp.broadcast_to(lax.rem(lax.axis_index("lat"), 2), (HALO, cols)) > 0
    for f in range(FIELDS):
        south_edge, north_edge = own_ref[f, south, :], own_ref[f, north, :]
        part = slice(f * cols, (f + 1) * cols)
        lat_near_ref[:, part] = jnp.where(odd, south_edge, north_edge)
        lat_far_ref[:, part] = jnp.where(odd, north_edge, south_edge)
    odd = odd[:, :LANES]
    south_edge, north_edge = west_edge_ref[south, :], west_edge_ref[north, :]
    part = slice(FIELDS * cols, FIELDS * cols + LANES)
    lat_near_ref[:, part] = jnp.where(odd, south_edge, north_edge)
    lat_far_ref[:, part] = jnp.where(odd, north_edge, south_edge)


def fine_faces(depth, across, along):
    count = len(depth)
    east_face = [jnp.minimum(depth[t], lane_shift(depth[t], 1)) * across[t] for t in range(count)]
    north_face = [jnp.minimum(depth[t], north_of(depth, t)) * along[t] for t in range(count)]
    return east_face, north_face


def level_down(level, east_face, north_face, source_term, source):
    stride = 1 << level
    count = len(source)
    west_face = [lane_shift(value, -stride) for value in east_face]
    faces = (east_face, west_face, north_face)
    inverse, diagonal = [], []
    for t in range(count):
        total = source_term[t] + ((east_face[t] + west_face[t]) + (north_face[t] + south_of(north_face, t)))
        diagonal.append(jnp.where(source_term[t] > 0.0, total, 1.0))
        inverse.append(DAMPING / diagonal[t])
    field = [inverse[t] * source[t] for t in range(count)]
    for _ in range(SWEEPS - 1):
        field = sweep(field, source, inverse, faces, stride)
    image = remainder(field, source, diagonal, faces, stride)
    kept = (faces, inverse, source, field, diagonal)

    return kept, image


def level_next(level, faces, source_term, image):
    stride = 1 << level
    east_face, _, north_face = faces
    firsts = range(0, len(image), 2)

    def coarse(tiles):
        sums = [tiles[t] + tiles[t + 1] for t in firsts]
        return [value + lane_shift(value, stride) for value in sums]

    east_next = [lane_shift(east_face[t] + east_face[t + 1], stride) for t in firsts]
    north_next = [north_face[t + 1] + lane_shift(north_face[t + 1], stride) for t in firsts]
    return east_next, north_next, coarse(source_term), coarse(image)


def lay_out(lat_count, own_ref, lat_near_ref, lat_far_ref, west_ref, west_far_ref, east_ref, scale_ref, grid_ref):
    rows, cols = own_ref.shape[1], own_ref.shape[2]
    columns, height = grid_ref.shape[1], grid_ref.shape[2]
    count = height // TILE
    own_columns = cols // LANES
    halo = (height - rows) // 2
    lat_index = lax.axis_index("lat")
    lat_odd = lax.rem(lat_index, 2)
    near_row = rows + pl.multiple_of(lat_odd * halo, TILE)
    far_row = rows + pl.multiple_of((1 - lat_odd) * halo, TILE)
    near_part = pl.ds(pl.multiple_of(lat_odd * (HALO - halo), TILE), halo)
    far_part = pl.ds(pl.multiple_of((1 - lat_odd) * (HALO - halo), TILE), halo)
    edge = FIELDS * cols + LANES
    last = LANES // HALO - 1
    at_end = (lat_index == 0) | (lat_index == lat_count - 1)

    def inside(value, far):
        return jnp.where(jnp.broadcast_to(at_end, value.shape), 0.0, value) if far else value

    parts = (
        (0, rows, None, west_ref[...], None if east_ref is None else east_ref[pl.ds(0, rows), :], False),
        (near_row, halo, lat_near_ref.at[near_part], lat_near_ref[near_part, edge : edge + LANES],
         None if east_ref is None else east_ref[pl.ds(rows, HALO), :], False),
        (far_row, halo, lat_far_ref.at[far_part], west_far_ref[far_part, :],
         None if east_ref is None else east_ref[pl.ds(rows + HALO, HALO), :], True),
    )
    for first, size, body_ref, west, east, far in parts:
        slot = iota((size, LANES), 1) // HALO
        for f in range(FIELDS):
            for c in range(own_columns):
                if body_ref is None:
                    value = own_ref[f, :, c * LANES : (c + 1) * LANES]
                else:
                    value = body_ref[:, f * cols + c * LANES : f * cols + (c + 1) * LANES]
                grid_ref[f, c, pl.ds(first, size), :] = inside(value, far)
            side = jnp.where(slot == (f + last) % (last + 1), west, 0.0)
            if east is not None:
                side = jnp.where(slot == f, east, side)
            grid_ref[f, own_columns, pl.ds(first, size), :] = inside(lane_shift(side, f * HALO), far)

    def load(f):
        return [
            jnp.concatenate(
                [grid_ref[f, c, pl.ds(t, TILE, stride=count), :] for c in range(columns)], axis=1
            )
            for t in range(count)
        ]

    depth, source_term, source = load(0), load(1), load(2)
    across = [jnp.concatenate([scale_ref[0, t]] * columns, axis=1) for t in range(count)]
    along = [jnp.concatenate([scale_ref[1, t]] * columns, axis=1) for t in range(count)]
    return fine_faces(depth, across, along) + (source_term, source)


def hold(lat_count, own_ref, lat_near_ref, lat_far_ref, west_ref, west_far_ref, east_ref, scale_ref, *rest):
    level_refs = [rest[KEPT * i : KEPT * i + KEPT] for i in range(LEVELS)]
    diagonal_ref, grid_ref = rest[KEPT * LEVELS :]
    state = lay_out(lat_count, own_ref, lat_near_ref, lat_far_ref, west_ref, west_far_ref, east_ref, scale_ref,
                    grid_ref)
    for level in range(LEVELS):
        (faces, inverse, source, field, diagonal), image = level_down(level, *state)
        swept = sweep(field, source, inverse, faces, 1 << level)
        for ref, tiles in zip(level_refs[level], faces + (inverse, source, swept)):
            keep(ref, tiles)
        if level == 0:
            keep(diagonal_ref, diagonal)
        if level < LEVELS - 1:
            state = level_next(level, faces, state[2], image)


def descend(lat_count, own_ref, lat_near_ref, lat_far_ref, west_ref, west_far_ref, west_edge_ref, scale_ref,
            pack_ref, edge_ref, grid_ref, plain_ref):
    rows = own_ref.shape[1]
    edge = slice(FIELDS * own_ref.shape[2], FIELDS * own_ref.shape[2] + LANES)
    edge_ref[pl.ds(0, rows), :] = west_edge_ref[...]
    edge_ref[pl.ds(rows, HALO), :] = lat_near_ref[:, edge]
    edge_ref[pl.ds(rows + HALO, HALO), :] = lat_far_ref[:, edge]
    lon_index = lax.axis_index("lon")
    cols = own_ref.shape[2]
    own_columns = cols // LANES
    columns = grid_ref.shape[1]
    state = lay_out(lat_count, own_ref, lat_near_ref, lat_far_ref, west_ref, west_far_ref, None, scale_ref,
                    grid_ref)
    for level in range(LEVELS):
        kept, image = level_down(level, *state)
        if level < LEVELS - 1:
            state = level_next(level, kept[0], state[2], image)

    east_face, north_face, source_term, _ = state
    for f, values in enumerate((image, east_face, north_face, source_term)):
        for t, value in enumerate(values):
            for c in range(columns):
                plain_ref[f, c, pl.ds(t, TILE, stride=len(values)), :] = value[:, c * LANES : (c + 1) * LANES]
    stride = 1 << LEVELS
    bottom_rows = rows // stride
    bottom_width = cols // stride
    group = LANES // bottom_width
    per_column = LANES // stride
    lane = iota((bottom_rows, LANES), 1)
    cell = lane % bottom_width - SHIFT
    column = jnp.where(cell < 0, own_columns, cell // per_column)
    west_part = jnp.where(cell < 0, LANES + cell * stride, (cell % per_column) * stride)
    east_part = west_part + stride // 2
    turn = lax.rem(lane // bottom_width + group - lax.rem(lon_index, group), group)
    packed = jnp.zeros((bottom_rows, LANES), jnp.float32)
    for f, picks in enumerate(((west_part, east_part), (east_part,), (west_part, east_part), (west_part, east_part))):
        flat = jnp.zeros((bottom_rows, LANES), jnp.float32)
        for c in range(columns):
            value = plain_ref[f, c, pl.ds(1, bottom_rows, stride=2), :]
            if f != 2:
                value = value + plain_ref[f, c, pl.ds(0, bottom_rows, stride=2), :]
            taken = sum(jnp.take_along_axis(value, pick, axis=1) for pick in picks)
            flat = jnp.where(column == c, taken, flat)
        packed = jnp.where(turn == f, flat, packed)
    for k in range(pack_ref.shape[0]):
        pack_ref[k] = packed


def total_of(tiles):
    parts = list(tiles)
    while len(parts) > 1:
        parts = [
            parts[i] + parts[i + 1] if i + 1 < len(parts) else parts[i] for i in range(0, len(parts), 2)
        ]
    value = parts[0]
    value = sum(value[:, c : c + LANES] for c in range(0, value.shape[1], LANES))
    return jnp.sum(jnp.sum(value, axis=0, keepdims=True), axis=1, keepdims=True)


def conjugate(source, east_face, north_face, source_term):
    height = source.shape[0]

    def split(value):
        return [value[r : r + TILE] for r in range(0, height, TILE)]

    def up(value):
        return pltpu.roll(value, height - 1, 0)

    def down(value):
        return pltpu.roll(value, 1, 0)

    west_face = lane_shift(east_face, -1)
    south_face = down(north_face)
    diagonal = source_term + ((east_face + west_face) + (north_face + south_face))

    def apply(value):
        return diagonal * value - (
            (east_face * lane_shift(value, 1) + west_face * lane_shift(value, -1))
            + (north_face * up(value) + south_face * down(value))
        )

    iterate = jnp.zeros_like(source)
    remain = source
    image_r = apply(source)
    direction = image_d = second = step_size = norm = None
    for step in range(BOTTOM_ITERS):
        norm_now = total_of(split(remain * remain))
        energy = total_of(split(remain * image_r))
        last = step == BOTTOM_ITERS - 1
        ahead = None if last else apply(image_r)
        if step == 0:
            step_size = norm_now / energy
            direction, image_d, second = remain, image_r, ahead
        else:
            ratio = norm_now / norm
            step_size = norm_now / (energy - ratio * (norm_now / step_size))
            direction = remain + ratio * direction
            if not last:
                image_d = image_r + ratio * image_d
                second = ahead + ratio * second
        norm = norm_now
        iterate = iterate + step_size * direction
        if not last:
            remain = remain - step_size * image_d
            image_r = image_r - step_size * second
    return iterate


def ascend(lat_count, lon_count, blocks_ref, *rest):
    level_refs = [rest[KEPT * i : KEPT * i + KEPT] for i in range(LEVELS)]
    diagonal_ref, solution_ref, residual_ref, window_ref, order_ref, sems = rest[KEPT * LEVELS :]
    lon_index = lax.axis_index("lon")
    lat_index = lax.axis_index("lat")
    rows, cols = solution_ref.shape
    count, width = diagonal_ref.shape[0], diagonal_ref.shape[2]
    own_columns = cols // LANES
    columns = width // LANES
    stride = 1 << LEVELS
    bottom_rows = rows // stride
    bottom_width = cols // stride
    group = LANES // bottom_width
    slot = iota((bottom_rows, LANES), 1) // bottom_width
    fields = []
    for f in range(4):
        strips = []
        for a in range(lat_count):
            pieces = []
            for c in range(lon_count // group):
                merged = None
                for j in range(group):
                    block = blocks_ref[(c * group + j) * lat_count + a]
                    merged = block if merged is None else jnp.where(slot == (f + j) % group, block, merged)
                pieces.append(lane_shift(merged, f * bottom_width))
            strips.append(jnp.concatenate(pieces, axis=1))
        fields.append(jnp.concatenate(strips, axis=0))
    iterate = conjugate(*fields)

    bottom_height = lat_count * bottom_rows
    whole_width = lon_count * bottom_width
    pad = 2 * TILE
    window_ref[pl.ds(0, pad), :] = jnp.zeros((pad, LANES), jnp.float32)
    window_ref[pl.ds(pad + bottom_height, pad), :] = jnp.zeros((pad, LANES), jnp.float32)
    half = LANES // 2
    margin = half // stride
    shift = lax.rem(margin - SHIFT - lon_index * bottom_width + whole_width, whole_width)
    window_ref[pl.ds(pad, bottom_height), :] = pltpu.roll(iterate, shift, 1)[:, :LANES]
    start = pl.multiple_of(lat_index * bottom_rows, TILE)
    tiles = count >> LEVELS
    lane = iota((TILE, LANES), 1)
    ahead = (rows + HALO) // stride // tiles
    sublane = iota((TILE, LANES), 0)
    step = 1 << (LEVELS - 1)
    center, plus, minus = [], [], []
    for t in range(tiles):
        upper = window_ref[pl.ds(start + pad + t, TILE, stride=tiles), :]
        lower = window_ref[pl.ds(start + pad + t - tiles * TILE, TILE, stride=tiles), :]
        value = jnp.where(sublane < ahead, upper, lower)
        for target, move in ((center, 0), (plus, step), (minus, -step)):
            parts = []
            for c in range(columns):
                place = c * LANES + lane + (move + width)
                place = jnp.where(place >= width, place - width, place)
                place = jnp.where(place >= width, place - width, place)
                pick = jnp.where(place < cols + half, margin + place // stride, (place - (cols + half)) // stride)
                parts.append(jnp.take_along_axis(value, pick, axis=1))
            target.append(jnp.concatenate(parts, axis=1))

    lane = iota((TILE, width), 1)
    for level in range(LEVELS - 1, -1, -1):
        stride = 1 << level
        east_face, west_face, north_face, inverse, source, swept = map(tiles_of, level_refs[level])
        faces = (east_face, west_face, north_face)
        if level < LEVELS - 1:
            first = lax.rem(lane // stride, 2) == 0
            east = [lane_shift(value, stride) for value in field]
            west = [lane_shift(value, -stride) for value in field]
            west_two = [lane_shift(value, -2 * stride) for value in field]
            coarse = range(len(field))
            center = [jnp.where(first, field[t], west[t]) for t in coarse]
            plus = [jnp.where(first, field[t], east[t]) for t in coarse]
            minus = [jnp.where(first, west_two[t], west[t]) for t in coarse]
        spread = [center[t // 2] for t in range(count >> level)]
        field = []
        for t in range(count >> level):
            around = (east_face[t] * plus[t // 2] + west_face[t] * minus[t // 2]) + (
                north_face[t] * north_of(spread, t) + south_of(north_face, t) * south_of(spread, t)
            )
            here = spread[t]
            if level == 0:
                here = jnp.where(east_face[t] + north_face[t] > 0.0, here, 0.0)
            field.append(swept[t] + ((1.0 - DAMPING) * here + inverse[t] * around))
        for _ in range(SWEEPS - 1):
            field = sweep(field, source, inverse, faces, stride)
    correction = field
    own_sublanes = rows // count

    def send_out(k, ref, tiles):
        copies = []
        for c in range(own_columns):
            part = slice(c * LANES, (c + 1) * LANES)
            for t in range(count):
                order_ref[k, c, pl.ds(t, own_sublanes, stride=count), :] = tiles[t][:own_sublanes, part]
            copies.append(pltpu.make_async_copy(order_ref.at[k, c], ref.at[:, part], sems.at[k, c]))
            copies[-1].start()
        return copies

    copies = send_out(0, solution_ref, correction)
    final = remainder(correction, source, tiles_of(diagonal_ref), faces, 1)
    copies += send_out(1, residual_ref, final)
    for copy in copies:
        copy.wait()


def near_pairs(lat_count):
    return [(a, a ^ 1) for a in range(lat_count)]


def far_pairs(lon_count, lat_count, east):
    pairs = []
    for i in range(lon_count):
        for a in range(lat_count):
            b = a + 1 if a % 2 else a - 1
            j = (i + east) % lon_count
            if b < 0 or b == lat_count:
                b, j = a, i ^ 1
            pairs.append((i * lat_count + a, j * lat_count + b))
    return pairs


def on_device(lat_count, lon_count, forcing, surface_term, sea_cells, levels):
    rows, cols = forcing.shape
    height, width = rows + 2 * HALO, cols + LANES
    count = height // TILE
    f32 = jnp.float32
    vmem = pl.BlockSpec(memory_space=pltpu.VMEM)
    hbm = pl.BlockSpec(memory_space=pltpu.HBM)
    params = pltpu.CompilerParams(vmem_limit_bytes=VMEM_LIMIT)
    lat_index = lax.axis_index("lat").astype(jnp.int32)
    inputs = [
        pltpu.with_memory_space_constraint(x, pltpu.HBM) for x in (forcing, surface_term, sea_cells, levels)
    ]
    own, east_edge, west_edge = pl.pallas_call(
        prepare,
        out_shape=[
            jax.ShapeDtypeStruct((FIELDS, rows, cols), f32),
            jax.ShapeDtypeStruct((rows, LANES), f32),
            jax.ShapeDtypeStruct((rows, LANES), f32),
        ],
        in_specs=[hbm] * 4,
        out_specs=[vmem] * 3,
        scratch_shapes=[
            pltpu.VMEM((rows, cols), f32),
            pltpu.VMEM((rows, cols), f32),
            pltpu.VMEM((rows, cols), jnp.int32),
            pltpu.VMEM((rows, cols), jnp.int32),
            pltpu.SemaphoreType.DMA((4,)),
        ],
        compiler_params=params,
        name="prepare",
    )(*inputs)

    lat_near, lat_far = pl.pallas_call(
        prepare_rows,
        out_shape=[jax.ShapeDtypeStruct((HALO, FIELDS * cols + LANES), f32)] * 2,
        in_specs=[vmem] * 2,
        out_specs=[vmem] * 2,
        compiler_params=params,
        name="prepare_rows",
    )(own, west_edge)

    diagonal_edge = pl.pallas_call(
        prepare_corner,
        out_shape=jax.ShapeDtypeStruct((HALO, LANES), f32),
        in_specs=[vmem] * 2,
        out_specs=vmem,
        compiler_params=params,
        name="prepare_corner",
    )(east_edge, lat_far)
    eastward = [(i, (i + 1) % lon_count) for i in range(lon_count)]
    westward = [(target, source) for source, target in eastward]
    west_halo = lax.ppermute(east_edge, "lon", eastward)
    lat_far = lax.ppermute(lat_far, ("lon", "lat"), far_pairs(lon_count, lat_count, 0))
    west_far = lax.ppermute(diagonal_edge, ("lon", "lat"), far_pairs(lon_count, lat_count, 1))
    odd = lat_index % 2 == 1
    lat_near = lax.ppermute(
        jnp.concatenate([lat_near, jnp.where(odd, west_halo[:HALO], west_halo[rows - HALO :])], axis=1),
        "lat",
        near_pairs(lat_count),
    )

    def scales(halo):
        tall = rows + 2 * halo
        tiles = tall // TILE
        row = jnp.arange(TILE)[None, :] * tiles + jnp.arange(tiles)[:, None]
        row = jnp.where(row < rows + halo, row, row - tall).astype(f32) + (lat_index * rows).astype(f32)
        center, northern = metric(row)
        return jnp.broadcast_to(jnp.stack([1.0 / center, northern])[..., None], (2, tiles, TILE, LANES))

    devices = lat_count * lon_count
    grid = pltpu.VMEM((FIELDS, width // LANES, height, LANES), f32)
    packed, edges = pl.pallas_call(
        functools.partial(descend, lat_count),
        out_shape=[
            jax.ShapeDtypeStruct((devices, rows >> LEVELS, LANES), f32),
            jax.ShapeDtypeStruct((height, LANES), f32),
        ],
        in_specs=[vmem] * 7,
        out_specs=[vmem] * 2,
        scratch_shapes=[
            pltpu.VMEM((FIELDS, width // LANES, rows + 2 * REACH, LANES), f32),
            pltpu.VMEM((4, width // LANES, (rows + 2 * REACH) >> (LEVELS - 1), LANES), f32),
        ],
        compiler_params=params,
        name="descend",
    )(own, lat_near, lat_far, west_halo, west_far, west_edge, scales(REACH))
    east_halo = lax.ppermute(edges, "lon", westward)
    blocks = lax.all_to_all(packed, ("lon", "lat"), 0, 0, tiled=True)

    level_shapes = []
    for level in range(LEVELS):
        level_shapes += [jax.ShapeDtypeStruct((count >> level, TILE, width), f32)] * KEPT
    held = pl.pallas_call(
        functools.partial(hold, lat_count),
        out_shape=level_shapes + [jax.ShapeDtypeStruct((count, TILE, width), f32)],
        in_specs=[vmem] * 7,
        out_specs=[vmem] * (1 + len(level_shapes)),
        scratch_shapes=[grid],
        compiler_params=params,
        cost_estimate=pl.CostEstimate(flops=0, bytes_accessed=60 * 1024 * 1024, transcendentals=0),
        name="hold",
    )(own, lat_near, lat_far, west_halo, west_far, east_halo, scales(HALO))

    return pl.pallas_call(
        functools.partial(ascend, lat_count, lon_count),
        out_shape=[jax.ShapeDtypeStruct((rows, cols), f32)] * 2,
        in_specs=[vmem] * (1 + len(held)),
        out_specs=[hbm] * 2,
        scratch_shapes=[
            pltpu.VMEM((lat_count * (rows >> LEVELS) + 4 * TILE, LANES), f32),
            pltpu.VMEM((2, cols // LANES, rows, LANES), f32),
            pltpu.SemaphoreType.DMA((2, cols // LANES)),
        ],
        compiler_params=params,
        name="ascend",
    )(blocks, *held)


def solution(mesh):
    body = functools.partial(on_device, mesh.shape["lat"], mesh.shape["lon"])
    return jax.shard_map(
        body,
        mesh=mesh,
        in_specs=(P("lat", "lon"),) * 4,
        out_specs=(P("lat", "lon"),) * 2,
        check_vma=False,
    )
```

```python
import functools

import jax
import jax.numpy as jnp
from jax import lax
from jax.experimental import pallas as pl
from jax.experimental.pallas import tpu as pltpu
from jax.sharding import PartitionSpec as P

LEVELS = 3
SWEEPS = 2
BOTTOM_ITERS = 6

DAMPING = 0.8
ROW_STEP = 150.0 / 8640.0
BAND_SOUTH = -50.0

HALO = 32
REACH = 16
LANES = 128
TILE = 8
FIELDS = 3
KEPT = 6
SHIFT = 2
VMEM_LIMIT = 8 * 1024 * 1024


def iota(shape, dim):
    return lax.broadcasted_iota(jnp.int32, shape, dim)


def lane_shift(field, count):
    return pltpu.roll(field, (-count) % field.shape[1], 1)


def north_of(tiles, t):
    if t + 1 < len(tiles):
        return tiles[t + 1]
    return pltpu.roll(tiles[0], TILE - 1, 0)


def south_of(tiles, t):
    if t > 0:
        return tiles[t - 1]
    return pltpu.roll(tiles[-1], 1, 0)


def neighbour_sum(field, faces, stride):
    east_face, west_face, north_face = faces
    upward = [north_face[t] * field[t] for t in range(len(field))]
    return [
        (east_face[t] * lane_shift(field[t], stride) + west_face[t] * lane_shift(field[t], -stride))
        + (north_face[t] * north_of(field, t) + south_of(upward, t))
        for t in range(len(field))
    ]


def sweep(field, source, inverse, faces, stride):
    around = neighbour_sum(field, faces, stride)
    return [
        (1.0 - DAMPING) * field[t] + inverse[t] * (source[t] + around[t]) for t in range(len(field))
    ]


def remainder(field, source, diagonal, faces, stride):
    around = neighbour_sum(field, faces, stride)
    return [source[t] - diagonal[t] * field[t] + around[t] for t in range(len(field))]


def tiles_of(ref):
    return [ref[t] for t in range(ref.shape[0])]


def keep(ref, tiles):
    for t, value in enumerate(tiles):
        ref[t] = value


def metric(row):
    center = jnp.cos(jnp.deg2rad(BAND_SOUTH + ROW_STEP * (row + 0.5)))
    northern = jnp.cos(jnp.deg2rad(BAND_SOUTH + ROW_STEP * (row + 1.0)))
    return center, northern


def prepare(forcing_ref, surface_ref, sea_ref, levels_ref,
            own_ref, east_edge_ref, west_edge_ref,
            forcing_buf, surface_buf, sea_buf, levels_buf, sems):
    copies = [
        pltpu.make_async_copy(source, target, sems.at[i])
        for i, (source, target) in enumerate((
            (levels_ref, levels_buf), (sea_ref, sea_buf), (surface_ref, surface_buf), (forcing_ref, forcing_buf),
        ))
    ]
    for copy in copies:
        copy.start()
    rows, cols = forcing_buf.shape
    first_row = lax.axis_index("lat") * rows
    row = (iota((rows, LANES), 0) + first_row).astype(jnp.float32)
    center = jnp.cos(jnp.deg2rad(BAND_SOUTH + ROW_STEP * (row + 0.5)))
    center = jnp.concatenate([center] * (cols // LANES), axis=1)
    for copy in copies:
        copy.wait()
    sea_mask = sea_buf[...].astype(jnp.float32)
    layers = levels_buf[...].astype(jnp.float32)
    depth = sea_mask * (layers * (0.00475 + 0.00025 * layers))
    fields = (depth, surface_buf[...] * center * sea_mask, forcing_buf[...] * sea_mask)
    slot = iota((rows, LANES), 1) // HALO
    slots = LANES // HALO
    west_edge = jnp.zeros((rows, LANES), jnp.float32)
    east_edge = jnp.zeros((rows, LANES), jnp.float32)
    for f, value in enumerate(fields):
        own_ref[f] = value
        west_edge = jnp.where(slot == f, lane_shift(value[:, :LANES], -f * HALO), west_edge)
        east_edge = jnp.where(
            slot == (f + slots - 1) % slots, lane_shift(value[:, cols - LANES :], -f * HALO), east_edge
        )
    east_edge_ref[...] = east_edge
    west_edge_ref[...] = west_edge


def prepare_corner(east_edge_ref, rows_ref, diagonal_edge_ref):
    rows = east_edge_ref.shape[0]
    odd = jnp.broadcast_to(lax.rem(lax.axis_index("lat"), 2), diagonal_edge_ref.shape) > 0
    diagonal_edge_ref[...] = jnp.where(odd, east_edge_ref[pl.ds(rows - HALO, HALO), :], east_edge_ref[pl.ds(0, HALO), :])


def prepare_rows(own_ref, west_edge_ref, lat_near_ref, lat_far_ref):
    rows, cols = own_ref.shape[1:]
    south, north = pl.ds(0, HALO), pl.ds(rows - HALO, HALO)
    odd = jnp.broadcast_to(lax.rem(lax.axis_index("lat"), 2), (HALO, cols)) > 0
    for f in range(FIELDS):
        south_edge, north_edge = own_ref[f, south, :], own_ref[f, north, :]
        part = slice(f * cols, (f + 1) * cols)
        lat_near_ref[:, part] = jnp.where(odd, south_edge, north_edge)
        lat_far_ref[:, part] = jnp.where(odd, north_edge, south_edge)
    odd = odd[:, :LANES]
    south_edge, north_edge = west_edge_ref[south, :], west_edge_ref[north, :]
    part = slice(FIELDS * cols, FIELDS * cols + LANES)
    lat_near_ref[:, part] = jnp.where(odd, south_edge, north_edge)
    lat_far_ref[:, part] = jnp.where(odd, north_edge, south_edge)


def fine_faces(depth, across, along):
    count = len(depth)
    east_face = [jnp.minimum(depth[t], lane_shift(depth[t], 1)) * across[t] for t in range(count)]
    north_face = [jnp.minimum(depth[t], north_of(depth, t)) * along[t] for t in range(count)]
    return east_face, north_face


def level_down(level, east_face, north_face, source_term, source):
    stride = 1 << level
    count = len(source)
    west_face = [lane_shift(value, -stride) for value in east_face]
    faces = (east_face, west_face, north_face)
    inverse, diagonal = [], []
    for t in range(count):
        total = source_term[t] + ((east_face[t] + west_face[t]) + (north_face[t] + south_of(north_face, t)))
        diagonal.append(jnp.where(source_term[t] > 0.0, total, 1.0))
        inverse.append(DAMPING / diagonal[t])
    field = [inverse[t] * source[t] for t in range(count)]
    for _ in range(SWEEPS - 1):
        field = sweep(field, source, inverse, faces, stride)
    image = remainder(field, source, diagonal, faces, stride)
    kept = (faces, inverse, source, field, diagonal)

    return kept, image


def level_next(level, faces, source_term, image):
    stride = 1 << level
    east_face, _, north_face = faces
    firsts = range(0, len(image), 2)

    def coarse(tiles):
        sums = [tiles[t] + tiles[t + 1] for t in firsts]
        return [value + lane_shift(value, stride) for value in sums]

    east_next = [lane_shift(east_face[t] + east_face[t + 1], stride) for t in firsts]
    north_next = [north_face[t + 1] + lane_shift(north_face[t + 1], stride) for t in firsts]
    return east_next, north_next, coarse(source_term), coarse(image)


def lay_out(lat_count, own_ref, lat_near_ref, lat_far_ref, west_ref, west_near_ref, west_far_ref, scale_ref, grid_ref):
    rows, cols = own_ref.shape[1], own_ref.shape[2]
    columns, height = grid_ref.shape[1], grid_ref.shape[2]
    count = height // TILE
    own_columns = cols // LANES
    halo = (height - rows) // 2
    lat_index = lax.axis_index("lat")
    lat_odd = lax.rem(lat_index, 2)
    near_row = rows + pl.multiple_of(lat_odd * halo, TILE)
    far_row = rows + pl.multiple_of((1 - lat_odd) * halo, TILE)
    near_part = pl.ds(pl.multiple_of(lat_odd * (HALO - halo), TILE), halo)
    far_part = pl.ds(pl.multiple_of((1 - lat_odd) * (HALO - halo), TILE), halo)
    last = LANES // HALO - 1
    at_end = (lat_index == 0) | (lat_index == lat_count - 1)

    def inside(value, far):
        return jnp.where(jnp.broadcast_to(at_end, value.shape), 0.0, value) if far else value

    parts = (
        (0, rows, None, west_ref[...], False),
        (near_row, halo, lat_near_ref.at[near_part], west_near_ref[near_part, :], False),
        (far_row, halo, lat_far_ref.at[far_part], west_far_ref[far_part, :], True),
    )
    for first, size, body_ref, west, far in parts:
        slot = iota((size, LANES), 1) // HALO
        for f in range(FIELDS):
            for c in range(own_columns):
                if body_ref is None:
                    value = own_ref[f, :, c * LANES : (c + 1) * LANES]
                else:
                    value = body_ref[:, f * cols + c * LANES : f * cols + (c + 1) * LANES]
                grid_ref[f, c, pl.ds(first, size), :] = inside(value, far)
            side = jnp.where(slot == (f + last) % (last + 1), west, 0.0)
            grid_ref[f, own_columns, pl.ds(first, size), :] = inside(lane_shift(side, f * HALO), far)

    def load(f):
        return [
            jnp.concatenate(
                [grid_ref[f, c, pl.ds(t, TILE, stride=count), :] for c in range(columns)], axis=1
            )
            for t in range(count)
        ]

    depth, source_term, source = load(0), load(1), load(2)
    across = [jnp.concatenate([scale_ref[0, t]] * columns, axis=1) for t in range(count)]
    along = [jnp.concatenate([scale_ref[1, t]] * columns, axis=1) for t in range(count)]
    return depth, source_term, source, across, along


def way_down(depth, source_term, source, across, along, put):
    state = fine_faces(depth, across, along) + (source_term, source)
    for level in range(LEVELS):
        (faces, inverse, source, field, diagonal), image = level_down(level, *state)
        swept = sweep(field, source, inverse, faces, 1 << level)
        put(level, faces + (inverse, source, swept) + ((diagonal,) if level == 0 else ()))
        if level < LEVELS - 1:
            state = level_next(level, faces, state[2], image)


def split_refs(rest):
    level_refs = [list(rest[KEPT * i : KEPT * i + KEPT]) for i in range(LEVELS)]
    level_refs[0].append(rest[KEPT * LEVELS])
    return level_refs, rest[KEPT * LEVELS + 1 :]


def hold(lat_count, own_ref, lat_near_ref, lat_far_ref, west_ref, west_near_ref, west_far_ref, scale_ref, *rest):
    level_refs, (raw_ref, grid_ref) = split_refs(rest)
    values = lay_out(lat_count, own_ref, lat_near_ref, lat_far_ref, west_ref, west_near_ref, west_far_ref, scale_ref, grid_ref)
    cols = own_ref.shape[2]
    for f in range(FIELDS):
        for t, value in enumerate(values[f]):
            raw_ref[f, t] = value[:, cols - LANES : cols]

    def put(level, kept):
        for ref, tiles in zip(level_refs[level], kept):
            keep(ref, tiles)

    way_down(*values, put)


def patch(lat_count, raw_ref, east_ref, scale_ref, *rest):
    half = len(rest) // 2
    level_refs, (strip_ref,) = split_refs(rest[half:])
    count = raw_ref.shape[1]
    height = count * TILE
    rows = height - 2 * HALO
    lat_index = lax.axis_index("lat")
    lat_odd = lax.rem(lat_index, 2)
    near_row = rows + pl.multiple_of(lat_odd * HALO, HALO)
    far_row = rows + pl.multiple_of((1 - lat_odd) * HALO, HALO)
    at_end = (lat_index == 0) | (lat_index == lat_count - 1)
    for first, at, size, far in ((0, 0, rows, False), (near_row, rows, HALO, False), (far_row, rows + HALO, HALO, True)):
        side = east_ref[pl.ds(at, size), :]
        if far:
            side = jnp.where(jnp.broadcast_to(at_end, side.shape), 0.0, side)
        for f in range(FIELDS):
            strip_ref[f, pl.ds(first, size), :] = lane_shift(side, f * HALO)
    lane = iota((TILE, LANES), 1)
    own = lane >= LANES // 2
    fields = [
        [
            jnp.where(own, raw_ref[f, t],
                      jnp.where(lane < HALO, strip_ref[f, pl.ds(t, TILE, stride=count), :], 0.0))
            for t in range(count)
        ]
        for f in range(FIELDS)
    ]

    def put(level, kept):
        for ref, tiles in zip(level_refs[level], kept):
            last = ref.shape[2] - LANES
            for t, value in enumerate(tiles):
                ref[t, :, last - LANES : last] = jnp.where(lane >= LANES - HALO, value, ref[t, :, last - LANES : last])
                ref[t, :, last:] = jnp.where(own, ref[t, :, last:], value)

    way_down(*fields, [scale_ref[0, t] for t in range(count)], [scale_ref[1, t] for t in range(count)], put)


def descend(lat_count, own_ref, lat_near_ref, lat_far_ref, west_ref, west_near_ref, west_far_ref, west_edge_ref, scale_ref,
            pack_ref, edge_ref, grid_ref, plain_ref):
    rows = own_ref.shape[1]
    edge = slice(FIELDS * own_ref.shape[2], FIELDS * own_ref.shape[2] + LANES)
    edge_ref[pl.ds(0, rows), :] = west_edge_ref[...]
    edge_ref[pl.ds(rows, HALO), :] = lat_near_ref[:, edge]
    edge_ref[pl.ds(rows + HALO, HALO), :] = lat_far_ref[:, edge]
    lon_index = lax.axis_index("lon")
    cols = own_ref.shape[2]
    own_columns = cols // LANES
    columns = grid_ref.shape[1]
    depth, source_term, source, across, along = lay_out(
        lat_count, own_ref, lat_near_ref, lat_far_ref, west_ref, west_near_ref, west_far_ref, scale_ref, grid_ref
    )
    state = fine_faces(depth, across, along) + (source_term, source)
    for level in range(LEVELS):
        kept, image = level_down(level, *state)
        if level < LEVELS - 1:
            state = level_next(level, kept[0], state[2], image)

    east_face, north_face, source_term, _ = state
    for f, values in enumerate((image, east_face, north_face, source_term)):
        for t, value in enumerate(values):
            for c in range(columns):
                plain_ref[f, c, pl.ds(t, TILE, stride=len(values)), :] = value[:, c * LANES : (c + 1) * LANES]
    stride = 1 << LEVELS
    bottom_rows = rows // stride
    bottom_width = cols // stride
    group = LANES // bottom_width
    per_column = LANES // stride
    lane = iota((bottom_rows, LANES), 1)
    cell = lane % bottom_width - SHIFT
    column = jnp.where(cell < 0, own_columns, cell // per_column)
    west_part = jnp.where(cell < 0, LANES + cell * stride, (cell % per_column) * stride)
    east_part = west_part + stride // 2
    turn = lax.rem(lane // bottom_width + group - lax.rem(lon_index, group), group)
    packed = jnp.zeros((bottom_rows, LANES), jnp.float32)
    for f, picks in enumerate(((west_part, east_part), (east_part,), (west_part, east_part), (west_part, east_part))):
        flat = jnp.zeros((bottom_rows, LANES), jnp.float32)
        for c in range(columns):
            value = plain_ref[f, c, pl.ds(1, bottom_rows, stride=2), :]
            if f != 2:
                value = value + plain_ref[f, c, pl.ds(0, bottom_rows, stride=2), :]
            taken = sum(jnp.take_along_axis(value, pick, axis=1) for pick in picks)
            flat = jnp.where(column == c, taken, flat)
        packed = jnp.where(turn == f, flat, packed)
    for k in range(pack_ref.shape[0]):
        pack_ref[k] = packed


def total_of(tiles):
    parts = list(tiles)
    while len(parts) > 1:
        parts = [
            parts[i] + parts[i + 1] if i + 1 < len(parts) else parts[i] for i in range(0, len(parts), 2)
        ]
    value = parts[0]
    value = sum(value[:, c : c + LANES] for c in range(0, value.shape[1], LANES))
    return jnp.sum(jnp.sum(value, axis=0, keepdims=True), axis=1, keepdims=True)


def conjugate(source, east_face, north_face, source_term):
    height = source.shape[0]

    def split(value):
        return [value[r : r + TILE] for r in range(0, height, TILE)]

    def up(value):
        return pltpu.roll(value, height - 1, 0)

    def down(value):
        return pltpu.roll(value, 1, 0)

    west_face = lane_shift(east_face, -1)
    south_face = down(north_face)
    diagonal = source_term + ((east_face + west_face) + (north_face + south_face))

    def apply(value):
        return diagonal * value - (
            (east_face * lane_shift(value, 1) + west_face * lane_shift(value, -1))
            + (north_face * up(value) + south_face * down(value))
        )

    iterate = jnp.zeros_like(source)
    remain = source
    image_r = apply(source)
    direction = image_d = second = None
    over_norm = over_step = None
    for step in range(BOTTOM_ITERS):
        norm = total_of(split(remain * remain))
        energy = total_of(split(remain * image_r))
        last = step == BOTTOM_ITERS - 1
        ahead = None if last else apply(image_r)
        if step == 0:
            direction, image_d, second = remain, image_r, ahead
        else:
            ratio = norm * over_norm
            energy = energy - ratio * (norm * over_step)
            direction = remain + ratio * direction
            if not last:
                image_d = image_r + ratio * image_d
                second = ahead + ratio * second
        step_size = norm / energy
        over_norm = 1.0 / norm
        over_step = energy * over_norm
        iterate = iterate + step_size * direction
        if not last:
            remain = remain - step_size * image_d
            image_r = image_r - step_size * second
    return iterate


def ascend(lat_count, lon_count, blocks_ref, *rest):
    level_refs = [rest[KEPT * i : KEPT * i + KEPT] for i in range(LEVELS)]
    diagonal_ref, solution_ref, residual_ref, window_ref, order_ref, sems = rest[KEPT * LEVELS :]
    lon_index = lax.axis_index("lon")
    lat_index = lax.axis_index("lat")
    rows, cols = solution_ref.shape
    count, width = diagonal_ref.shape[0], diagonal_ref.shape[2]
    own_columns = cols // LANES
    columns = width // LANES
    stride = 1 << LEVELS
    bottom_rows = rows // stride
    bottom_width = cols // stride
    group = LANES // bottom_width
    slot = iota((bottom_rows, LANES), 1) // bottom_width
    fields = []
    for f in range(4):
        strips = []
        for a in range(lat_count):
            pieces = []
            for c in range(lon_count // group):
                merged = None
                for j in range(group):
                    block = blocks_ref[a * lon_count + c * group + j]
                    merged = block if merged is None else jnp.where(slot == (f + j) % group, block, merged)
                pieces.append(lane_shift(merged, f * bottom_width))
            strips.append(jnp.concatenate(pieces, axis=1))
        fields.append(jnp.concatenate(strips, axis=0))
    iterate = conjugate(*fields)

    bottom_height = lat_count * bottom_rows
    whole_width = lon_count * bottom_width
    pad = 2 * TILE
    window_ref[pl.ds(0, pad), :] = jnp.zeros((pad, LANES), jnp.float32)
    window_ref[pl.ds(pad + bottom_height, pad), :] = jnp.zeros((pad, LANES), jnp.float32)
    half = LANES // 2
    margin = half // stride
    shift = lax.rem(margin - SHIFT - lon_index * bottom_width + whole_width, whole_width)
    window_ref[pl.ds(pad, bottom_height), :] = pltpu.roll(iterate, shift, 1)[:, :LANES]
    start = pl.multiple_of(lat_index * bottom_rows, TILE)
    tiles = count >> LEVELS
    lane = iota((TILE, LANES), 1)
    ahead = (rows + HALO) // stride // tiles
    sublane = iota((TILE, LANES), 0)
    step = 1 << (LEVELS - 1)
    center, plus, minus = [], [], []
    for t in range(tiles):
        upper = window_ref[pl.ds(start + pad + t, TILE, stride=tiles), :]
        lower = window_ref[pl.ds(start + pad + t - tiles * TILE, TILE, stride=tiles), :]
        value = jnp.where(sublane < ahead, upper, lower)
        for target, move in ((center, 0), (plus, step), (minus, -step)):
            parts = []
            for c in range(columns):
                place = c * LANES + lane + (move + width)
                place = jnp.where(place >= width, place - width, place)
                place = jnp.where(place >= width, place - width, place)
                pick = jnp.where(place < cols + half, margin + place // stride, (place - (cols + half)) // stride)
                parts.append(jnp.take_along_axis(value, pick, axis=1))
            target.append(jnp.concatenate(parts, axis=1))

    lane = iota((TILE, width), 1)
    for level in range(LEVELS - 1, -1, -1):
        stride = 1 << level
        east_face, west_face, north_face, inverse, source, swept = map(tiles_of, level_refs[level])
        faces = (east_face, west_face, north_face)
        if level < LEVELS - 1:
            first = lax.rem(lane // stride, 2) == 0
            east = [lane_shift(value, stride) for value in field]
            west = [lane_shift(value, -stride) for value in field]
            west_two = [lane_shift(value, -2 * stride) for value in field]
            coarse = range(len(field))
            center = [jnp.where(first, field[t], west[t]) for t in coarse]
            plus = [jnp.where(first, field[t], east[t]) for t in coarse]
            minus = [jnp.where(first, west_two[t], west[t]) for t in coarse]
        spread = [center[t // 2] for t in range(count >> level)]
        field = []
        for t in range(count >> level):
            around = (east_face[t] * plus[t // 2] + west_face[t] * minus[t // 2]) + (
                north_face[t] * north_of(spread, t) + south_of(north_face, t) * south_of(spread, t)
            )
            here = spread[t]
            if level == 0:
                here = jnp.where(east_face[t] + north_face[t] > 0.0, here, 0.0)
            field.append(swept[t] + ((1.0 - DAMPING) * here + inverse[t] * around))
        for _ in range(SWEEPS - 1):
            field = sweep(field, source, inverse, faces, stride)
    correction = field
    own_sublanes = rows // count

    def send_out(k, ref, tiles):
        copies = []
        for c in range(own_columns):
            part = slice(c * LANES, (c + 1) * LANES)
            for t in range(count):
                order_ref[k, c, pl.ds(t, own_sublanes, stride=count), :] = tiles[t][:own_sublanes, part]
            copies.append(pltpu.make_async_copy(order_ref.at[k, c], ref.at[:, part], sems.at[k, c]))
            copies[-1].start()
        return copies

    copies = send_out(0, solution_ref, correction)
    final = remainder(correction, source, tiles_of(diagonal_ref), faces, 1)
    copies += send_out(1, residual_ref, final)
    for copy in copies:
        copy.wait()


def near_pairs(lat_count):
    return [(a, a ^ 1) for a in range(lat_count)]


def far_pairs(lon_count, lat_count, east):
    pairs = []
    for i in range(lon_count):
        for a in range(lat_count):
            b = a + 1 if a % 2 else a - 1
            j = (i + east) % lon_count
            if b < 0 or b == lat_count:
                b, j = a, i ^ 1
            pairs.append((i * lat_count + a, j * lat_count + b))
    return pairs


def on_device(lat_count, lon_count, forcing, surface_term, sea_cells, levels):
    rows, cols = forcing.shape
    height, width = rows + 2 * HALO, cols + LANES
    count = height // TILE
    f32 = jnp.float32
    vmem = pl.BlockSpec(memory_space=pltpu.VMEM)
    hbm = pl.BlockSpec(memory_space=pltpu.HBM)
    params = pltpu.CompilerParams(vmem_limit_bytes=VMEM_LIMIT)
    lat_index = lax.axis_index("lat").astype(jnp.int32)
    inputs = [
        pltpu.with_memory_space_constraint(x, pltpu.HBM) for x in (forcing, surface_term, sea_cells, levels)
    ]
    own, east_edge, west_edge = pl.pallas_call(
        prepare,
        out_shape=[
            jax.ShapeDtypeStruct((FIELDS, rows, cols), f32),
            jax.ShapeDtypeStruct((rows, LANES), f32),
            jax.ShapeDtypeStruct((rows, LANES), f32),
        ],
        in_specs=[hbm] * 4,
        out_specs=[vmem] * 3,
        scratch_shapes=[
            pltpu.VMEM((rows, cols), f32),
            pltpu.VMEM((rows, cols), f32),
            pltpu.VMEM((rows, cols), jnp.int32),
            pltpu.VMEM((rows, cols), jnp.int32),
            pltpu.SemaphoreType.DMA((4,)),
        ],
        compiler_params=params,
        name="prepare",
    )(*inputs)

    lat_near, lat_far = pl.pallas_call(
        prepare_rows,
        out_shape=[jax.ShapeDtypeStruct((HALO, FIELDS * cols + LANES), f32)] * 2,
        in_specs=[vmem] * 2,
        out_specs=[vmem] * 2,
        compiler_params=params,
        name="prepare_rows",
    )(own, west_edge)

    diagonal_edge = pl.pallas_call(
        prepare_corner,
        out_shape=jax.ShapeDtypeStruct((HALO, LANES), f32),
        in_specs=[vmem] * 2,
        out_specs=vmem,
        compiler_params=params,
        name="prepare_corner",
    )(east_edge, lat_far)
    eastward = [(i, (i + 1) % lon_count) for i in range(lon_count)]
    westward = [(target, source) for source, target in eastward]
    west_halo = lax.ppermute(east_edge, "lon", eastward)
    lat_far = lax.ppermute(lat_far, ("lon", "lat"), far_pairs(lon_count, lat_count, 0))
    west_far = lax.ppermute(diagonal_edge, ("lon", "lat"), far_pairs(lon_count, lat_count, 1))
    lat_near = lax.ppermute(lat_near, "lat", near_pairs(lat_count))
    odd = lat_index % 2 == 1
    west_near = lax.ppermute(
        jnp.where(odd, west_halo[:HALO], west_halo[rows - HALO :]), "lat", near_pairs(lat_count)
    )

    def scales(halo):
        tall = rows + 2 * halo
        tiles = tall // TILE
        row = jnp.arange(TILE)[None, :] * tiles + jnp.arange(tiles)[:, None]
        row = jnp.where(row < rows + halo, row, row - tall).astype(f32) + (lat_index * rows).astype(f32)
        center, northern = metric(row)
        return jnp.broadcast_to(jnp.stack([1.0 / center, northern])[..., None], (2, tiles, TILE, LANES))

    devices = lat_count * lon_count
    grid = pltpu.VMEM((FIELDS, width // LANES, height, LANES), f32)
    packed, edges = pl.pallas_call(
        functools.partial(descend, lat_count),
        out_shape=[
            jax.ShapeDtypeStruct((devices, rows >> LEVELS, LANES), f32),
            jax.ShapeDtypeStruct((height, LANES), f32),
        ],
        in_specs=[vmem] * 8,
        out_specs=[vmem] * 2,
        scratch_shapes=[
            pltpu.VMEM((FIELDS, width // LANES, rows + 2 * REACH, LANES), f32),
            pltpu.VMEM((4, width // LANES, (rows + 2 * REACH) >> (LEVELS - 1), LANES), f32),
        ],
        compiler_params=params,
        name="descend",
    )(own, lat_near, lat_far, west_halo, west_near, west_far, west_edge, scales(REACH))
    east_halo = lax.ppermute(edges, "lon", westward)
    blocks = lax.all_to_all(packed, ("lat", "lon"), 0, 0, tiled=True)

    level_shapes = []
    for level in range(LEVELS):
        level_shapes += [jax.ShapeDtypeStruct((count >> level, TILE, width), f32)] * KEPT
    held_shapes = level_shapes + [jax.ShapeDtypeStruct((count, TILE, width), f32)]
    fine_scale = scales(HALO)
    held = pl.pallas_call(
        functools.partial(hold, lat_count),
        out_shape=held_shapes + [jax.ShapeDtypeStruct((FIELDS, count, TILE, LANES), f32)],
        in_specs=[vmem] * 7,
        out_specs=[vmem] * (1 + len(held_shapes)),
        scratch_shapes=[grid],
        compiler_params=params,
        cost_estimate=pl.CostEstimate(flops=0, bytes_accessed=60 * 1024 * 1024, transcendentals=0),
        name="hold",
    )(own, lat_near, lat_far, west_halo, west_near, west_far, fine_scale)
    held, raw = held[:-1], held[-1]
    held = pl.pallas_call(
        functools.partial(patch, lat_count),
        out_shape=held_shapes,
        in_specs=[vmem] * (3 + len(held_shapes)),
        out_specs=[vmem] * len(held_shapes),
        scratch_shapes=[pltpu.VMEM((FIELDS, height, LANES), f32)],
        input_output_aliases={3 + i: i for i in range(len(held_shapes))},
        compiler_params=params,
        name="patch",
    )(raw, east_halo, fine_scale, *held)

    return pl.pallas_call(
        functools.partial(ascend, lat_count, lon_count),
        out_shape=[jax.ShapeDtypeStruct((rows, cols), f32)] * 2,
        in_specs=[vmem] * (1 + len(held)),
        out_specs=[hbm] * 2,
        scratch_shapes=[
            pltpu.VMEM((lat_count * (rows >> LEVELS) + 4 * TILE, LANES), f32),
            pltpu.VMEM((2, cols // LANES, rows, LANES), f32),
            pltpu.SemaphoreType.DMA((2, cols // LANES)),
        ],
        compiler_params=params,
        name="ascend",
    )(blocks, *held)


def solution(mesh):
    body = functools.partial(on_device, mesh.shape["lat"], mesh.shape["lon"])
    return jax.shard_map(
        body,
        mesh=mesh,
        in_specs=(P("lat", "lon"),) * 4,
        out_specs=(P("lat", "lon"),) * 2,
        check_vma=False,
    )
```

```python
import functools

import jax
import jax.numpy as jnp
from jax import lax
from jax.experimental import pallas as pl
from jax.experimental.pallas import tpu as pltpu
from jax.sharding import PartitionSpec as P

LEVELS = 3
SWEEPS = 2
BOTTOM_ITERS = 6

DAMPING = 0.8
ROW_STEP = 150.0 / 8640.0
BAND_SOUTH = -50.0

HALO = 32
REACH = 16
LANES = 128
TILE = 8
FIELDS = 3
KEPT = 6
SHIFT = 2
VMEM_LIMIT = 8 * 1024 * 1024


def iota(shape, dim):
    return lax.broadcasted_iota(jnp.int32, shape, dim)


def lane_shift(field, count):
    return pltpu.roll(field, (-count) % field.shape[1], 1)


def north_of(tiles, t):
    if t + 1 < len(tiles):
        return tiles[t + 1]
    return pltpu.roll(tiles[0], TILE - 1, 0)


def south_of(tiles, t):
    if t > 0:
        return tiles[t - 1]
    return pltpu.roll(tiles[-1], 1, 0)


def neighbour_sum(field, faces, stride):
    east_face, west_face, north_face = faces
    upward = [north_face[t] * field[t] for t in range(len(field))]
    return [
        (east_face[t] * lane_shift(field[t], stride) + west_face[t] * lane_shift(field[t], -stride))
        + (north_face[t] * north_of(field, t) + south_of(upward, t))
        for t in range(len(field))
    ]


def sweep(field, source, inverse, faces, stride):
    around = neighbour_sum(field, faces, stride)
    return [
        (1.0 - DAMPING) * field[t] + inverse[t] * (source[t] + around[t]) for t in range(len(field))
    ]


def remainder(field, source, diagonal, faces, stride):
    around = neighbour_sum(field, faces, stride)
    return [source[t] - diagonal[t] * field[t] + around[t] for t in range(len(field))]


def tiles_of(ref):
    return [ref[t] for t in range(ref.shape[0])]


def keep(ref, tiles):
    for t, value in enumerate(tiles):
        ref[t] = value


def metric(row):
    center = jnp.cos(jnp.deg2rad(BAND_SOUTH + ROW_STEP * (row + 0.5)))
    northern = jnp.cos(jnp.deg2rad(BAND_SOUTH + ROW_STEP * (row + 1.0)))
    return center, northern


def prepare(forcing_ref, surface_ref, sea_ref, levels_ref,
            own_ref, east_edge_ref, west_edge_ref,
            forcing_buf, surface_buf, sea_buf, levels_buf, sems):
    copies = [
        pltpu.make_async_copy(source, target, sems.at[i])
        for i, (source, target) in enumerate((
            (levels_ref, levels_buf), (sea_ref, sea_buf), (surface_ref, surface_buf), (forcing_ref, forcing_buf),
        ))
    ]
    for copy in copies:
        copy.start()
    rows, cols = forcing_buf.shape
    first_row = lax.axis_index("lat") * rows
    row = (iota((rows, LANES), 0) + first_row).astype(jnp.float32)
    center = jnp.cos(jnp.deg2rad(BAND_SOUTH + ROW_STEP * (row + 0.5)))
    center = jnp.concatenate([center] * (cols // LANES), axis=1)
    for copy in copies:
        copy.wait()
    sea_mask = sea_buf[...].astype(jnp.float32)
    layers = levels_buf[...].astype(jnp.float32)
    depth = sea_mask * (layers * (0.00475 + 0.00025 * layers))
    fields = (depth, surface_buf[...] * center * sea_mask, forcing_buf[...] * sea_mask)
    slot = iota((rows, LANES), 1) // HALO
    slots = LANES // HALO
    west_edge = jnp.zeros((rows, LANES), jnp.float32)
    east_edge = jnp.zeros((rows, LANES), jnp.float32)
    for f, value in enumerate(fields):
        own_ref[f] = value
        west_edge = jnp.where(slot == f, lane_shift(value[:, :LANES], -f * HALO), west_edge)
        east_edge = jnp.where(
            slot == (f + slots - 1) % slots, lane_shift(value[:, cols - LANES :], -f * HALO), east_edge
        )
    east_edge_ref[...] = east_edge
    west_edge_ref[...] = west_edge


def prepare_corner(east_edge_ref, rows_ref, diagonal_edge_ref):
    rows = east_edge_ref.shape[0]
    odd = jnp.broadcast_to(lax.rem(lax.axis_index("lat"), 2), diagonal_edge_ref.shape) > 0
    diagonal_edge_ref[...] = jnp.where(odd, east_edge_ref[pl.ds(rows - HALO, HALO), :], east_edge_ref[pl.ds(0, HALO), :])


def prepare_rows(own_ref, west_edge_ref, lat_near_ref, lat_far_ref):
    rows, cols = own_ref.shape[1:]
    south, north = pl.ds(0, HALO), pl.ds(rows - HALO, HALO)
    odd = jnp.broadcast_to(lax.rem(lax.axis_index("lat"), 2), (HALO, cols)) > 0
    for f in range(FIELDS):
        south_edge, north_edge = own_ref[f, south, :], own_ref[f, north, :]
        part = slice(f * cols, (f + 1) * cols)
        lat_near_ref[:, part] = jnp.where(odd, south_edge, north_edge)
        lat_far_ref[:, part] = jnp.where(odd, north_edge, south_edge)
    odd = odd[:, :LANES]
    south_edge, north_edge = west_edge_ref[south, :], west_edge_ref[north, :]
    part = slice(FIELDS * cols, FIELDS * cols + LANES)
    lat_near_ref[:, part] = jnp.where(odd, south_edge, north_edge)
    lat_far_ref[:, part] = jnp.where(odd, north_edge, south_edge)


def fine_faces(depth, across, along):
    tiles = range(len(depth))
    east_face = [jnp.minimum(depth[t], lane_shift(depth[t], 1)) * across[t] for t in tiles]
    west_face = [jnp.minimum(depth[t], lane_shift(depth[t], -1)) * across[t] for t in tiles]
    north_face = [jnp.minimum(depth[t], north_of(depth, t)) * along[t] for t in tiles]
    return east_face, west_face, north_face


def coefficients(level, faces, source_term):
    east_face, west_face, north_face = faces
    diagonal = []
    for t in range(len(source_term)):
        total = source_term[t] + ((east_face[t] + west_face[t]) + (north_face[t] + south_of(north_face, t)))
        diagonal.append(jnp.where(source_term[t] > 0.0, total, 1.0))
    return faces, [DAMPING / value for value in diagonal], diagonal


def next_coefficients(level, faces, source_term):
    stride = 1 << level
    east_face, _, north_face = faces
    firsts = range(0, len(source_term), 2)
    east_sums = [east_face[t] + east_face[t + 1] for t in firsts]
    term_sums = [source_term[t] + source_term[t + 1] for t in firsts]
    east_next = [lane_shift(value, stride) for value in east_sums]
    west_next = [lane_shift(value, -stride) for value in east_sums]
    north_next = [north_face[t + 1] + lane_shift(north_face[t + 1], stride) for t in firsts]
    return (east_next, west_next, north_next), [value + lane_shift(value, stride) for value in term_sums]


def all_coefficients(depth, source_term, across, along):
    faces = fine_faces(depth, across, along)
    levels = []
    for level in range(LEVELS):
        levels.append(coefficients(level, faces, source_term) + (source_term,))
        if level < LEVELS - 1:
            faces, source_term = next_coefficients(level, faces, source_term)
    return levels


def level_down(level, faces, inverse, diagonal, source, sides):
    stride = 1 << level
    count = len(source)
    field = [inverse[t] * source[t] for t in range(count)]
    for k in range(SWEEPS - 1):
        if k == 0 and sides is not None:
            east_face, west_face, north_face = faces
            plus, minus = sides
            upward = [north_face[t] * field[t] for t in range(count)]
            around = [
                (
                    east_face[t] * (lane_shift(inverse[t], stride) * plus[t])
                    + west_face[t] * (lane_shift(inverse[t], -stride) * minus[t])
                )
                + (north_face[t] * north_of(field, t) + south_of(upward, t))
                for t in range(count)
            ]
            field = [(1.0 - DAMPING) * field[t] + inverse[t] * (source[t] + around[t]) for t in range(count)]
        else:
            field = sweep(field, source, inverse, faces, stride)
    return field, remainder(field, source, diagonal, faces, stride)


def level_next(level, image):
    stride = 1 << level
    left = [image[t] + image[t + 1] for t in range(0, len(image), 2)]
    source = [value + lane_shift(value, stride) for value in left]
    if left[0].shape[1] > LANES:
        return source, None
    plus = [lane_shift(value, 2 * stride) + lane_shift(value, 3 * stride) for value in left]
    minus = [lane_shift(value, -2 * stride) + lane_shift(value, -stride) for value in left]
    return source, (plus, minus)


def lay_out(lat_count, own_ref, lat_near_ref, lat_far_ref, west_ref, west_near_ref, west_far_ref, scale_ref, grid_ref):
    rows, cols = own_ref.shape[1], own_ref.shape[2]
    columns, height = grid_ref.shape[1], grid_ref.shape[2]
    count = height // TILE
    own_columns = cols // LANES
    halo = (height - rows) // 2
    lat_index = lax.axis_index("lat")
    lat_odd = lax.rem(lat_index, 2)
    near_row = rows + pl.multiple_of(lat_odd * halo, TILE)
    far_row = rows + pl.multiple_of((1 - lat_odd) * halo, TILE)
    near_part = pl.ds(pl.multiple_of(lat_odd * (HALO - halo), TILE), halo)
    far_part = pl.ds(pl.multiple_of((1 - lat_odd) * (HALO - halo), TILE), halo)
    last = LANES // HALO - 1
    at_end = (lat_index == 0) | (lat_index == lat_count - 1)

    def inside(value, far):
        return jnp.where(jnp.broadcast_to(at_end, value.shape), 0.0, value) if far else value

    parts = (
        (0, rows, None, west_ref[...], False),
        (near_row, halo, lat_near_ref.at[near_part], west_near_ref[near_part, :], False),
        (far_row, halo, lat_far_ref.at[far_part], west_far_ref[far_part, :], True),
    )
    for first, size, body_ref, west, far in parts:
        slot = iota((size, LANES), 1) // HALO
        for f in range(FIELDS):
            for c in range(own_columns):
                if body_ref is None:
                    value = own_ref[f, :, c * LANES : (c + 1) * LANES]
                else:
                    value = body_ref[:, f * cols + c * LANES : f * cols + (c + 1) * LANES]
                grid_ref[f, c, pl.ds(first, size), :] = inside(value, far)
            side = jnp.where(slot == (f + last) % (last + 1), west, 0.0)
            grid_ref[f, own_columns, pl.ds(first, size), :] = inside(lane_shift(side, f * HALO), far)

    def load(f):
        return [
            jnp.concatenate(
                [grid_ref[f, c, pl.ds(t, TILE, stride=count), :] for c in range(columns)], axis=1
            )
            for t in range(count)
        ]

    depth, source_term, source = load(0), load(1), load(2)
    across = [jnp.concatenate([scale_ref[0, t]] * columns, axis=1) for t in range(count)]
    along = [jnp.concatenate([scale_ref[1, t]] * columns, axis=1) for t in range(count)]
    return depth, source_term, source, across, along


def way_down(depth, source_term, source, across, along, put):
    levels = all_coefficients(depth, source_term, across, along)
    sides = None
    for level, (faces, inverse, diagonal, _) in enumerate(levels):
        field, image = level_down(level, faces, inverse, diagonal, source, sides)
        swept = sweep(field, source, inverse, faces, 1 << level)
        put(level, faces + (inverse, source, swept) + ((diagonal,) if level == 0 else ()))
        if level < LEVELS - 1:
            source, sides = level_next(level, image)


def split_refs(rest):
    level_refs = [list(rest[KEPT * i : KEPT * i + KEPT]) for i in range(LEVELS)]
    level_refs[0].append(rest[KEPT * LEVELS])
    return level_refs, rest[KEPT * LEVELS + 1 :]


def hold(lat_count, own_ref, lat_near_ref, lat_far_ref, west_ref, west_near_ref, west_far_ref, scale_ref, *rest):
    level_refs, (raw_ref, grid_ref) = split_refs(rest)
    values = lay_out(lat_count, own_ref, lat_near_ref, lat_far_ref, west_ref, west_near_ref, west_far_ref, scale_ref, grid_ref)
    cols = own_ref.shape[2]
    for f in range(FIELDS):
        for t, value in enumerate(values[f]):
            raw_ref[f, t] = value[:, cols - LANES : cols]

    def put(level, kept):
        for ref, tiles in zip(level_refs[level], kept):
            keep(ref, tiles)

    way_down(*values, put)


def patch(lat_count, raw_ref, east_ref, scale_ref, *rest):
    half = len(rest) // 2
    held_refs, _ = split_refs(rest[:half])
    level_refs, (strip_ref,) = split_refs(rest[half:])
    count = raw_ref.shape[1]
    height = count * TILE
    rows = height - 2 * HALO
    lat_index = lax.axis_index("lat")
    lat_odd = lax.rem(lat_index, 2)
    near_row = rows + pl.multiple_of(lat_odd * HALO, HALO)
    far_row = rows + pl.multiple_of((1 - lat_odd) * HALO, HALO)
    at_end = (lat_index == 0) | (lat_index == lat_count - 1)
    for first, at, size, far in ((0, 0, rows, False), (near_row, rows, HALO, False), (far_row, rows + HALO, HALO, True)):
        side = east_ref[pl.ds(at, size), :]
        if far:
            side = jnp.where(jnp.broadcast_to(at_end, side.shape), 0.0, side)
        for f in range(FIELDS):
            strip_ref[f, pl.ds(first, size), :] = lane_shift(side, f * HALO)
    lane = iota((TILE, LANES), 1)
    own = lane >= LANES // 2
    fields = [
        [
            jnp.where(own, raw_ref[f, t],
                      jnp.where(lane < HALO, strip_ref[f, pl.ds(t, TILE, stride=count), :], 0.0))
            for t in range(count)
        ]
        for f in range(FIELDS)
    ]

    def put(level, kept):
        for held_ref, ref, tiles in zip(held_refs[level], level_refs[level], kept):
            last = ref.shape[2] - LANES
            for t, value in enumerate(tiles):
                held = held_ref[t]
                edge = jnp.where(lane >= LANES - HALO, value, held[:, last - LANES : last])
                halo = jnp.where(own, held[:, last:], value)
                ref[t] = jnp.concatenate([held[:, : last - LANES], edge, halo], axis=1)

    way_down(*fields, [scale_ref[0, t] for t in range(count)], [scale_ref[1, t] for t in range(count)], put)


def descend(lat_count, own_ref, lat_near_ref, lat_far_ref, west_ref, west_near_ref, west_far_ref, west_edge_ref, scale_ref,
            pack_ref, edge_ref, grid_ref, plain_ref):
    rows = own_ref.shape[1]
    edge = slice(FIELDS * own_ref.shape[2], FIELDS * own_ref.shape[2] + LANES)
    edge_ref[pl.ds(0, rows), :] = west_edge_ref[...]
    edge_ref[pl.ds(rows, HALO), :] = lat_near_ref[:, edge]
    edge_ref[pl.ds(rows + HALO, HALO), :] = lat_far_ref[:, edge]
    lon_index = lax.axis_index("lon")
    cols = own_ref.shape[2]
    own_columns = cols // LANES
    columns = grid_ref.shape[1]
    depth, source_term, source, across, along = lay_out(
        lat_count, own_ref, lat_near_ref, lat_far_ref, west_ref, west_near_ref, west_far_ref, scale_ref, grid_ref
    )
    levels = all_coefficients(depth, source_term, across, along)
    sides = None
    for level, (faces, inverse, diagonal, source_term) in enumerate(levels):
        _, image = level_down(level, faces, inverse, diagonal, source, sides)
        if level < LEVELS - 1:
            source, sides = level_next(level, image)

    east_face, _, north_face = faces
    for f, values in enumerate((image, east_face, north_face, source_term)):
        for t, value in enumerate(values):
            for c in range(columns):
                plain_ref[f, c, pl.ds(t, TILE, stride=len(values)), :] = value[:, c * LANES : (c + 1) * LANES]
    stride = 1 << LEVELS
    bottom_rows = rows // stride
    bottom_width = cols // stride
    group = LANES // bottom_width
    per_column = LANES // stride
    lane = iota((bottom_rows, LANES), 1)
    cell = lane % bottom_width - SHIFT
    column = jnp.where(cell < 0, own_columns, cell // per_column)
    west_part = jnp.where(cell < 0, LANES + cell * stride, (cell % per_column) * stride)
    east_part = west_part + stride // 2
    turn = lax.rem(lane // bottom_width + group - lax.rem(lon_index, group), group)
    packed = jnp.zeros((bottom_rows, LANES), jnp.float32)
    for f, picks in enumerate(((west_part, east_part), (east_part,), (west_part, east_part), (west_part, east_part))):
        flat = jnp.zeros((bottom_rows, LANES), jnp.float32)
        for c in range(columns):
            value = plain_ref[f, c, pl.ds(1, bottom_rows, stride=2), :]
            if f != 2:
                value = value + plain_ref[f, c, pl.ds(0, bottom_rows, stride=2), :]
            taken = sum(jnp.take_along_axis(value, pick, axis=1) for pick in picks)
            flat = jnp.where(column == c, taken, flat)
        packed = jnp.where(turn == f, flat, packed)
    for k in range(pack_ref.shape[0]):
        pack_ref[k] = packed


def total_of(tiles):
    parts = list(tiles)
    while len(parts) > 1:
        parts = [
            parts[i] + parts[i + 1] if i + 1 < len(parts) else parts[i] for i in range(0, len(parts), 2)
        ]
    value = parts[0]
    value = sum(value[:, c : c + LANES] for c in range(0, value.shape[1], LANES))
    return jnp.sum(jnp.sum(value, axis=0, keepdims=True), axis=1, keepdims=True)


def conjugate(source, east_face, north_face, source_term):
    height = source.shape[0]

    def split(value):
        return [value[r : r + TILE] for r in range(0, height, TILE)]

    def up(value):
        return pltpu.roll(value, height - 1, 0)

    def down(value):
        return pltpu.roll(value, 1, 0)

    west_face = lane_shift(east_face, -1)
    south_face = down(north_face)
    diagonal = source_term + ((east_face + west_face) + (north_face + south_face))

    def apply(value):
        return diagonal * value - (
            (east_face * lane_shift(value, 1) + west_face * lane_shift(value, -1))
            + (north_face * up(value) + south_face * down(value))
        )

    iterate = jnp.zeros_like(source)
    remain = source
    image_r = apply(source)
    direction = image_d = second = None
    over_norm = over_step = None
    for step in range(BOTTOM_ITERS):
        norm = total_of(split(remain * remain))
        energy = total_of(split(remain * image_r))
        last = step == BOTTOM_ITERS - 1
        ahead = None if last else apply(image_r)
        if step == 0:
            direction, image_d, second = remain, image_r, ahead
        else:
            ratio = norm * over_norm
            energy = energy - ratio * (norm * over_step)
            direction = remain + ratio * direction
            if not last:
                image_d = image_r + ratio * image_d
                second = ahead + ratio * second
        step_size = norm / energy
        over_norm = 1.0 / norm
        over_step = energy * over_norm
        iterate = iterate + step_size * direction
        if not last:
            remain = remain - step_size * image_d
            image_r = image_r - step_size * second
    return iterate


def ascend(lat_count, lon_count, blocks_ref, *rest):
    level_refs = [rest[KEPT * i : KEPT * i + KEPT] for i in range(LEVELS)]
    diagonal_ref, solution_ref, residual_ref, window_ref, order_ref, sems = rest[KEPT * LEVELS :]
    lon_index = lax.axis_index("lon")
    lat_index = lax.axis_index("lat")
    rows, cols = solution_ref.shape
    count, width = diagonal_ref.shape[0], diagonal_ref.shape[2]
    own_columns = cols // LANES
    columns = width // LANES
    stride = 1 << LEVELS
    bottom_rows = rows // stride
    bottom_width = cols // stride
    group = LANES // bottom_width
    slot = iota((bottom_rows, LANES), 1) // bottom_width
    fields = []
    for f in range(4):
        strips = []
        for a in range(lat_count):
            pieces = []
            for c in range(lon_count // group):
                merged = None
                for j in range(group):
                    block = blocks_ref[a * lon_count + c * group + j]
                    merged = block if merged is None else jnp.where(slot == (f + j) % group, block, merged)
                pieces.append(lane_shift(merged, f * bottom_width))
            strips.append(jnp.concatenate(pieces, axis=1))
        fields.append(jnp.concatenate(strips, axis=0))
    iterate = conjugate(*fields)

    bottom_height = lat_count * bottom_rows
    whole_width = lon_count * bottom_width
    pad = 2 * TILE
    window_ref[pl.ds(0, pad), :] = jnp.zeros((pad, LANES), jnp.float32)
    window_ref[pl.ds(pad + bottom_height, pad), :] = jnp.zeros((pad, LANES), jnp.float32)
    half = LANES // 2
    margin = half // stride
    shift = lax.rem(margin - SHIFT - lon_index * bottom_width + whole_width, whole_width)
    window_ref[pl.ds(pad, bottom_height), :] = pltpu.roll(iterate, shift, 1)[:, :LANES]
    start = pl.multiple_of(lat_index * bottom_rows, TILE)
    tiles = count >> LEVELS
    lane = iota((TILE, LANES), 1)
    ahead = (rows + HALO) // stride // tiles
    sublane = iota((TILE, LANES), 0)
    step = 1 << (LEVELS - 1)
    center, plus, minus = [], [], []
    for t in range(tiles):
        upper = window_ref[pl.ds(start + pad + t, TILE, stride=tiles), :]
        lower = window_ref[pl.ds(start + pad + t - tiles * TILE, TILE, stride=tiles), :]
        value = jnp.where(sublane < ahead, upper, lower)
        for target, move in ((center, 0), (plus, step), (minus, -step)):
            parts = []
            for c in range(columns):
                place = c * LANES + lane + (move + width)
                place = jnp.where(place >= width, place - width, place)
                place = jnp.where(place >= width, place - width, place)
                pick = jnp.where(place < cols + half, margin + place // stride, (place - (cols + half)) // stride)
                parts.append(jnp.take_along_axis(value, pick, axis=1))
            target.append(jnp.concatenate(parts, axis=1))

    lane = iota((TILE, width), 1)
    for level in range(LEVELS - 1, -1, -1):
        stride = 1 << level
        east_face, west_face, north_face, inverse, source, swept = map(tiles_of, level_refs[level])
        faces = (east_face, west_face, north_face)
        if level < LEVELS - 1:
            first = lax.rem(lane // stride, 2) == 0
            east = [lane_shift(value, stride) for value in field]
            west = [lane_shift(value, -stride) for value in field]
            west_two = [lane_shift(value, -2 * stride) for value in field]
            coarse = range(len(field))
            center = [jnp.where(first, field[t], west[t]) for t in coarse]
            plus = [jnp.where(first, field[t], east[t]) for t in coarse]
            minus = [jnp.where(first, west_two[t], west[t]) for t in coarse]
        spread = [center[t // 2] for t in range(count >> level)]
        field = []
        for t in range(count >> level):
            around = (east_face[t] * plus[t // 2] + west_face[t] * minus[t // 2]) + (
                north_face[t] * north_of(spread, t) + south_of(north_face, t) * south_of(spread, t)
            )
            here = spread[t]
            if level == 0:
                here = jnp.where(east_face[t] + north_face[t] > 0.0, here, 0.0)
            field.append(swept[t] + ((1.0 - DAMPING) * here + inverse[t] * around))
        for _ in range(SWEEPS - 1):
            field = sweep(field, source, inverse, faces, stride)
    correction = field
    own_sublanes = rows // count

    def send_out(k, ref, tiles):
        copies = []
        for c in range(own_columns):
            part = slice(c * LANES, (c + 1) * LANES)
            for t in range(count):
                order_ref[k, c, pl.ds(t, own_sublanes, stride=count), :] = tiles[t][:own_sublanes, part]
            copies.append(pltpu.make_async_copy(order_ref.at[k, c], ref.at[:, part], sems.at[k, c]))
            copies[-1].start()
        return copies

    copies = send_out(0, solution_ref, correction)
    final = remainder(correction, source, tiles_of(diagonal_ref), faces, 1)
    copies += send_out(1, residual_ref, final)
    for copy in copies:
        copy.wait()


def near_pairs(lat_count):
    return [(a, a ^ 1) for a in range(lat_count)]


def far_pairs(lon_count, lat_count, east):
    pairs = []
    for i in range(lon_count):
        for a in range(lat_count):
            b = a + 1 if a % 2 else a - 1
            j = (i + east) % lon_count
            if b < 0 or b == lat_count:
                b, j = a, i ^ 1
            pairs.append((i * lat_count + a, j * lat_count + b))
    return pairs


def on_device(lat_count, lon_count, forcing, surface_term, sea_cells, levels):
    rows, cols = forcing.shape
    height, width = rows + 2 * HALO, cols + LANES
    count = height // TILE
    f32 = jnp.float32
    vmem = pl.BlockSpec(memory_space=pltpu.VMEM)
    hbm = pl.BlockSpec(memory_space=pltpu.HBM)
    params = pltpu.CompilerParams(vmem_limit_bytes=VMEM_LIMIT)
    lat_index = lax.axis_index("lat").astype(jnp.int32)
    inputs = [
        pltpu.with_memory_space_constraint(x, pltpu.HBM) for x in (forcing, surface_term, sea_cells, levels)
    ]
    own, east_edge, west_edge = pl.pallas_call(
        prepare,
        out_shape=[
            jax.ShapeDtypeStruct((FIELDS, rows, cols), f32),
            jax.ShapeDtypeStruct((rows, LANES), f32),
            jax.ShapeDtypeStruct((rows, LANES), f32),
        ],
        in_specs=[hbm] * 4,
        out_specs=[vmem] * 3,
        scratch_shapes=[
            pltpu.VMEM((rows, cols), f32),
            pltpu.VMEM((rows, cols), f32),
            pltpu.VMEM((rows, cols), jnp.int32),
            pltpu.VMEM((rows, cols), jnp.int32),
            pltpu.SemaphoreType.DMA((4,)),
        ],
        compiler_params=params,
        name="prepare",
    )(*inputs)

    lat_near, lat_far = pl.pallas_call(
        prepare_rows,
        out_shape=[jax.ShapeDtypeStruct((HALO, FIELDS * cols + LANES), f32)] * 2,
        in_specs=[vmem] * 2,
        out_specs=[vmem] * 2,
        compiler_params=params,
        name="prepare_rows",
    )(own, west_edge)

    diagonal_edge = pl.pallas_call(
        prepare_corner,
        out_shape=jax.ShapeDtypeStruct((HALO, LANES), f32),
        in_specs=[vmem] * 2,
        out_specs=vmem,
        compiler_params=params,
        name="prepare_corner",
    )(east_edge, lat_far)
    eastward = [(i, (i + 1) % lon_count) for i in range(lon_count)]
    westward = [(target, source) for source, target in eastward]
    west_halo = lax.ppermute(east_edge, "lon", eastward)
    lat_far = lax.ppermute(lat_far, ("lon", "lat"), far_pairs(lon_count, lat_count, 0))
    west_far = lax.ppermute(diagonal_edge, ("lon", "lat"), far_pairs(lon_count, lat_count, 1))
    lat_near = lax.ppermute(lat_near, "lat", near_pairs(lat_count))
    odd = lat_index % 2 == 1
    west_near = lax.ppermute(
        jnp.where(odd, west_halo[:HALO], west_halo[rows - HALO :]), "lat", near_pairs(lat_count)
    )

    def scales(halo):
        tall = rows + 2 * halo
        tiles = tall // TILE
        row = jnp.arange(TILE)[None, :] * tiles + jnp.arange(tiles)[:, None]
        row = jnp.where(row < rows + halo, row, row - tall).astype(f32) + (lat_index * rows).astype(f32)
        center, northern = metric(row)
        return jnp.broadcast_to(jnp.stack([1.0 / center, northern])[..., None], (2, tiles, TILE, LANES))

    devices = lat_count * lon_count
    grid = pltpu.VMEM((FIELDS, width // LANES, height, LANES), f32)
    packed, edges = pl.pallas_call(
        functools.partial(descend, lat_count),
        out_shape=[
            jax.ShapeDtypeStruct((devices, rows >> LEVELS, LANES), f32),
            jax.ShapeDtypeStruct((height, LANES), f32),
        ],
        in_specs=[vmem] * 8,
        out_specs=[vmem] * 2,
        scratch_shapes=[
            pltpu.VMEM((FIELDS, width // LANES, rows + 2 * REACH, LANES), f32),
            pltpu.VMEM((4, width // LANES, (rows + 2 * REACH) >> (LEVELS - 1), LANES), f32),
        ],
        compiler_params=params,
        name="descend",
    )(own, lat_near, lat_far, west_halo, west_near, west_far, west_edge, scales(REACH))
    east_halo = lax.ppermute(edges, "lon", westward)
    blocks = lax.all_to_all(packed, ("lat", "lon"), 0, 0, tiled=True)

    level_shapes = []
    for level in range(LEVELS):
        level_shapes += [jax.ShapeDtypeStruct((count >> level, TILE, width), f32)] * KEPT
    held_shapes = level_shapes + [jax.ShapeDtypeStruct((count, TILE, width), f32)]
    fine_scale = scales(HALO)
    held = pl.pallas_call(
        functools.partial(hold, lat_count),
        out_shape=held_shapes + [jax.ShapeDtypeStruct((FIELDS, count, TILE, LANES), f32)],
        in_specs=[vmem] * 7,
        out_specs=[vmem] * (1 + len(held_shapes)),
        scratch_shapes=[grid],
        compiler_params=params,
        cost_estimate=pl.CostEstimate(flops=0, bytes_accessed=60 * 1024 * 1024, transcendentals=0),
        name="hold",
    )(own, lat_near, lat_far, west_halo, west_near, west_far, fine_scale)
    held, raw = held[:-1], held[-1]
    held = pl.pallas_call(
        functools.partial(patch, lat_count),
        out_shape=held_shapes,
        in_specs=[vmem] * (3 + len(held_shapes)),
        out_specs=[vmem] * len(held_shapes),
        scratch_shapes=[pltpu.VMEM((FIELDS, height, LANES), f32)],
        compiler_params=params,
        name="patch",
    )(raw, east_halo, fine_scale, *held)

    return pl.pallas_call(
        functools.partial(ascend, lat_count, lon_count),
        out_shape=[jax.ShapeDtypeStruct((rows, cols), f32)] * 2,
        in_specs=[vmem] * (1 + len(held)),
        out_specs=[hbm] * 2,
        scratch_shapes=[
            pltpu.VMEM((lat_count * (rows >> LEVELS) + 4 * TILE, LANES), f32),
            pltpu.VMEM((2, cols // LANES, rows, LANES), f32),
            pltpu.SemaphoreType.DMA((2, cols // LANES)),
        ],
        compiler_params=params,
        name="ascend",
    )(blocks, *held)


def solution(mesh):
    body = functools.partial(on_device, mesh.shape["lat"], mesh.shape["lon"])
    return jax.shard_map(
        body,
        mesh=mesh,
        in_specs=(P("lat", "lon"),) * 4,
        out_specs=(P("lat", "lon"),) * 2,
        check_vma=False,
    )
```

```python
import functools

import jax
import jax.numpy as jnp
from jax import lax
from jax.experimental import pallas as pl
from jax.experimental.pallas import tpu as pltpu
from jax.sharding import PartitionSpec as P

LEVELS = 3
SWEEPS = 2
BOTTOM_ITERS = 6

DAMPING = 0.8
ROW_STEP = 150.0 / 8640.0
BAND_SOUTH = -50.0

HALO = 32
REACH = 16
LANES = 128
TILE = 8
FIELDS = 3
KEPT = 6
SHIFT = 2
VMEM_LIMIT = 8 * 1024 * 1024


def iota(shape, dim):
    return lax.broadcasted_iota(jnp.int32, shape, dim)


def lane_shift(field, count):
    return pltpu.roll(field, (-count) % field.shape[1], 1)


def north_of(tiles, t):
    if t + 1 < len(tiles):
        return tiles[t + 1]
    return pltpu.roll(tiles[0], TILE - 1, 0)


def south_of(tiles, t):
    if t > 0:
        return tiles[t - 1]
    return pltpu.roll(tiles[-1], 1, 0)


def neighbour_sum(field, faces, stride):
    east_face, west_face, north_face = faces
    upward = [north_face[t] * field[t] for t in range(len(field))]
    return [
        (east_face[t] * lane_shift(field[t], stride) + west_face[t] * lane_shift(field[t], -stride))
        + (north_face[t] * north_of(field, t) + south_of(upward, t))
        for t in range(len(field))
    ]


def sweep(field, source, inverse, faces, stride):
    around = neighbour_sum(field, faces, stride)
    return [
        (1.0 - DAMPING) * field[t] + inverse[t] * (source[t] + around[t]) for t in range(len(field))
    ]


def remainder(field, source, diagonal, faces, stride):
    around = neighbour_sum(field, faces, stride)
    return [source[t] - diagonal[t] * field[t] + around[t] for t in range(len(field))]


def tiles_of(ref):
    return [ref[t] for t in range(ref.shape[0])]


def keep(ref, tiles):
    for t, value in enumerate(tiles):
        ref[t] = value


def metric(row):
    center = jnp.cos(jnp.deg2rad(BAND_SOUTH + ROW_STEP * (row + 0.5)))
    northern = jnp.cos(jnp.deg2rad(BAND_SOUTH + ROW_STEP * (row + 1.0)))
    return center, northern


def prepare(forcing_ref, surface_ref, sea_ref, levels_ref,
            own_ref, east_edge_ref, west_edge_ref,
            forcing_buf, surface_buf, sea_buf, levels_buf, sems):
    copies = [
        pltpu.make_async_copy(source, target, sems.at[i])
        for i, (source, target) in enumerate((
            (levels_ref, levels_buf), (sea_ref, sea_buf), (surface_ref, surface_buf), (forcing_ref, forcing_buf),
        ))
    ]
    for copy in copies:
        copy.start()
    rows, cols = forcing_buf.shape
    first_row = lax.axis_index("lat") * rows
    row = (iota((rows, LANES), 0) + first_row).astype(jnp.float32)
    center = jnp.cos(jnp.deg2rad(BAND_SOUTH + ROW_STEP * (row + 0.5)))
    center = jnp.concatenate([center] * (cols // LANES), axis=1)
    for copy in copies:
        copy.wait()
    sea_mask = sea_buf[...].astype(jnp.float32)
    layers = levels_buf[...].astype(jnp.float32)
    depth = sea_mask * (layers * (0.00475 + 0.00025 * layers))
    fields = (depth, surface_buf[...] * center * sea_mask, forcing_buf[...] * sea_mask)
    slot = iota((rows, LANES), 1) // HALO
    slots = LANES // HALO
    west_edge = jnp.zeros((rows, LANES), jnp.float32)
    east_edge = jnp.zeros((rows, LANES), jnp.float32)
    for f, value in enumerate(fields):
        own_ref[f] = value
        west_edge = jnp.where(slot == f, lane_shift(value[:, :LANES], -f * HALO), west_edge)
        east_edge = jnp.where(
            slot == (f + slots - 1) % slots, lane_shift(value[:, cols - LANES :], -f * HALO), east_edge
        )
    east_edge_ref[...] = east_edge
    west_edge_ref[...] = west_edge


def prepare_corner(east_edge_ref, rows_ref, diagonal_edge_ref):
    rows = east_edge_ref.shape[0]
    odd = jnp.broadcast_to(lax.rem(lax.axis_index("lat"), 2), diagonal_edge_ref.shape) > 0
    diagonal_edge_ref[...] = jnp.where(odd, east_edge_ref[pl.ds(rows - HALO, HALO), :], east_edge_ref[pl.ds(0, HALO), :])


def prepare_rows(own_ref, west_edge_ref, lat_near_ref, lat_far_ref):
    rows, cols = own_ref.shape[1:]
    south, north = pl.ds(0, HALO), pl.ds(rows - HALO, HALO)
    odd = jnp.broadcast_to(lax.rem(lax.axis_index("lat"), 2), (HALO, cols)) > 0
    for f in range(FIELDS):
        south_edge, north_edge = own_ref[f, south, :], own_ref[f, north, :]
        part = slice(f * cols, (f + 1) * cols)
        lat_near_ref[:, part] = jnp.where(odd, south_edge, north_edge)
        lat_far_ref[:, part] = jnp.where(odd, north_edge, south_edge)
    odd = odd[:, :LANES]
    south_edge, north_edge = west_edge_ref[south, :], west_edge_ref[north, :]
    part = slice(FIELDS * cols, FIELDS * cols + LANES)
    lat_near_ref[:, part] = jnp.where(odd, south_edge, north_edge)
    lat_far_ref[:, part] = jnp.where(odd, north_edge, south_edge)


def fine_faces(depth, across, along):
    tiles = range(len(depth))
    east_face = [jnp.minimum(depth[t], lane_shift(depth[t], 1)) * across[t] for t in tiles]
    west_face = [jnp.minimum(depth[t], lane_shift(depth[t], -1)) * across[t] for t in tiles]
    north_face = [jnp.minimum(depth[t], north_of(depth, t)) * along[t] for t in tiles]
    return east_face, west_face, north_face


def coefficients(level, faces, source_term):
    east_face, west_face, north_face = faces
    diagonal = []
    for t in range(len(source_term)):
        total = source_term[t] + ((east_face[t] + west_face[t]) + (north_face[t] + south_of(north_face, t)))
        diagonal.append(jnp.where(source_term[t] > 0.0, total, 1.0))
    return faces, [DAMPING / value for value in diagonal], diagonal


def next_coefficients(level, faces, source_term):
    stride = 1 << level
    east_face, _, north_face = faces
    firsts = range(0, len(source_term), 2)
    east_sums = [east_face[t] + east_face[t + 1] for t in firsts]
    term_sums = [source_term[t] + source_term[t + 1] for t in firsts]
    east_next = [lane_shift(value, stride) for value in east_sums]
    west_next = [lane_shift(value, -stride) for value in east_sums]
    north_next = [north_face[t + 1] + lane_shift(north_face[t + 1], stride) for t in firsts]
    return (east_next, west_next, north_next), [value + lane_shift(value, stride) for value in term_sums]


def all_coefficients(depth, source_term, across, along):
    faces = fine_faces(depth, across, along)
    levels = []
    for level in range(LEVELS):
        levels.append(coefficients(level, faces, source_term) + (source_term,))
        if level < LEVELS - 1:
            faces, source_term = next_coefficients(level, faces, source_term)
    return levels


def level_down(level, faces, inverse, diagonal, source, sides):
    stride = 1 << level
    count = len(source)
    field = [inverse[t] * source[t] for t in range(count)]
    for k in range(SWEEPS - 1):
        if k == 0 and sides is not None:
            east_face, west_face, north_face = faces
            plus, minus = sides
            upward = [north_face[t] * field[t] for t in range(count)]
            around = [
                (
                    east_face[t] * (lane_shift(inverse[t], stride) * plus[t])
                    + west_face[t] * (lane_shift(inverse[t], -stride) * minus[t])
                )
                + (north_face[t] * north_of(field, t) + south_of(upward, t))
                for t in range(count)
            ]
            field = [(1.0 - DAMPING) * field[t] + inverse[t] * (source[t] + around[t]) for t in range(count)]
        else:
            field = sweep(field, source, inverse, faces, stride)
    return field, remainder(field, source, diagonal, faces, stride)


def level_next(level, image):
    stride = 1 << level
    left = [image[t] + image[t + 1] for t in range(0, len(image), 2)]
    source = [value + lane_shift(value, stride) for value in left]
    if left[0].shape[1] > LANES:
        return source, None
    plus = [lane_shift(value, 2 * stride) + lane_shift(value, 3 * stride) for value in left]
    minus = [lane_shift(value, -2 * stride) + lane_shift(value, -stride) for value in left]
    return source, (plus, minus)


def lay_out(lat_count, own_ref, lat_near_ref, lat_far_ref, west_ref, west_near_ref, west_far_ref, scale_ref, grid_ref):
    rows, cols = own_ref.shape[1], own_ref.shape[2]
    columns, height = grid_ref.shape[1], grid_ref.shape[2]
    count = height // TILE
    own_columns = cols // LANES
    halo = (height - rows) // 2
    lat_index = lax.axis_index("lat")
    lat_odd = lax.rem(lat_index, 2)
    near_row = rows + pl.multiple_of(lat_odd * halo, TILE)
    far_row = rows + pl.multiple_of((1 - lat_odd) * halo, TILE)
    near_part = pl.ds(pl.multiple_of(lat_odd * (HALO - halo), TILE), halo)
    far_part = pl.ds(pl.multiple_of((1 - lat_odd) * (HALO - halo), TILE), halo)
    last = LANES // HALO - 1
    at_end = (lat_index == 0) | (lat_index == lat_count - 1)

    def inside(value, far):
        return jnp.where(jnp.broadcast_to(at_end, value.shape), 0.0, value) if far else value

    parts = (
        (0, rows, None, west_ref[...], False),
        (near_row, halo, lat_near_ref.at[near_part], west_near_ref[near_part, :], False),
        (far_row, halo, lat_far_ref.at[far_part], west_far_ref[far_part, :], True),
    )
    for first, size, body_ref, west, far in parts:
        slot = iota((size, LANES), 1) // HALO
        for f in range(FIELDS):
            for c in range(own_columns):
                if body_ref is None:
                    value = own_ref[f, :, c * LANES : (c + 1) * LANES]
                else:
                    value = body_ref[:, f * cols + c * LANES : f * cols + (c + 1) * LANES]
                grid_ref[f, c, pl.ds(first, size), :] = inside(value, far)
            side = jnp.where(slot == (f + last) % (last + 1), west, 0.0)
            grid_ref[f, own_columns, pl.ds(first, size), :] = inside(lane_shift(side, f * HALO), far)

    def load(f):
        return [
            jnp.concatenate(
                [grid_ref[f, c, pl.ds(t, TILE, stride=count), :] for c in range(columns)], axis=1
            )
            for t in range(count)
        ]

    depth, source_term, source = load(0), load(1), load(2)
    across = [jnp.concatenate([scale_ref[0, t]] * columns, axis=1) for t in range(count)]
    along = [jnp.concatenate([scale_ref[1, t]] * columns, axis=1) for t in range(count)]
    return depth, source_term, source, across, along


def way_down(depth, source_term, source, across, along, put):
    levels = all_coefficients(depth, source_term, across, along)
    sides = None
    for level, (faces, inverse, diagonal, _) in enumerate(levels):
        field, image = level_down(level, faces, inverse, diagonal, source, sides)
        swept = sweep(field, source, inverse, faces, 1 << level)
        put(level, faces + (inverse, source, swept) + ((diagonal,) if level == 0 else ()))
        if level < LEVELS - 1:
            source, sides = level_next(level, image)


def split_refs(rest):
    level_refs = [list(rest[KEPT * i : KEPT * i + KEPT]) for i in range(LEVELS)]
    level_refs[0].append(rest[KEPT * LEVELS])
    return level_refs, rest[KEPT * LEVELS + 1 :]


def hold(lat_count, own_ref, lat_near_ref, lat_far_ref, west_ref, west_near_ref, west_far_ref, scale_ref, *rest):
    level_refs, (raw_ref, grid_ref) = split_refs(rest)
    values = lay_out(lat_count, own_ref, lat_near_ref, lat_far_ref, west_ref, west_near_ref, west_far_ref, scale_ref, grid_ref)
    cols = own_ref.shape[2]
    for f in range(FIELDS):
        for t, value in enumerate(values[f]):
            raw_ref[f, t] = value[:, cols - LANES : cols]

    def put(level, kept):
        for ref, tiles in zip(level_refs[level], kept):
            keep(ref, tiles)

    way_down(*values, put)


def patch(lat_count, raw_ref, east_ref, scale_ref, *rest):
    half = len(rest) // 2
    held_refs, _ = split_refs(rest[:half])
    level_refs, (strip_ref,) = split_refs(rest[half:])
    count = raw_ref.shape[1]
    height = count * TILE
    rows = height - 2 * HALO
    lat_index = lax.axis_index("lat")
    lat_odd = lax.rem(lat_index, 2)
    near_row = rows + pl.multiple_of(lat_odd * HALO, HALO)
    far_row = rows + pl.multiple_of((1 - lat_odd) * HALO, HALO)
    at_end = (lat_index == 0) | (lat_index == lat_count - 1)
    for first, at, size, far in ((0, 0, rows, False), (near_row, rows, HALO, False), (far_row, rows + HALO, HALO, True)):
        side = east_ref[pl.ds(at, size), :]
        if far:
            side = jnp.where(jnp.broadcast_to(at_end, side.shape), 0.0, side)
        for f in range(FIELDS):
            strip_ref[f, pl.ds(first, size), :] = lane_shift(side, f * HALO)
    lane = iota((TILE, LANES), 1)
    own = lane >= LANES // 2
    fields = [
        [
            jnp.where(own, raw_ref[f, t],
                      jnp.where(lane < HALO, strip_ref[f, pl.ds(t, TILE, stride=count), :], 0.0))
            for t in range(count)
        ]
        for f in range(FIELDS)
    ]

    def put(level, kept):
        for held_ref, ref, tiles in zip(held_refs[level], level_refs[level], kept):
            last = ref.shape[2] - LANES
            for t, value in enumerate(tiles):
                held = held_ref[t]
                edge = jnp.where(lane >= LANES - HALO, value, held[:, last - LANES : last])
                halo = jnp.where(own, held[:, last:], value)
                ref[t] = jnp.concatenate([held[:, : last - LANES], edge, halo], axis=1)

    way_down(*fields, [scale_ref[0, t] for t in range(count)], [scale_ref[1, t] for t in range(count)], put)


def descend(lat_count, own_ref, lat_near_ref, lat_far_ref, west_ref, west_near_ref, west_far_ref, west_edge_ref, scale_ref,
            pack_ref, edge_ref, grid_ref, plain_ref):
    rows = own_ref.shape[1]
    edge = slice(FIELDS * own_ref.shape[2], FIELDS * own_ref.shape[2] + LANES)
    edge_ref[pl.ds(0, rows), :] = west_edge_ref[...]
    edge_ref[pl.ds(rows, HALO), :] = lat_near_ref[:, edge]
    edge_ref[pl.ds(rows + HALO, HALO), :] = lat_far_ref[:, edge]
    lon_index = lax.axis_index("lon")
    cols = own_ref.shape[2]
    own_columns = cols // LANES
    columns = grid_ref.shape[1]
    depth, source_term, source, across, along = lay_out(
        lat_count, own_ref, lat_near_ref, lat_far_ref, west_ref, west_near_ref, west_far_ref, scale_ref, grid_ref
    )
    levels = all_coefficients(depth, source_term, across, along)
    sides = None
    for level, (faces, inverse, diagonal, source_term) in enumerate(levels):
        _, image = level_down(level, faces, inverse, diagonal, source, sides)
        if level < LEVELS - 1:
            source, sides = level_next(level, image)

    east_face, _, north_face = faces
    for f, values in enumerate((image, east_face, north_face, source_term)):
        for t, value in enumerate(values):
            for c in range(columns):
                plain_ref[f, c, pl.ds(t, TILE, stride=len(values)), :] = value[:, c * LANES : (c + 1) * LANES]
    stride = 1 << LEVELS
    bottom_rows = rows // stride
    bottom_width = cols // stride
    group = LANES // bottom_width
    per_column = LANES // stride
    lane = iota((bottom_rows, LANES), 1)
    cell = lane % bottom_width - SHIFT
    column = jnp.where(cell < 0, own_columns, cell // per_column)
    west_part = jnp.where(cell < 0, LANES + cell * stride, (cell % per_column) * stride)
    east_part = west_part + stride // 2
    turn = lax.rem(lane // bottom_width + group - lax.rem(lon_index, group), group)
    packed = jnp.zeros((bottom_rows, LANES), jnp.float32)
    for f, picks in enumerate(((west_part, east_part), (east_part,), (west_part, east_part), (west_part, east_part))):
        flat = jnp.zeros((bottom_rows, LANES), jnp.float32)
        for c in range(columns):
            value = plain_ref[f, c, pl.ds(1, bottom_rows, stride=2), :]
            if f != 2:
                value = value + plain_ref[f, c, pl.ds(0, bottom_rows, stride=2), :]
            taken = sum(jnp.take_along_axis(value, pick, axis=1) for pick in picks)
            flat = jnp.where(column == c, taken, flat)
        packed = jnp.where(turn == f, flat, packed)
    for k in range(pack_ref.shape[0]):
        pack_ref[k] = packed


def total_of(tiles):
    parts = list(tiles)
    while len(parts) > 1:
        parts = [
            parts[i] + parts[i + 1] if i + 1 < len(parts) else parts[i] for i in range(0, len(parts), 2)
        ]
    value = parts[0]
    value = sum(value[:, c : c + LANES] for c in range(0, value.shape[1], LANES))
    return jnp.sum(jnp.sum(value, axis=0, keepdims=True), axis=1, keepdims=True)


def conjugate(source, east_face, north_face, source_term):
    height = source.shape[0]

    def split(value):
        return [value[r : r + TILE] for r in range(0, height, TILE)]

    def up(value):
        return pltpu.roll(value, height - 1, 0)

    def down(value):
        return pltpu.roll(value, 1, 0)

    west_face = lane_shift(east_face, -1)
    south_face = down(north_face)
    diagonal = source_term + ((east_face + west_face) + (north_face + south_face))

    def apply(value):
        return diagonal * value - (
            (east_face * lane_shift(value, 1) + west_face * lane_shift(value, -1))
            + (north_face * up(value) + south_face * down(value))
        )

    iterate = jnp.zeros_like(source)
    remain = source
    image_r = apply(source)
    direction = image_d = second = None
    over_norm = over_step = None
    for step in range(BOTTOM_ITERS):
        norm = total_of(split(remain * remain))
        energy = total_of(split(remain * image_r))
        last = step == BOTTOM_ITERS - 1
        ahead = None if last else apply(image_r)
        if step == 0:
            direction, image_d, second = remain, image_r, ahead
        else:
            ratio = norm * over_norm
            energy = energy - ratio * (norm * over_step)
            direction = remain + ratio * direction
            if not last:
                image_d = image_r + ratio * image_d
                second = ahead + ratio * second
        step_size = norm / energy
        over_norm = 1.0 / norm
        over_step = energy * over_norm
        iterate = iterate + step_size * direction
        if not last:
            remain = remain - step_size * image_d
            image_r = image_r - step_size * second
    return iterate


def ascend(lat_count, lon_count, blocks_ref, *rest):
    level_refs = [rest[KEPT * i : KEPT * i + KEPT] for i in range(LEVELS)]
    diagonal_ref, solution_ref, residual_ref, window_ref, order_ref, sems = rest[KEPT * LEVELS :]
    lon_index = lax.axis_index("lon")
    lat_index = lax.axis_index("lat")
    rows, cols = solution_ref.shape
    count, width = diagonal_ref.shape[0], diagonal_ref.shape[2]
    own_columns = cols // LANES
    columns = width // LANES
    stride = 1 << LEVELS
    bottom_rows = rows // stride
    bottom_width = cols // stride
    group = LANES // bottom_width
    slot = iota((bottom_rows, LANES), 1) // bottom_width
    fields = []
    for f in range(4):
        strips = []
        for a in range(lat_count):
            pieces = []
            for c in range(lon_count // group):
                merged = None
                for j in range(group):
                    block = blocks_ref[a * lon_count + c * group + j]
                    merged = block if merged is None else jnp.where(slot == (f + j) % group, block, merged)
                pieces.append(lane_shift(merged, f * bottom_width))
            strips.append(jnp.concatenate(pieces, axis=1))
        fields.append(jnp.concatenate(strips, axis=0))
    iterate = conjugate(*fields)

    bottom_height = lat_count * bottom_rows
    whole_width = lon_count * bottom_width
    pad = 2 * TILE
    window_ref[pl.ds(0, pad), :] = jnp.zeros((pad, LANES), jnp.float32)
    window_ref[pl.ds(pad + bottom_height, pad), :] = jnp.zeros((pad, LANES), jnp.float32)
    half = LANES // 2
    margin = half // stride
    shift = lax.rem(margin - SHIFT - lon_index * bottom_width + whole_width, whole_width)
    window_ref[pl.ds(pad, bottom_height), :] = pltpu.roll(iterate, shift, 1)[:, :LANES]
    start = pl.multiple_of(lat_index * bottom_rows, TILE)
    tiles = count >> LEVELS
    lane = iota((TILE, LANES), 1)
    ahead = (rows + HALO) // stride // tiles
    sublane = iota((TILE, LANES), 0)
    step = 1 << (LEVELS - 1)
    center, plus, minus = [], [], []
    for t in range(tiles):
        upper = window_ref[pl.ds(start + pad + t, TILE, stride=tiles), :]
        lower = window_ref[pl.ds(start + pad + t - tiles * TILE, TILE, stride=tiles), :]
        value = jnp.where(sublane < ahead, upper, lower)
        for target, move in ((center, 0), (plus, step), (minus, -step)):
            parts = []
            for c in range(columns):
                place = c * LANES + lane + (move + width)
                place = jnp.where(place >= width, place - width, place)
                place = jnp.where(place >= width, place - width, place)
                pick = jnp.where(place < cols + half, margin + place // stride, (place - (cols + half)) // stride)
                parts.append(jnp.take_along_axis(value, pick, axis=1))
            target.append(jnp.concatenate(parts, axis=1))

    lane = iota((TILE, width), 1)
    for level in range(LEVELS - 1, -1, -1):
        stride = 1 << level
        east_face, west_face, north_face, inverse, source, swept = map(tiles_of, level_refs[level])
        faces = (east_face, west_face, north_face)
        if level < LEVELS - 1:
            first = lax.rem(lane // stride, 2) == 0
            east = [lane_shift(value, stride) for value in field]
            west = [lane_shift(value, -stride) for value in field]
            west_two = [lane_shift(value, -2 * stride) for value in field]
            coarse = range(len(field))
            center = [jnp.where(first, field[t], west[t]) for t in coarse]
            plus = [jnp.where(first, field[t], east[t]) for t in coarse]
            minus = [jnp.where(first, west_two[t], west[t]) for t in coarse]
        spread = [center[t // 2] for t in range(count >> level)]
        field = []
        for t in range(count >> level):
            around = (east_face[t] * plus[t // 2] + west_face[t] * minus[t // 2]) + (
                north_face[t] * north_of(spread, t) + south_of(north_face, t) * south_of(spread, t)
            )
            here = spread[t]
            if level == 0:
                here = jnp.where(east_face[t] + north_face[t] > 0.0, here, 0.0)
            field.append(swept[t] + ((1.0 - DAMPING) * here + inverse[t] * around))
        for _ in range(SWEEPS - 1):
            field = sweep(field, source, inverse, faces, stride)
    correction = field
    own_sublanes = rows // count

    def send_out(k, ref, tiles):
        copies = []
        for c in range(own_columns):
            part = slice(c * LANES, (c + 1) * LANES)
            for t in range(count):
                order_ref[k, c, pl.ds(t, own_sublanes, stride=count), :] = tiles[t][:own_sublanes, part]
            copies.append(pltpu.make_async_copy(order_ref.at[k, c], ref.at[:, part], sems.at[k, c]))
            copies[-1].start()
        return copies

    copies = send_out(0, solution_ref, correction)
    final = remainder(correction, source, tiles_of(diagonal_ref), faces, 1)
    copies += send_out(1, residual_ref, final)
    for copy in copies:
        copy.wait()


def near_pairs(lat_count):
    return [(a, a ^ 1) for a in range(lat_count)]


def far_pairs(lon_count, lat_count, east):
    pairs = []
    for i in range(lon_count):
        for a in range(lat_count):
            b = a + 1 if a % 2 else a - 1
            j = (i + east) % lon_count
            if b < 0 or b == lat_count:
                b, j = a, i ^ 1
            pairs.append((i * lat_count + a, j * lat_count + b))
    return pairs


def on_device(lat_count, lon_count, forcing, surface_term, sea_cells, levels):
    rows, cols = forcing.shape
    height, width = rows + 2 * HALO, cols + LANES
    count = height // TILE
    f32 = jnp.float32
    vmem = pl.BlockSpec(memory_space=pltpu.VMEM)
    hbm = pl.BlockSpec(memory_space=pltpu.HBM)
    params = pltpu.CompilerParams(vmem_limit_bytes=VMEM_LIMIT)
    lat_index = lax.axis_index("lat").astype(jnp.int32)
    inputs = [
        pltpu.with_memory_space_constraint(x, pltpu.HBM) for x in (forcing, surface_term, sea_cells, levels)
    ]
    own, east_edge, west_edge = pl.pallas_call(
        prepare,
        out_shape=[
            jax.ShapeDtypeStruct((FIELDS, rows, cols), f32),
            jax.ShapeDtypeStruct((rows, LANES), f32),
            jax.ShapeDtypeStruct((rows, LANES), f32),
        ],
        in_specs=[hbm] * 4,
        out_specs=[vmem] * 3,
        scratch_shapes=[
            pltpu.VMEM((rows, cols), f32),
            pltpu.VMEM((rows, cols), f32),
            pltpu.VMEM((rows, cols), jnp.int32),
            pltpu.VMEM((rows, cols), jnp.int32),
            pltpu.SemaphoreType.DMA((4,)),
        ],
        compiler_params=params,
        name="prepare",
    )(*inputs)

    lat_near, lat_far = pl.pallas_call(
        prepare_rows,
        out_shape=[jax.ShapeDtypeStruct((HALO, FIELDS * cols + LANES), f32)] * 2,
        in_specs=[vmem] * 2,
        out_specs=[vmem] * 2,
        compiler_params=params,
        name="prepare_rows",
    )(own, west_edge)

    diagonal_edge = pl.pallas_call(
        prepare_corner,
        out_shape=jax.ShapeDtypeStruct((HALO, LANES), f32),
        in_specs=[vmem] * 2,
        out_specs=vmem,
        compiler_params=params,
        name="prepare_corner",
    )(east_edge, lat_far)
    eastward = [(i, (i + 1) % lon_count) for i in range(lon_count)]
    westward = [(target, source) for source, target in eastward]
    west_halo = lax.ppermute(east_edge, "lon", eastward)
    lat_far = lax.ppermute(lat_far, ("lon", "lat"), far_pairs(lon_count, lat_count, 0))
    west_far = lax.ppermute(diagonal_edge, ("lon", "lat"), far_pairs(lon_count, lat_count, 1))
    lat_near = lax.ppermute(lat_near, "lat", near_pairs(lat_count))
    odd = lat_index % 2 == 1
    west_near = lax.ppermute(
        jnp.where(odd, west_halo[:HALO], west_halo[rows - HALO :]), "lat", near_pairs(lat_count)
    )

    def scales(halo):
        tall = rows + 2 * halo
        tiles = tall // TILE
        row = jnp.arange(TILE)[None, :] * tiles + jnp.arange(tiles)[:, None]
        row = jnp.where(row < rows + halo, row, row - tall).astype(f32) + (lat_index * rows).astype(f32)
        center, northern = metric(row)
        return jnp.broadcast_to(jnp.stack([1.0 / center, northern])[..., None], (2, tiles, TILE, LANES))

    devices = lat_count * lon_count
    grid = pltpu.VMEM((FIELDS, width // LANES, height, LANES), f32)
    packed, edges = pl.pallas_call(
        functools.partial(descend, lat_count),
        out_shape=[
            jax.ShapeDtypeStruct((devices, rows >> LEVELS, LANES), f32),
            jax.ShapeDtypeStruct((height, LANES), f32),
        ],
        in_specs=[vmem] * 8,
        out_specs=[vmem] * 2,
        scratch_shapes=[
            pltpu.VMEM((FIELDS, width // LANES, rows + 2 * REACH, LANES), f32),
            pltpu.VMEM((4, width // LANES, (rows + 2 * REACH) >> (LEVELS - 1), LANES), f32),
        ],
        compiler_params=params,
        name="descend",
    )(own, lat_near, lat_far, west_halo, west_near, west_far, west_edge, scales(REACH))
    east_halo = lax.ppermute(edges, "lon", westward)
    blocks = lax.all_to_all(packed, ("lat", "lon"), 0, 0, tiled=True)

    level_shapes = []
    for level in range(LEVELS):
        level_shapes += [jax.ShapeDtypeStruct((count >> level, TILE, width), f32)] * KEPT
    held_shapes = level_shapes + [jax.ShapeDtypeStruct((count, TILE, width), f32)]
    fine_scale = scales(HALO)
    held = pl.pallas_call(
        functools.partial(hold, lat_count),
        out_shape=held_shapes + [jax.ShapeDtypeStruct((FIELDS, count, TILE, LANES), f32)],
        in_specs=[vmem] * 7,
        out_specs=[vmem] * (1 + len(held_shapes)),
        scratch_shapes=[grid],
        compiler_params=params,
        name="hold",
    )(own, lat_near, lat_far, west_halo, west_near, west_far, fine_scale)
    held, raw = held[:-1], held[-1]
    held = pl.pallas_call(
        functools.partial(patch, lat_count),
        out_shape=held_shapes,
        in_specs=[vmem] * (3 + len(held_shapes)),
        out_specs=[vmem] * len(held_shapes),
        scratch_shapes=[pltpu.VMEM((FIELDS, height, LANES), f32)],
        compiler_params=params,
        name="patch",
    )(raw, east_halo, fine_scale, *held)

    return pl.pallas_call(
        functools.partial(ascend, lat_count, lon_count),
        out_shape=[jax.ShapeDtypeStruct((rows, cols), f32)] * 2,
        in_specs=[vmem] * (1 + len(held)),
        out_specs=[hbm] * 2,
        scratch_shapes=[
            pltpu.VMEM((lat_count * (rows >> LEVELS) + 4 * TILE, LANES), f32),
            pltpu.VMEM((2, cols // LANES, rows, LANES), f32),
            pltpu.SemaphoreType.DMA((2, cols // LANES)),
        ],
        compiler_params=params,
        name="ascend",
    )(blocks, *held)


def solution(mesh):
    body = functools.partial(on_device, mesh.shape["lat"], mesh.shape["lon"])
    return jax.shard_map(
        body,
        mesh=mesh,
        in_specs=(P("lat", "lon"),) * 4,
        out_specs=(P("lat", "lon"),) * 2,
        check_vma=False,
    )
```

```python
import functools

import jax
import jax.numpy as jnp
from jax import lax
from jax.experimental import pallas as pl
from jax.experimental.pallas import tpu as pltpu
from jax.sharding import PartitionSpec as P

LEVELS = 3
SWEEPS = 2
BOTTOM_ITERS = 6

DAMPING = 0.8
ROW_STEP = 150.0 / 8640.0
BAND_SOUTH = -50.0

HALO = 32
REACH = 16
LANES = 128
TILE = 8
FIELDS = 3
KEPT = 6
SHIFT = 2
VMEM_LIMIT = 8 * 1024 * 1024


def iota(shape, dim):
    return lax.broadcasted_iota(jnp.int32, shape, dim)


def lane_shift(field, count):
    return pltpu.roll(field, (-count) % field.shape[1], 1)


def north_of(tiles, t):
    if t + 1 < len(tiles):
        return tiles[t + 1]
    return pltpu.roll(tiles[0], TILE - 1, 0)


def south_of(tiles, t):
    if t > 0:
        return tiles[t - 1]
    return pltpu.roll(tiles[-1], 1, 0)


def neighbour_sum(field, faces, stride):
    east_face, west_face, north_face = faces
    upward = [north_face[t] * field[t] for t in range(len(field))]
    return [
        (east_face[t] * lane_shift(field[t], stride) + west_face[t] * lane_shift(field[t], -stride))
        + (north_face[t] * north_of(field, t) + south_of(upward, t))
        for t in range(len(field))
    ]


def sweep(field, source, inverse, faces, stride):
    around = neighbour_sum(field, faces, stride)
    return [
        (1.0 - DAMPING) * field[t] + inverse[t] * (source[t] + around[t]) for t in range(len(field))
    ]


def remainder(field, source, diagonal, faces, stride):
    around = neighbour_sum(field, faces, stride)
    return [source[t] - diagonal[t] * field[t] + around[t] for t in range(len(field))]


def tiles_of(ref):
    return [ref[t] for t in range(ref.shape[0])]


def keep(ref, tiles):
    for t, value in enumerate(tiles):
        ref[t] = value


def metric(row):
    center = jnp.cos(jnp.deg2rad(BAND_SOUTH + ROW_STEP * (row + 0.5)))
    northern = jnp.cos(jnp.deg2rad(BAND_SOUTH + ROW_STEP * (row + 1.0)))
    return center, northern


def prepare(forcing_ref, surface_ref, sea_ref, levels_ref,
            own_ref, east_edge_ref, west_edge_ref,
            forcing_buf, surface_buf, sea_buf, levels_buf, sems):
    copies = [
        pltpu.make_async_copy(source, target, sems.at[i])
        for i, (source, target) in enumerate((
            (levels_ref, levels_buf), (sea_ref, sea_buf), (surface_ref, surface_buf), (forcing_ref, forcing_buf),
        ))
    ]
    for copy in copies:
        copy.start()
    rows, cols = forcing_buf.shape
    first_row = lax.axis_index("lat") * rows
    row = (iota((rows, LANES), 0) + first_row).astype(jnp.float32)
    center = jnp.cos(jnp.deg2rad(BAND_SOUTH + ROW_STEP * (row + 0.5)))
    center = jnp.concatenate([center] * (cols // LANES), axis=1)
    for copy in copies:
        copy.wait()
    sea_mask = sea_buf[...].astype(jnp.float32)
    layers = levels_buf[...].astype(jnp.float32)
    depth = sea_mask * (layers * (0.00475 + 0.00025 * layers))
    fields = (depth, surface_buf[...] * center * sea_mask, forcing_buf[...] * sea_mask)
    slot = iota((rows, LANES), 1) // HALO
    slots = LANES // HALO
    west_edge = jnp.zeros((rows, LANES), jnp.float32)
    east_edge = jnp.zeros((rows, LANES), jnp.float32)
    for f, value in enumerate(fields):
        own_ref[f] = value
        west_edge = jnp.where(slot == f, lane_shift(value[:, :LANES], -f * HALO), west_edge)
        east_edge = jnp.where(
            slot == (f + slots - 1) % slots, lane_shift(value[:, cols - LANES :], -f * HALO), east_edge
        )
    east_edge_ref[...] = east_edge
    west_edge_ref[...] = west_edge


def prepare_corner(east_edge_ref, diagonal_edge_ref):
    rows = east_edge_ref.shape[0]
    odd = jnp.broadcast_to(lax.rem(lax.axis_index("lat"), 2), diagonal_edge_ref.shape) > 0
    diagonal_edge_ref[...] = jnp.where(odd, east_edge_ref[pl.ds(rows - HALO, HALO), :], east_edge_ref[pl.ds(0, HALO), :])


def prepare_rows(own_ref, west_edge_ref, lat_near_ref, lat_far_ref):
    rows, cols = own_ref.shape[1:]
    south, north = pl.ds(0, HALO), pl.ds(rows - HALO, HALO)
    odd = jnp.broadcast_to(lax.rem(lax.axis_index("lat"), 2), (HALO, cols)) > 0
    for f in range(FIELDS):
        south_edge, north_edge = own_ref[f, south, :], own_ref[f, north, :]
        part = slice(f * cols, (f + 1) * cols)
        lat_near_ref[:, part] = jnp.where(odd, south_edge, north_edge)
        lat_far_ref[:, part] = jnp.where(odd[:REACH], north_edge[HALO - REACH :], south_edge[:REACH])
    odd = odd[:, :LANES]
    south_edge, north_edge = west_edge_ref[south, :], west_edge_ref[north, :]
    edge = FIELDS * cols
    lat_near_ref[:, edge : edge + LANES] = jnp.where(odd, south_edge, north_edge)
    far_edge = jnp.where(odd, north_edge, south_edge)
    lat_far_ref[:, edge : edge + LANES] = far_edge[:REACH]
    lat_far_ref[:, edge + LANES :] = far_edge[REACH:]


def prepare_rest(own_ref, corner_ref, lat_rest_ref):
    rows, cols = own_ref.shape[1:]
    odd = jnp.broadcast_to(lax.rem(lax.axis_index("lat"), 2), (HALO - REACH, cols)) > 0
    for f in range(FIELDS):
        north_part = own_ref[f, pl.ds(rows - HALO, HALO - REACH), :]
        south_part = own_ref[f, pl.ds(REACH, HALO - REACH), :]
        lat_rest_ref[:, f * cols : (f + 1) * cols] = jnp.where(odd, north_part, south_part)


def fine_faces(depth, across, along):
    tiles = range(len(depth))
    east_face = [jnp.minimum(depth[t], lane_shift(depth[t], 1)) * across[t] for t in tiles]
    west_face = [jnp.minimum(depth[t], lane_shift(depth[t], -1)) * across[t] for t in tiles]
    north_face = [jnp.minimum(depth[t], north_of(depth, t)) * along[t] for t in tiles]
    return east_face, west_face, north_face


def coefficients(level, faces, source_term):
    east_face, west_face, north_face = faces
    diagonal = []
    for t in range(len(source_term)):
        total = source_term[t] + ((east_face[t] + west_face[t]) + (north_face[t] + south_of(north_face, t)))
        diagonal.append(jnp.where(source_term[t] > 0.0, total, 1.0))
    return faces, [DAMPING / value for value in diagonal], diagonal


def next_coefficients(level, faces, source_term):
    stride = 1 << level
    east_face, _, north_face = faces
    firsts = range(0, len(source_term), 2)
    east_sums = [east_face[t] + east_face[t + 1] for t in firsts]
    term_sums = [source_term[t] + source_term[t + 1] for t in firsts]
    east_next = [lane_shift(value, stride) for value in east_sums]
    west_next = [lane_shift(value, -stride) for value in east_sums]
    north_next = [north_face[t + 1] + lane_shift(north_face[t + 1], stride) for t in firsts]
    return (east_next, west_next, north_next), [value + lane_shift(value, stride) for value in term_sums]


def all_coefficients(depth, source_term, across, along):
    faces = fine_faces(depth, across, along)
    levels = []
    for level in range(LEVELS):
        levels.append(coefficients(level, faces, source_term) + (source_term,))
        if level < LEVELS - 1:
            faces, source_term = next_coefficients(level, faces, source_term)
    return levels


def level_down(level, faces, inverse, diagonal, source, sides):
    stride = 1 << level
    count = len(source)
    field = [inverse[t] * source[t] for t in range(count)]
    for k in range(SWEEPS - 1):
        if k == 0 and sides is not None:
            east_face, west_face, north_face = faces
            plus, minus = sides
            upward = [north_face[t] * field[t] for t in range(count)]
            around = [
                (
                    east_face[t] * (lane_shift(inverse[t], stride) * plus[t])
                    + west_face[t] * (lane_shift(inverse[t], -stride) * minus[t])
                )
                + (north_face[t] * north_of(field, t) + south_of(upward, t))
                for t in range(count)
            ]
            field = [(1.0 - DAMPING) * field[t] + inverse[t] * (source[t] + around[t]) for t in range(count)]
        else:
            field = sweep(field, source, inverse, faces, stride)
    return field, remainder(field, source, diagonal, faces, stride)


def level_next(level, image):
    stride = 1 << level
    left = [image[t] + image[t + 1] for t in range(0, len(image), 2)]
    source = [value + lane_shift(value, stride) for value in left]
    if left[0].shape[1] > LANES:
        return source, None
    plus = [lane_shift(value, 2 * stride) + lane_shift(value, 3 * stride) for value in left]
    minus = [lane_shift(value, -2 * stride) + lane_shift(value, -stride) for value in left]
    return source, (plus, minus)


def lay_out(lat_count, own_ref, lat_near_ref, lat_far_ref, lat_rest_ref, west_ref, west_near_ref, west_far_ref, scale_ref, grid_ref):
    rows, cols = own_ref.shape[1], own_ref.shape[2]
    columns, height = grid_ref.shape[1], grid_ref.shape[2]
    count = height // TILE
    own_columns = cols // LANES
    halo = (height - rows) // 2
    lat_index = lax.axis_index("lat")
    lat_odd = lax.rem(lat_index, 2)
    near_row = rows + pl.multiple_of(lat_odd * halo, TILE)
    far_row = rows + pl.multiple_of((1 - lat_odd) * halo, TILE)
    near_part = pl.ds(pl.multiple_of(lat_odd * (HALO - halo), TILE), halo)
    far_part = pl.ds(pl.multiple_of((1 - lat_odd) * (HALO - halo), TILE), halo)
    last = LANES // HALO - 1
    at_end = (lat_index == 0) | (lat_index == lat_count - 1)

    def inside(value, far):
        return jnp.where(jnp.broadcast_to(at_end, value.shape), 0.0, value) if far else value

    parts = (
        (0, rows, None, west_ref[...], False),
        (near_row, halo, lat_near_ref.at[near_part], west_near_ref[near_part, :], False),
        (far_row, halo, lat_far_ref, west_far_ref[far_part, :], True),
    )
    for first, size, body_ref, west, far in parts:
        slot = iota((size, LANES), 1) // HALO
        for f in range(FIELDS):
            for c in range(own_columns):
                part = slice(f * cols + c * LANES, f * cols + (c + 1) * LANES)
                if far and halo > REACH:
                    seam = far_row + pl.multiple_of((1 - lat_odd) * (halo - REACH), TILE)
                    rest = far_row + pl.multiple_of(lat_odd * REACH, TILE)
                    grid_ref[f, c, pl.ds(seam, REACH), :] = inside(lat_far_ref[:, part], far)
                    grid_ref[f, c, pl.ds(rest, halo - REACH), :] = inside(lat_rest_ref[:, part], far)
                    continue
                if body_ref is None:
                    value = own_ref[f, :, c * LANES : (c + 1) * LANES]
                else:
                    value = body_ref[:, part]
                grid_ref[f, c, pl.ds(first, size), :] = inside(value, far)
            side = jnp.where(slot == (f + last) % (last + 1), west, 0.0)
            grid_ref[f, own_columns, pl.ds(first, size), :] = inside(lane_shift(side, f * HALO), far)

    def load(f):
        return [
            jnp.concatenate(
                [grid_ref[f, c, pl.ds(t, TILE, stride=count), :] for c in range(columns)], axis=1
            )
            for t in range(count)
        ]

    depth, source_term, source = load(0), load(1), load(2)
    across = [jnp.concatenate([scale_ref[0, t]] * columns, axis=1) for t in range(count)]
    along = [jnp.concatenate([scale_ref[1, t]] * columns, axis=1) for t in range(count)]
    return depth, source_term, source, across, along


def way_down(depth, source_term, source, across, along, put):
    levels = all_coefficients(depth, source_term, across, along)
    sides = None
    for level, (faces, inverse, diagonal, _) in enumerate(levels):
        field, image = level_down(level, faces, inverse, diagonal, source, sides)
        swept = sweep(field, source, inverse, faces, 1 << level)
        put(level, faces + (inverse, source, swept) + ((diagonal,) if level == 0 else ()))
        if level < LEVELS - 1:
            source, sides = level_next(level, image)


def split_refs(rest):
    level_refs = [list(rest[KEPT * i : KEPT * i + KEPT]) for i in range(LEVELS)]
    level_refs[0].append(rest[KEPT * LEVELS])
    return level_refs, rest[KEPT * LEVELS + 1 :]


def hold(lat_count, own_ref, lat_near_ref, lat_far_ref, lat_rest_ref, west_ref, west_near_ref, west_far_ref, scale_ref, *rest):
    level_refs, (raw_ref, grid_ref) = split_refs(rest)
    values = lay_out(lat_count, own_ref, lat_near_ref, lat_far_ref, lat_rest_ref, west_ref, west_near_ref, west_far_ref, scale_ref, grid_ref)
    cols = own_ref.shape[2]
    for f in range(FIELDS):
        for t, value in enumerate(values[f]):
            raw_ref[f, t] = value[:, cols - LANES : cols]

    def put(level, kept):
        for ref, tiles in zip(level_refs[level], kept):
            keep(ref, tiles)

    way_down(*values, put)


def patch(lat_count, raw_ref, east_ref, scale_ref, *rest):
    half = len(rest) // 2
    held_refs, _ = split_refs(rest[:half])
    level_refs, (strip_ref,) = split_refs(rest[half:])
    count = raw_ref.shape[1]
    height = count * TILE
    rows = height - 2 * HALO
    lat_index = lax.axis_index("lat")
    lat_odd = lax.rem(lat_index, 2)
    near_row = rows + pl.multiple_of(lat_odd * HALO, HALO)
    far_row = rows + pl.multiple_of((1 - lat_odd) * HALO, HALO)
    at_end = (lat_index == 0) | (lat_index == lat_count - 1)
    for first, at, size, far in ((0, 0, rows, False), (near_row, rows, HALO, False), (far_row, rows + HALO, HALO, True)):
        side = east_ref[pl.ds(at, size), :]
        if far:
            side = jnp.where(jnp.broadcast_to(at_end, side.shape), 0.0, side)
        for f in range(FIELDS):
            strip_ref[f, pl.ds(first, size), :] = lane_shift(side, f * HALO)
    lane = iota((TILE, LANES), 1)
    own = lane >= LANES // 2
    fields = [
        [
            jnp.where(own, raw_ref[f, t],
                      jnp.where(lane < HALO, strip_ref[f, pl.ds(t, TILE, stride=count), :], 0.0))
            for t in range(count)
        ]
        for f in range(FIELDS)
    ]

    def put(level, kept):
        for held_ref, ref, tiles in zip(held_refs[level], level_refs[level], kept):
            last = ref.shape[2] - LANES
            for t, value in enumerate(tiles):
                held = held_ref[t]
                edge = jnp.where(lane >= LANES - HALO, value, held[:, last - LANES : last])
                halo = jnp.where(own, held[:, last:], value)
                ref[t] = jnp.concatenate([held[:, : last - LANES], edge, halo], axis=1)

    way_down(*fields, [scale_ref[0, t] for t in range(count)], [scale_ref[1, t] for t in range(count)], put)


def descend(lat_count, own_ref, lat_near_ref, lat_far_ref, west_ref, west_near_ref, west_far_ref, west_edge_ref, scale_ref,
            pack_ref, edge_ref, grid_ref, plain_ref):
    rows = own_ref.shape[1]
    edge = slice(FIELDS * own_ref.shape[2], FIELDS * own_ref.shape[2] + LANES)
    edge_ref[pl.ds(0, rows), :] = west_edge_ref[...]
    edge_ref[pl.ds(rows, HALO), :] = lat_near_ref[:, edge]
    edge_ref[pl.ds(rows + HALO, REACH), :] = lat_far_ref[:, edge]
    edge_ref[pl.ds(rows + HALO + REACH, HALO - REACH), :] = lat_far_ref[:, edge.stop :]
    lon_index = lax.axis_index("lon")
    cols = own_ref.shape[2]
    own_columns = cols // LANES
    columns = grid_ref.shape[1]
    depth, source_term, source, across, along = lay_out(
        lat_count, own_ref, lat_near_ref, lat_far_ref, None, west_ref, west_near_ref, west_far_ref, scale_ref, grid_ref
    )
    levels = all_coefficients(depth, source_term, across, along)
    sides = None
    for level, (faces, inverse, diagonal, source_term) in enumerate(levels):
        _, image = level_down(level, faces, inverse, diagonal, source, sides)
        if level < LEVELS - 1:
            source, sides = level_next(level, image)

    east_face, _, north_face = faces
    for f, values in enumerate((image, east_face, north_face, source_term)):
        for t, value in enumerate(values):
            for c in range(columns):
                plain_ref[f, c, pl.ds(t, TILE, stride=len(values)), :] = value[:, c * LANES : (c + 1) * LANES]
    stride = 1 << LEVELS
    bottom_rows = rows // stride
    bottom_width = cols // stride
    group = LANES // bottom_width
    per_column = LANES // stride
    lane = iota((bottom_rows, LANES), 1)
    cell = lane % bottom_width - SHIFT
    column = jnp.where(cell < 0, own_columns, cell // per_column)
    west_part = jnp.where(cell < 0, LANES + cell * stride, (cell % per_column) * stride)
    east_part = west_part + stride // 2
    turn = lax.rem(lane // bottom_width + group - lax.rem(lon_index, group), group)
    packed = jnp.zeros((bottom_rows, LANES), jnp.float32)
    for f, picks in enumerate(((west_part, east_part), (east_part,), (west_part, east_part), (west_part, east_part))):
        flat = jnp.zeros((bottom_rows, LANES), jnp.float32)
        for c in range(columns):
            value = plain_ref[f, c, pl.ds(1, bottom_rows, stride=2), :]
            if f != 2:
                value = value + plain_ref[f, c, pl.ds(0, bottom_rows, stride=2), :]
            taken = sum(jnp.take_along_axis(value, pick, axis=1) for pick in picks)
            flat = jnp.where(column == c, taken, flat)
        packed = jnp.where(turn == f, flat, packed)
    for k in range(pack_ref.shape[0]):
        pack_ref[k] = packed


def total_of(tiles):
    parts = list(tiles)
    while len(parts) > 1:
        parts = [
            parts[i] + parts[i + 1] if i + 1 < len(parts) else parts[i] for i in range(0, len(parts), 2)
        ]
    value = parts[0]
    value = sum(value[:, c : c + LANES] for c in range(0, value.shape[1], LANES))
    return jnp.sum(jnp.sum(value, axis=0, keepdims=True), axis=1, keepdims=True)


def conjugate(source, east_face, north_face, source_term):
    height = source.shape[0]

    def split(value):
        return [value[r : r + TILE] for r in range(0, height, TILE)]

    def up(value):
        return pltpu.roll(value, height - 1, 0)

    def down(value):
        return pltpu.roll(value, 1, 0)

    west_face = lane_shift(east_face, -1)
    south_face = down(north_face)
    diagonal = source_term + ((east_face + west_face) + (north_face + south_face))

    def apply(value):
        return diagonal * value - (
            (east_face * lane_shift(value, 1) + west_face * lane_shift(value, -1))
            + (north_face * up(value) + south_face * down(value))
        )

    iterate = jnp.zeros_like(source)
    remain = source
    image_r = apply(source)
    direction = image_d = second = None
    over_norm = over_step = None
    for step in range(BOTTOM_ITERS):
        norm = total_of(split(remain * remain))
        energy = total_of(split(remain * image_r))
        last = step == BOTTOM_ITERS - 1
        ahead = None if last else apply(image_r)
        if step == 0:
            direction, image_d, second = remain, image_r, ahead
        else:
            ratio = norm * over_norm
            energy = energy - ratio * (norm * over_step)
            direction = remain + ratio * direction
            if not last:
                image_d = image_r + ratio * image_d
                second = ahead + ratio * second
        step_size = norm / energy
        over_norm = 1.0 / norm
        over_step = energy * over_norm
        iterate = iterate + step_size * direction
        if not last:
            remain = remain - step_size * image_d
            image_r = image_r - step_size * second
    return iterate


def ascend(lat_count, lon_count, blocks_ref, *rest):
    level_refs = [rest[KEPT * i : KEPT * i + KEPT] for i in range(LEVELS)]
    diagonal_ref, solution_ref, residual_ref, window_ref, order_ref, sems = rest[KEPT * LEVELS :]
    lon_index = lax.axis_index("lon")
    lat_index = lax.axis_index("lat")
    rows, cols = solution_ref.shape
    count, width = diagonal_ref.shape[0], diagonal_ref.shape[2]
    own_columns = cols // LANES
    columns = width // LANES
    stride = 1 << LEVELS
    bottom_rows = rows // stride
    bottom_width = cols // stride
    group = LANES // bottom_width
    slot = iota((bottom_rows, LANES), 1) // bottom_width
    fields = []
    for f in range(4):
        strips = []
        for a in range(lat_count):
            pieces = []
            for c in range(lon_count // group):
                merged = None
                for j in range(group):
                    block = blocks_ref[a * lon_count + c * group + j]
                    merged = block if merged is None else jnp.where(slot == (f + j) % group, block, merged)
                pieces.append(lane_shift(merged, f * bottom_width))
            strips.append(jnp.concatenate(pieces, axis=1))
        fields.append(jnp.concatenate(strips, axis=0))
    iterate = conjugate(*fields)

    bottom_height = lat_count * bottom_rows
    whole_width = lon_count * bottom_width
    pad = 2 * TILE
    window_ref[pl.ds(0, pad), :] = jnp.zeros((pad, LANES), jnp.float32)
    window_ref[pl.ds(pad + bottom_height, pad), :] = jnp.zeros((pad, LANES), jnp.float32)
    half = LANES // 2
    margin = half // stride
    shift = lax.rem(margin - SHIFT - lon_index * bottom_width + whole_width, whole_width)
    window_ref[pl.ds(pad, bottom_height), :] = pltpu.roll(iterate, shift, 1)[:, :LANES]
    start = pl.multiple_of(lat_index * bottom_rows, TILE)
    tiles = count >> LEVELS
    lane = iota((TILE, LANES), 1)
    ahead = (rows + HALO) // stride // tiles
    sublane = iota((TILE, LANES), 0)
    step = 1 << (LEVELS - 1)
    center, plus, minus = [], [], []
    for t in range(tiles):
        upper = window_ref[pl.ds(start + pad + t, TILE, stride=tiles), :]
        lower = window_ref[pl.ds(start + pad + t - tiles * TILE, TILE, stride=tiles), :]
        value = jnp.where(sublane < ahead, upper, lower)
        for target, move in ((center, 0), (plus, step), (minus, -step)):
            parts = []
            for c in range(columns):
                place = c * LANES + lane + (move + width)
                place = jnp.where(place >= width, place - width, place)
                place = jnp.where(place >= width, place - width, place)
                pick = jnp.where(place < cols + half, margin + place // stride, (place - (cols + half)) // stride)
                parts.append(jnp.take_along_axis(value, pick, axis=1))
            target.append(jnp.concatenate(parts, axis=1))

    lane = iota((TILE, width), 1)
    for level in range(LEVELS - 1, -1, -1):
        stride = 1 << level
        east_face, west_face, north_face, inverse, source, swept = map(tiles_of, level_refs[level])
        faces = (east_face, west_face, north_face)
        if level < LEVELS - 1:
            first = lax.rem(lane // stride, 2) == 0
            east = [lane_shift(value, stride) for value in field]
            west = [lane_shift(value, -stride) for value in field]
            west_two = [lane_shift(value, -2 * stride) for value in field]
            coarse = range(len(field))
            center = [jnp.where(first, field[t], west[t]) for t in coarse]
            plus = [jnp.where(first, field[t], east[t]) for t in coarse]
            minus = [jnp.where(first, west_two[t], west[t]) for t in coarse]
        spread = [center[t // 2] for t in range(count >> level)]
        field = []
        for t in range(count >> level):
            around = (east_face[t] * plus[t // 2] + west_face[t] * minus[t // 2]) + (
                north_face[t] * north_of(spread, t) + south_of(north_face, t) * south_of(spread, t)
            )
            here = spread[t]
            if level == 0:
                here = jnp.where(east_face[t] + north_face[t] > 0.0, here, 0.0)
            field.append(swept[t] + ((1.0 - DAMPING) * here + inverse[t] * around))
        for _ in range(SWEEPS - 1):
            field = sweep(field, source, inverse, faces, stride)
    correction = field
    own_sublanes = rows // count

    def send_out(k, ref, tiles):
        copies = []
        for c in range(own_columns):
            part = slice(c * LANES, (c + 1) * LANES)
            for t in range(count):
                order_ref[k, c, pl.ds(t, own_sublanes, stride=count), :] = tiles[t][:own_sublanes, part]
            copies.append(pltpu.make_async_copy(order_ref.at[k, c], ref.at[:, part], sems.at[k, c]))
            copies[-1].start()
        return copies

    copies = send_out(0, solution_ref, correction)
    final = remainder(correction, source, tiles_of(diagonal_ref), faces, 1)
    copies += send_out(1, residual_ref, final)
    for copy in copies:
        copy.wait()


def near_pairs(lat_count):
    return [(a, a ^ 1) for a in range(lat_count)]


def far_pairs(lon_count, lat_count, east):
    pairs = []
    for i in range(lon_count):
        for a in range(lat_count):
            b = a + 1 if a % 2 else a - 1
            j = (i + east) % lon_count
            if b < 0 or b == lat_count:
                b, j = a, i ^ 1
            pairs.append((i * lat_count + a, j * lat_count + b))
    return pairs


def on_device(lat_count, lon_count, forcing, surface_term, sea_cells, levels):
    rows, cols = forcing.shape
    height, width = rows + 2 * HALO, cols + LANES
    count = height // TILE
    f32 = jnp.float32
    vmem = pl.BlockSpec(memory_space=pltpu.VMEM)
    hbm = pl.BlockSpec(memory_space=pltpu.HBM)
    params = pltpu.CompilerParams(vmem_limit_bytes=VMEM_LIMIT)
    lat_index = lax.axis_index("lat").astype(jnp.int32)
    inputs = [
        pltpu.with_memory_space_constraint(x, pltpu.HBM) for x in (forcing, surface_term, sea_cells, levels)
    ]
    own, east_edge, west_edge = pl.pallas_call(
        prepare,
        out_shape=[
            jax.ShapeDtypeStruct((FIELDS, rows, cols), f32),
            jax.ShapeDtypeStruct((rows, LANES), f32),
            jax.ShapeDtypeStruct((rows, LANES), f32),
        ],
        in_specs=[hbm] * 4,
        out_specs=[vmem] * 3,
        scratch_shapes=[
            pltpu.VMEM((rows, cols), f32),
            pltpu.VMEM((rows, cols), f32),
            pltpu.VMEM((rows, cols), jnp.int32),
            pltpu.VMEM((rows, cols), jnp.int32),
            pltpu.SemaphoreType.DMA((4,)),
        ],
        compiler_params=params,
        name="prepare",
    )(*inputs)

    lat_near, lat_far = pl.pallas_call(
        prepare_rows,
        out_shape=[
            jax.ShapeDtypeStruct((HALO, FIELDS * cols + LANES), f32),
            jax.ShapeDtypeStruct((REACH, FIELDS * cols + 2 * LANES), f32),
        ],
        in_specs=[vmem] * 2,
        out_specs=[vmem] * 2,
        compiler_params=params,
        name="prepare_rows",
    )(own, west_edge)

    diagonal_edge = pl.pallas_call(
        prepare_corner,
        out_shape=jax.ShapeDtypeStruct((HALO, LANES), f32),
        in_specs=[vmem],
        out_specs=vmem,
        compiler_params=params,
        name="prepare_corner",
    )(east_edge)
    lat_rest = pl.pallas_call(
        prepare_rest,
        out_shape=jax.ShapeDtypeStruct((HALO - REACH, FIELDS * cols), f32),
        in_specs=[vmem] * 2,
        out_specs=vmem,
        compiler_params=params,
        name="prepare_rest",
    )(own, diagonal_edge)

    eastward = [(i, (i + 1) % lon_count) for i in range(lon_count)]
    westward = [(target, source) for source, target in eastward]
    west_halo = lax.ppermute(east_edge, "lon", eastward)
    lat_far = lax.ppermute(lat_far, ("lon", "lat"), far_pairs(lon_count, lat_count, 0))
    west_far = lax.ppermute(diagonal_edge, ("lon", "lat"), far_pairs(lon_count, lat_count, 1))
    lat_near = lax.ppermute(lat_near, "lat", near_pairs(lat_count))
    lat_rest, west_halo = lax.optimization_barrier((lat_rest, west_halo))
    lat_rest = lax.ppermute(lat_rest, ("lon", "lat"), far_pairs(lon_count, lat_count, 0))
    odd = lat_index % 2 == 1
    west_near = lax.ppermute(
        jnp.where(odd, west_halo[:HALO], west_halo[rows - HALO :]), "lat", near_pairs(lat_count)
    )

    def scales(halo):
        tall = rows + 2 * halo
        tiles = tall // TILE
        row = jnp.arange(TILE)[None, :] * tiles + jnp.arange(tiles)[:, None]
        row = jnp.where(row < rows + halo, row, row - tall).astype(f32) + (lat_index * rows).astype(f32)
        center, northern = metric(row)
        return jnp.broadcast_to(jnp.stack([1.0 / center, northern])[..., None], (2, tiles, TILE, LANES))

    devices = lat_count * lon_count
    grid = pltpu.VMEM((FIELDS, width // LANES, height, LANES), f32)
    packed, edges = pl.pallas_call(
        functools.partial(descend, lat_count),
        out_shape=[
            jax.ShapeDtypeStruct((devices, rows >> LEVELS, LANES), f32),
            jax.ShapeDtypeStruct((height, LANES), f32),
        ],
        in_specs=[vmem] * 8,
        out_specs=[vmem] * 2,
        scratch_shapes=[
            pltpu.VMEM((FIELDS, width // LANES, rows + 2 * REACH, LANES), f32),
            pltpu.VMEM((4, width // LANES, (rows + 2 * REACH) >> (LEVELS - 1), LANES), f32),
        ],
        compiler_params=params,
        name="descend",
    )(own, lat_near, lat_far, west_halo, west_near, west_far, west_edge, scales(REACH))
    east_halo = lax.ppermute(edges, "lon", westward)
    packed, lat_rest = lax.optimization_barrier((packed, lat_rest))
    blocks = lax.all_to_all(packed, ("lat", "lon"), 0, 0, tiled=True)

    level_shapes = []
    for level in range(LEVELS):
        level_shapes += [jax.ShapeDtypeStruct((count >> level, TILE, width), f32)] * KEPT
    held_shapes = level_shapes + [jax.ShapeDtypeStruct((count, TILE, width), f32)]
    fine_scale = scales(HALO)
    held = pl.pallas_call(
        functools.partial(hold, lat_count),
        out_shape=held_shapes + [jax.ShapeDtypeStruct((FIELDS, count, TILE, LANES), f32)],
        in_specs=[vmem] * 8,
        out_specs=[vmem] * (1 + len(held_shapes)),
        scratch_shapes=[grid],
        compiler_params=params,
        cost_estimate=pl.CostEstimate(flops=0, bytes_accessed=60 * 1024 * 1024, transcendentals=0),
        name="hold",
    )(own, lat_near, lat_far, lat_rest, west_halo, west_near, west_far, fine_scale)
    held, raw = held[:-1], held[-1]
    held = pl.pallas_call(
        functools.partial(patch, lat_count),
        out_shape=held_shapes,
        in_specs=[vmem] * (3 + len(held_shapes)),
        out_specs=[vmem] * len(held_shapes),
        scratch_shapes=[pltpu.VMEM((FIELDS, height, LANES), f32)],
        compiler_params=params,
        name="patch",
    )(raw, east_halo, fine_scale, *held)

    return pl.pallas_call(
        functools.partial(ascend, lat_count, lon_count),
        out_shape=[jax.ShapeDtypeStruct((rows, cols), f32)] * 2,
        in_specs=[vmem] * (1 + len(held)),
        out_specs=[hbm] * 2,
        scratch_shapes=[
            pltpu.VMEM((lat_count * (rows >> LEVELS) + 4 * TILE, LANES), f32),
            pltpu.VMEM((2, cols // LANES, rows, LANES), f32),
            pltpu.SemaphoreType.DMA((2, cols // LANES)),
        ],
        compiler_params=params,
        name="ascend",
    )(blocks, *held)


def solution(mesh):
    body = functools.partial(on_device, mesh.shape["lat"], mesh.shape["lon"])
    return jax.shard_map(
        body,
        mesh=mesh,
        in_specs=(P("lat", "lon"),) * 4,
        out_specs=(P("lat", "lon"),) * 2,
        check_vma=False,
    )
```

```python
import functools

import jax
import jax.numpy as jnp
from jax import lax
from jax.experimental import pallas as pl
from jax.experimental.pallas import tpu as pltpu
from jax.sharding import PartitionSpec as P

LEVELS = 3
SWEEPS = 2
BOTTOM_ITERS = 6

DAMPING = 0.8
ROW_STEP = 150.0 / 8640.0
BAND_SOUTH = -50.0

HALO = 32
REACH = 16
LANES = 128
TILE = 8
FIELDS = 3
KEPT = 6
SHIFT = 2
VMEM_LIMIT = 8 * 1024 * 1024


def iota(shape, dim):
    return lax.broadcasted_iota(jnp.int32, shape, dim)


def lane_shift(field, count):
    return pltpu.roll(field, (-count) % field.shape[1], 1)


def north_of(tiles, t):
    if t + 1 < len(tiles):
        return tiles[t + 1]
    return pltpu.roll(tiles[0], TILE - 1, 0)


def south_of(tiles, t):
    if t > 0:
        return tiles[t - 1]
    return pltpu.roll(tiles[-1], 1, 0)


def neighbour_sum(field, faces, stride):
    east_face, west_face, north_face = faces
    upward = [north_face[t] * field[t] for t in range(len(field))]
    return [
        (east_face[t] * lane_shift(field[t], stride) + west_face[t] * lane_shift(field[t], -stride))
        + (north_face[t] * north_of(field, t) + south_of(upward, t))
        for t in range(len(field))
    ]


def sweep(field, source, inverse, faces, stride):
    around = neighbour_sum(field, faces, stride)
    return [
        (1.0 - DAMPING) * field[t] + inverse[t] * (source[t] + around[t]) for t in range(len(field))
    ]


def remainder(field, source, diagonal, faces, stride):
    around = neighbour_sum(field, faces, stride)
    return [source[t] - diagonal[t] * field[t] + around[t] for t in range(len(field))]


def tiles_of(ref):
    return [ref[t] for t in range(ref.shape[0])]


def keep(ref, tiles):
    for t, value in enumerate(tiles):
        ref[t] = value


def metric(row):
    center = jnp.cos(jnp.deg2rad(BAND_SOUTH + ROW_STEP * (row + 0.5)))
    northern = jnp.cos(jnp.deg2rad(BAND_SOUTH + ROW_STEP * (row + 1.0)))
    return center, northern


def prepare(forcing_ref, surface_ref, sea_ref, levels_ref,
            own_ref, east_edge_ref, west_edge_ref,
            forcing_buf, surface_buf, sea_buf, levels_buf, sems):
    copies = [
        pltpu.make_async_copy(source, target, sems.at[i])
        for i, (source, target) in enumerate((
            (levels_ref, levels_buf), (sea_ref, sea_buf), (surface_ref, surface_buf), (forcing_ref, forcing_buf),
        ))
    ]
    for copy in copies:
        copy.start()
    rows, cols = forcing_buf.shape
    first_row = lax.axis_index("lat") * rows
    row = (iota((rows, LANES), 0) + first_row).astype(jnp.float32)
    center = jnp.cos(jnp.deg2rad(BAND_SOUTH + ROW_STEP * (row + 0.5)))
    center = jnp.concatenate([center] * (cols // LANES), axis=1)
    for copy in copies:
        copy.wait()
    sea_mask = sea_buf[...].astype(jnp.float32)
    layers = levels_buf[...].astype(jnp.float32)
    depth = sea_mask * (layers * (0.00475 + 0.00025 * layers))
    fields = (depth, surface_buf[...] * center * sea_mask, forcing_buf[...] * sea_mask)
    slot = iota((rows, LANES), 1) // HALO
    slots = LANES // HALO
    west_edge = jnp.zeros((rows, LANES), jnp.float32)
    east_edge = jnp.zeros((rows, LANES), jnp.float32)
    for f, value in enumerate(fields):
        own_ref[f] = value
        west_edge = jnp.where(slot == f, lane_shift(value[:, :LANES], -f * HALO), west_edge)
        east_edge = jnp.where(
            slot == (f + slots - 1) % slots, lane_shift(value[:, cols - LANES :], -f * HALO), east_edge
        )
    east_edge_ref[...] = east_edge
    west_edge_ref[...] = west_edge


def prepare_corner(east_edge_ref, diagonal_edge_ref):
    rows = east_edge_ref.shape[0]
    odd = jnp.broadcast_to(lax.rem(lax.axis_index("lat"), 2), diagonal_edge_ref.shape) > 0
    diagonal_edge_ref[...] = jnp.where(odd, east_edge_ref[pl.ds(rows - HALO, HALO), :], east_edge_ref[pl.ds(0, HALO), :])


def prepare_rows(own_ref, west_edge_ref, lat_near_ref, lat_far_ref):
    rows, cols = own_ref.shape[1:]
    south, north = pl.ds(0, HALO), pl.ds(rows - HALO, HALO)
    odd = jnp.broadcast_to(lax.rem(lax.axis_index("lat"), 2), (HALO, cols)) > 0
    for f in range(FIELDS):
        south_edge, north_edge = own_ref[f, south, :], own_ref[f, north, :]
        part = slice(f * cols, (f + 1) * cols)
        lat_near_ref[:, part] = jnp.where(odd, south_edge, north_edge)
        lat_far_ref[:, part] = jnp.where(odd[:REACH], north_edge[HALO - REACH :], south_edge[:REACH])
    odd = odd[:, :LANES]
    south_edge, north_edge = west_edge_ref[south, :], west_edge_ref[north, :]
    edge = FIELDS * cols
    lat_near_ref[:, edge : edge + LANES] = jnp.where(odd, south_edge, north_edge)
    far_edge = jnp.where(odd, north_edge, south_edge)
    lat_far_ref[:, edge : edge + LANES] = far_edge[:REACH]
    lat_far_ref[:, edge + LANES :] = far_edge[REACH:]


def prepare_rest(own_ref, corner_ref, lat_rest_ref):
    rows, cols = own_ref.shape[1:]
    odd = jnp.broadcast_to(lax.rem(lax.axis_index("lat"), 2), (HALO - REACH, cols)) > 0
    for f in range(FIELDS):
        north_part = own_ref[f, pl.ds(rows - HALO, HALO - REACH), :]
        south_part = own_ref[f, pl.ds(REACH, HALO - REACH), :]
        lat_rest_ref[:, f * cols : (f + 1) * cols] = jnp.where(odd, north_part, south_part)


def fine_faces(depth, across, along):
    tiles = range(len(depth))
    east_face = [jnp.minimum(depth[t], lane_shift(depth[t], 1)) * across[t] for t in tiles]
    west_face = [jnp.minimum(depth[t], lane_shift(depth[t], -1)) * across[t] for t in tiles]
    north_face = [jnp.minimum(depth[t], north_of(depth, t)) * along[t] for t in tiles]
    return east_face, west_face, north_face


def coefficients(level, faces, source_term):
    east_face, west_face, north_face = faces
    diagonal = []
    for t in range(len(source_term)):
        total = source_term[t] + ((east_face[t] + west_face[t]) + (north_face[t] + south_of(north_face, t)))
        diagonal.append(jnp.where(source_term[t] > 0.0, total, 1.0))
    return faces, [DAMPING / value for value in diagonal], diagonal


def next_coefficients(level, faces, source_term):
    stride = 1 << level
    east_face, _, north_face = faces
    firsts = range(0, len(source_term), 2)
    east_sums = [east_face[t] + east_face[t + 1] for t in firsts]
    term_sums = [source_term[t] + source_term[t + 1] for t in firsts]
    east_next = [lane_shift(value, stride) for value in east_sums]
    west_next = [lane_shift(value, -stride) for value in east_sums]
    north_next = [north_face[t + 1] + lane_shift(north_face[t + 1], stride) for t in firsts]
    return (east_next, west_next, north_next), [value + lane_shift(value, stride) for value in term_sums]


def all_coefficients(depth, source_term, across, along):
    faces = fine_faces(depth, across, along)
    levels = []
    for level in range(LEVELS):
        levels.append(coefficients(level, faces, source_term) + (source_term,))
        if level < LEVELS - 1:
            faces, source_term = next_coefficients(level, faces, source_term)
    return levels


def level_down(level, faces, inverse, diagonal, source, sides):
    stride = 1 << level
    count = len(source)
    field = [inverse[t] * source[t] for t in range(count)]
    for k in range(SWEEPS - 1):
        if k == 0 and sides is not None:
            east_face, west_face, north_face = faces
            plus, minus = sides
            upward = [north_face[t] * field[t] for t in range(count)]
            around = [
                (
                    east_face[t] * (lane_shift(inverse[t], stride) * plus[t])
                    + west_face[t] * (lane_shift(inverse[t], -stride) * minus[t])
                )
                + (north_face[t] * north_of(field, t) + south_of(upward, t))
                for t in range(count)
            ]
            field = [(1.0 - DAMPING) * field[t] + inverse[t] * (source[t] + around[t]) for t in range(count)]
        else:
            field = sweep(field, source, inverse, faces, stride)
    return field, remainder(field, source, diagonal, faces, stride)


def level_next(level, image):
    stride = 1 << level
    left = [image[t] + image[t + 1] for t in range(0, len(image), 2)]
    source = [value + lane_shift(value, stride) for value in left]
    if left[0].shape[1] > LANES:
        return source, None
    plus = [lane_shift(value, 2 * stride) + lane_shift(value, 3 * stride) for value in left]
    minus = [lane_shift(value, -2 * stride) + lane_shift(value, -stride) for value in left]
    return source, (plus, minus)


def lay_out(lat_count, own_ref, lat_near_ref, lat_far_ref, lat_rest_ref, west_ref, west_near_ref, west_far_ref, scale_ref, grid_ref):
    rows, cols = own_ref.shape[1], own_ref.shape[2]
    columns, height = grid_ref.shape[1], grid_ref.shape[2]
    count = height // TILE
    own_columns = cols // LANES
    halo = (height - rows) // 2
    lat_index = lax.axis_index("lat")
    lat_odd = lax.rem(lat_index, 2)
    near_row = rows + pl.multiple_of(lat_odd * halo, TILE)
    far_row = rows + pl.multiple_of((1 - lat_odd) * halo, TILE)
    near_part = pl.ds(pl.multiple_of(lat_odd * (HALO - halo), TILE), halo)
    far_part = pl.ds(pl.multiple_of((1 - lat_odd) * (HALO - halo), TILE), halo)
    last = LANES // HALO - 1
    at_end = (lat_index == 0) | (lat_index == lat_count - 1)

    def inside(value, far):
        return jnp.where(jnp.broadcast_to(at_end, value.shape), 0.0, value) if far else value

    parts = (
        (0, rows, None, west_ref[...], False),
        (near_row, halo, lat_near_ref.at[near_part], west_near_ref[near_part, :], False),
        (far_row, halo, lat_far_ref, west_far_ref[far_part, :], True),
    )
    for first, size, body_ref, west, far in parts:
        slot = iota((size, LANES), 1) // HALO
        for f in range(FIELDS):
            for c in range(own_columns):
                part = slice(f * cols + c * LANES, f * cols + (c + 1) * LANES)
                if far and halo > REACH:
                    seam = far_row + pl.multiple_of((1 - lat_odd) * (halo - REACH), TILE)
                    rest = far_row + pl.multiple_of(lat_odd * REACH, TILE)
                    grid_ref[f, c, pl.ds(seam, REACH), :] = inside(lat_far_ref[:, part], far)
                    grid_ref[f, c, pl.ds(rest, halo - REACH), :] = inside(lat_rest_ref[:, part], far)
                    continue
                if body_ref is None:
                    value = own_ref[f, :, c * LANES : (c + 1) * LANES]
                else:
                    value = body_ref[:, part]
                grid_ref[f, c, pl.ds(first, size), :] = inside(value, far)
            side = jnp.where(slot == (f + last) % (last + 1), west, 0.0)
            grid_ref[f, own_columns, pl.ds(first, size), :] = inside(lane_shift(side, f * HALO), far)

    def load(f):
        return [
            jnp.concatenate(
                [grid_ref[f, c, pl.ds(t, TILE, stride=count), :] for c in range(columns)], axis=1
            )
            for t in range(count)
        ]

    depth, source_term, source = load(0), load(1), load(2)
    across = [jnp.concatenate([scale_ref[0, t]] * columns, axis=1) for t in range(count)]
    along = [jnp.concatenate([scale_ref[1, t]] * columns, axis=1) for t in range(count)]
    return depth, source_term, source, across, along


def way_down(depth, source_term, source, across, along, put):
    levels = all_coefficients(depth, source_term, across, along)
    sides = None
    for level, (faces, inverse, diagonal, _) in enumerate(levels):
        field, image = level_down(level, faces, inverse, diagonal, source, sides)
        swept = sweep(field, source, inverse, faces, 1 << level)
        put(level, faces + (inverse, source, swept) + ((diagonal,) if level == 0 else ()))
        if level < LEVELS - 1:
            source, sides = level_next(level, image)


def split_refs(rest):
    level_refs = [list(rest[KEPT * i : KEPT * i + KEPT]) for i in range(LEVELS)]
    level_refs[0].append(rest[KEPT * LEVELS])
    return level_refs, rest[KEPT * LEVELS + 1 :]


def hold(lat_count, own_ref, lat_near_ref, lat_far_ref, lat_rest_ref, west_ref, west_near_ref, west_far_ref, scale_ref, *rest):
    level_refs, (raw_ref, grid_ref) = split_refs(rest)
    values = lay_out(lat_count, own_ref, lat_near_ref, lat_far_ref, lat_rest_ref, west_ref, west_near_ref, west_far_ref, scale_ref, grid_ref)
    cols = own_ref.shape[2]
    for f in range(FIELDS):
        for t, value in enumerate(values[f]):
            raw_ref[f, t] = value[:, cols - LANES : cols]

    def put(level, kept):
        for ref, tiles in zip(level_refs[level], kept):
            keep(ref, tiles)

    way_down(*values, put)


def patch(lat_count, raw_ref, east_ref, scale_ref, *rest):
    half = len(rest) // 2
    held_refs, _ = split_refs(rest[:half])
    level_refs, (strip_ref,) = split_refs(rest[half:])
    count = raw_ref.shape[1]
    height = count * TILE
    rows = height - 2 * HALO
    lat_index = lax.axis_index("lat")
    lat_odd = lax.rem(lat_index, 2)
    near_row = rows + pl.multiple_of(lat_odd * HALO, HALO)
    far_row = rows + pl.multiple_of((1 - lat_odd) * HALO, HALO)
    at_end = (lat_index == 0) | (lat_index == lat_count - 1)
    for first, at, size, far in ((0, 0, rows, False), (near_row, rows, HALO, False), (far_row, rows + HALO, HALO, True)):
        side = east_ref[pl.ds(at, size), :]
        if far:
            side = jnp.where(jnp.broadcast_to(at_end, side.shape), 0.0, side)
        for f in range(FIELDS):
            strip_ref[f, pl.ds(first, size), :] = lane_shift(side, f * HALO)
    lane = iota((TILE, LANES), 1)
    own = lane >= LANES // 2
    fields = [
        [
            jnp.where(own, raw_ref[f, t],
                      jnp.where(lane < HALO, strip_ref[f, pl.ds(t, TILE, stride=count), :], 0.0))
            for t in range(count)
        ]
        for f in range(FIELDS)
    ]

    def put(level, kept):
        for held_ref, ref, tiles in zip(held_refs[level], level_refs[level], kept):
            last = ref.shape[2] - LANES
            for t, value in enumerate(tiles):
                held = held_ref[t]
                edge = jnp.where(lane >= LANES - HALO, value, held[:, last - LANES : last])
                halo = jnp.where(own, held[:, last:], value)
                ref[t] = jnp.concatenate([held[:, : last - LANES], edge, halo], axis=1)

    way_down(*fields, [scale_ref[0, t] for t in range(count)], [scale_ref[1, t] for t in range(count)], put)


def gather_edges(lat_near_ref, lat_far_ref, west_edge_ref, edge_ref):
    rows = west_edge_ref.shape[0]
    edge = slice(lat_near_ref.shape[1] - LANES, lat_near_ref.shape[1])
    edge_ref[pl.ds(0, rows), :] = west_edge_ref[...]
    edge_ref[pl.ds(rows, HALO), :] = lat_near_ref[:, edge]
    edge_ref[pl.ds(rows + HALO, REACH), :] = lat_far_ref[:, edge]
    edge_ref[pl.ds(rows + HALO + REACH, HALO - REACH), :] = lat_far_ref[:, edge.stop :]


def descend(lat_count, own_ref, lat_near_ref, lat_far_ref, west_ref, west_near_ref, west_far_ref, scale_ref,
            pack_ref, grid_ref, plain_ref):
    rows = own_ref.shape[1]
    lon_index = lax.axis_index("lon")
    cols = own_ref.shape[2]
    own_columns = cols // LANES
    columns = grid_ref.shape[1]
    depth, source_term, source, across, along = lay_out(
        lat_count, own_ref, lat_near_ref, lat_far_ref, None, west_ref, west_near_ref, west_far_ref, scale_ref, grid_ref
    )
    levels = all_coefficients(depth, source_term, across, along)
    sides = None
    for level, (faces, inverse, diagonal, source_term) in enumerate(levels):
        _, image = level_down(level, faces, inverse, diagonal, source, sides)
        if level < LEVELS - 1:
            source, sides = level_next(level, image)

    east_face, _, north_face = faces
    for f, values in enumerate((image, east_face, north_face, source_term)):
        for t, value in enumerate(values):
            for c in range(columns):
                plain_ref[f, c, pl.ds(t, TILE, stride=len(values)), :] = value[:, c * LANES : (c + 1) * LANES]
    stride = 1 << LEVELS
    bottom_rows = rows // stride
    bottom_width = cols // stride
    group = LANES // bottom_width
    per_column = LANES // stride
    lane = iota((bottom_rows, LANES), 1)
    cell = lane % bottom_width - SHIFT
    column = jnp.where(cell < 0, own_columns, cell // per_column)
    west_part = jnp.where(cell < 0, LANES + cell * stride, (cell % per_column) * stride)
    east_part = west_part + stride // 2
    turn = lax.rem(lane // bottom_width + group - lax.rem(lon_index, group), group)
    packed = jnp.zeros((bottom_rows, LANES), jnp.float32)
    for f, picks in enumerate(((west_part, east_part), (east_part,), (west_part, east_part), (west_part, east_part))):
        flat = jnp.zeros((bottom_rows, LANES), jnp.float32)
        for c in range(columns):
            value = plain_ref[f, c, pl.ds(1, bottom_rows, stride=2), :]
            if f != 2:
                value = value + plain_ref[f, c, pl.ds(0, bottom_rows, stride=2), :]
            taken = sum(jnp.take_along_axis(value, pick, axis=1) for pick in picks)
            flat = jnp.where(column == c, taken, flat)
        packed = jnp.where(turn == f, flat, packed)
    for k in range(pack_ref.shape[0]):
        pack_ref[k] = packed


def total_of(tiles):
    parts = list(tiles)
    while len(parts) > 1:
        parts = [
            parts[i] + parts[i + 1] if i + 1 < len(parts) else parts[i] for i in range(0, len(parts), 2)
        ]
    value = parts[0]
    value = sum(value[:, c : c + LANES] for c in range(0, value.shape[1], LANES))
    return jnp.sum(jnp.sum(value, axis=0, keepdims=True), axis=1, keepdims=True)


def conjugate(source, east_face, north_face, source_term):
    height = source.shape[0]

    def split(value):
        return [value[r : r + TILE] for r in range(0, height, TILE)]

    def up(value):
        return pltpu.roll(value, height - 1, 0)

    def down(value):
        return pltpu.roll(value, 1, 0)

    west_face = lane_shift(east_face, -1)
    south_face = down(north_face)
    diagonal = source_term + ((east_face + west_face) + (north_face + south_face))

    def apply(value):
        return diagonal * value - (
            (east_face * lane_shift(value, 1) + west_face * lane_shift(value, -1))
            + (north_face * up(value) + south_face * down(value))
        )

    iterate = jnp.zeros_like(source)
    remain = source
    image_r = apply(source)
    direction = image_d = second = None
    over_norm = over_step = None
    for step in range(BOTTOM_ITERS):
        norm = total_of(split(remain * remain))
        energy = total_of(split(remain * image_r))
        last = step == BOTTOM_ITERS - 1
        ahead = None if last else apply(image_r)
        if step == 0:
            direction, image_d, second = remain, image_r, ahead
        else:
            ratio = norm * over_norm
            energy = energy - ratio * (norm * over_step)
            direction = remain + ratio * direction
            if not last:
                image_d = image_r + ratio * image_d
                second = ahead + ratio * second
        step_size = norm / energy
        over_norm = 1.0 / norm
        over_step = energy * over_norm
        iterate = iterate + step_size * direction
        if not last:
            remain = remain - step_size * image_d
            image_r = image_r - step_size * second
    return iterate


def ascend(lat_count, lon_count, blocks_ref, *rest):
    level_refs = [rest[KEPT * i : KEPT * i + KEPT] for i in range(LEVELS)]
    diagonal_ref, solution_ref, residual_ref, window_ref, order_ref, sems = rest[KEPT * LEVELS :]
    lon_index = lax.axis_index("lon")
    lat_index = lax.axis_index("lat")
    rows, cols = solution_ref.shape
    count, width = diagonal_ref.shape[0], diagonal_ref.shape[2]
    own_columns = cols // LANES
    columns = width // LANES
    stride = 1 << LEVELS
    bottom_rows = rows // stride
    bottom_width = cols // stride
    group = LANES // bottom_width
    slot = iota((bottom_rows, LANES), 1) // bottom_width
    fields = []
    for f in range(4):
        strips = []
        for a in range(lat_count):
            pieces = []
            for c in range(lon_count // group):
                merged = None
                for j in range(group):
                    block = blocks_ref[a * lon_count + c * group + j]
                    merged = block if merged is None else jnp.where(slot == (f + j) % group, block, merged)
                pieces.append(lane_shift(merged, f * bottom_width))
            strips.append(jnp.concatenate(pieces, axis=1))
        fields.append(jnp.concatenate(strips, axis=0))
    iterate = conjugate(*fields)

    bottom_height = lat_count * bottom_rows
    whole_width = lon_count * bottom_width
    pad = 2 * TILE
    window_ref[pl.ds(0, pad), :] = jnp.zeros((pad, LANES), jnp.float32)
    window_ref[pl.ds(pad + bottom_height, pad), :] = jnp.zeros((pad, LANES), jnp.float32)
    half = LANES // 2
    margin = half // stride
    shift = lax.rem(margin - SHIFT - lon_index * bottom_width + whole_width, whole_width)
    window_ref[pl.ds(pad, bottom_height), :] = pltpu.roll(iterate, shift, 1)[:, :LANES]
    start = pl.multiple_of(lat_index * bottom_rows, TILE)
    tiles = count >> LEVELS
    lane = iota((TILE, LANES), 1)
    ahead = (rows + HALO) // stride // tiles
    sublane = iota((TILE, LANES), 0)
    step = 1 << (LEVELS - 1)
    center, plus, minus = [], [], []
    for t in range(tiles):
        upper = window_ref[pl.ds(start + pad + t, TILE, stride=tiles), :]
        lower = window_ref[pl.ds(start + pad + t - tiles * TILE, TILE, stride=tiles), :]
        value = jnp.where(sublane < ahead, upper, lower)
        for target, move in ((center, 0), (plus, step), (minus, -step)):
            parts = []
            for c in range(columns):
                place = c * LANES + lane + (move + width)
                place = jnp.where(place >= width, place - width, place)
                place = jnp.where(place >= width, place - width, place)
                pick = jnp.where(place < cols + half, margin + place // stride, (place - (cols + half)) // stride)
                parts.append(jnp.take_along_axis(value, pick, axis=1))
            target.append(jnp.concatenate(parts, axis=1))

    lane = iota((TILE, width), 1)
    for level in range(LEVELS - 1, -1, -1):
        stride = 1 << level
        east_face, west_face, north_face, inverse, source, swept = map(tiles_of, level_refs[level])
        faces = (east_face, west_face, north_face)
        if level < LEVELS - 1:
            first = lax.rem(lane // stride, 2) == 0
            east = [lane_shift(value, stride) for value in field]
            west = [lane_shift(value, -stride) for value in field]
            west_two = [lane_shift(value, -2 * stride) for value in field]
            coarse = range(len(field))
            center = [jnp.where(first, field[t], west[t]) for t in coarse]
            plus = [jnp.where(first, field[t], east[t]) for t in coarse]
            minus = [jnp.where(first, west_two[t], west[t]) for t in coarse]
        spread = [center[t // 2] for t in range(count >> level)]
        field = []
        for t in range(count >> level):
            around = (east_face[t] * plus[t // 2] + west_face[t] * minus[t // 2]) + (
                north_face[t] * north_of(spread, t) + south_of(north_face, t) * south_of(spread, t)
            )
            here = spread[t]
            if level == 0:
                here = jnp.where(east_face[t] + north_face[t] > 0.0, here, 0.0)
            field.append(swept[t] + ((1.0 - DAMPING) * here + inverse[t] * around))
        for _ in range(SWEEPS - 1):
            field = sweep(field, source, inverse, faces, stride)
    correction = field
    own_sublanes = rows // count

    def send_out(k, ref, tiles):
        copies = []
        for c in range(own_columns):
            part = slice(c * LANES, (c + 1) * LANES)
            for t in range(count):
                order_ref[k, c, pl.ds(t, own_sublanes, stride=count), :] = tiles[t][:own_sublanes, part]
            copies.append(pltpu.make_async_copy(order_ref.at[k, c], ref.at[:, part], sems.at[k, c]))
            copies[-1].start()
        return copies

    copies = send_out(0, solution_ref, correction)
    final = remainder(correction, source, tiles_of(diagonal_ref), faces, 1)
    copies += send_out(1, residual_ref, final)
    for copy in copies:
        copy.wait()


def near_pairs(lat_count):
    return [(a, a ^ 1) for a in range(lat_count)]


def far_pairs(lon_count, lat_count, east):
    pairs = []
    for i in range(lon_count):
        for a in range(lat_count):
            b = a + 1 if a % 2 else a - 1
            j = (i + east) % lon_count
            if b < 0 or b == lat_count:
                b, j = a, i ^ 1
            pairs.append((i * lat_count + a, j * lat_count + b))
    return pairs


def on_device(lat_count, lon_count, forcing, surface_term, sea_cells, levels):
    rows, cols = forcing.shape
    height, width = rows + 2 * HALO, cols + LANES
    count = height // TILE
    f32 = jnp.float32
    vmem = pl.BlockSpec(memory_space=pltpu.VMEM)
    hbm = pl.BlockSpec(memory_space=pltpu.HBM)
    params = pltpu.CompilerParams(vmem_limit_bytes=VMEM_LIMIT)
    lat_index = lax.axis_index("lat").astype(jnp.int32)
    inputs = [
        pltpu.with_memory_space_constraint(x, pltpu.HBM) for x in (forcing, surface_term, sea_cells, levels)
    ]
    own, east_edge, west_edge = pl.pallas_call(
        prepare,
        out_shape=[
            jax.ShapeDtypeStruct((FIELDS, rows, cols), f32),
            jax.ShapeDtypeStruct((rows, LANES), f32),
            jax.ShapeDtypeStruct((rows, LANES), f32),
        ],
        in_specs=[hbm] * 4,
        out_specs=[vmem] * 3,
        scratch_shapes=[
            pltpu.VMEM((rows, cols), f32),
            pltpu.VMEM((rows, cols), f32),
            pltpu.VMEM((rows, cols), jnp.int32),
            pltpu.VMEM((rows, cols), jnp.int32),
            pltpu.SemaphoreType.DMA((4,)),
        ],
        compiler_params=params,
        name="prepare",
    )(*inputs)

    lat_near, lat_far = pl.pallas_call(
        prepare_rows,
        out_shape=[
            jax.ShapeDtypeStruct((HALO, FIELDS * cols + LANES), f32),
            jax.ShapeDtypeStruct((REACH, FIELDS * cols + 2 * LANES), f32),
        ],
        in_specs=[vmem] * 2,
        out_specs=[vmem] * 2,
        compiler_params=params,
        name="prepare_rows",
    )(own, west_edge)

    diagonal_edge = pl.pallas_call(
        prepare_corner,
        out_shape=jax.ShapeDtypeStruct((HALO, LANES), f32),
        in_specs=[vmem],
        out_specs=vmem,
        compiler_params=params,
        name="prepare_corner",
    )(east_edge)
    lat_rest = pl.pallas_call(
        prepare_rest,
        out_shape=jax.ShapeDtypeStruct((HALO - REACH, FIELDS * cols), f32),
        in_specs=[vmem] * 2,
        out_specs=vmem,
        compiler_params=params,
        name="prepare_rest",
    )(own, diagonal_edge)

    eastward = [(i, (i + 1) % lon_count) for i in range(lon_count)]
    westward = [(target, source) for source, target in eastward]
    west_halo = lax.ppermute(east_edge, "lon", eastward)
    lat_far = lax.ppermute(lat_far, ("lon", "lat"), far_pairs(lon_count, lat_count, 0))
    west_far = lax.ppermute(diagonal_edge, ("lon", "lat"), far_pairs(lon_count, lat_count, 1))
    lat_near = lax.ppermute(lat_near, "lat", near_pairs(lat_count))
    lat_rest, west_halo = lax.optimization_barrier((lat_rest, west_halo))
    lat_rest = lax.ppermute(lat_rest, ("lon", "lat"), far_pairs(lon_count, lat_count, 0))
    odd = lat_index % 2 == 1
    west_near = lax.ppermute(
        jnp.where(odd, west_halo[:HALO], west_halo[rows - HALO :]), "lat", near_pairs(lat_count)
    )

    def scales(halo):
        tall = rows + 2 * halo
        tiles = tall // TILE
        row = jnp.arange(TILE)[None, :] * tiles + jnp.arange(tiles)[:, None]
        row = jnp.where(row < rows + halo, row, row - tall).astype(f32) + (lat_index * rows).astype(f32)
        center, northern = metric(row)
        return jnp.broadcast_to(jnp.stack([1.0 / center, northern])[..., None], (2, tiles, TILE, LANES))

    devices = lat_count * lon_count
    grid = pltpu.VMEM((FIELDS, width // LANES, height, LANES), f32)
    edges = pl.pallas_call(
        gather_edges,
        out_shape=jax.ShapeDtypeStruct((height, LANES), f32),
        in_specs=[vmem] * 3,
        out_specs=vmem,
        compiler_params=params,
        name="gather_edges",
    )(lat_near, lat_far, west_edge)
    packed = pl.pallas_call(
        functools.partial(descend, lat_count),
        out_shape=[
            jax.ShapeDtypeStruct((devices, rows >> LEVELS, LANES), f32),
        ],
        in_specs=[vmem] * 7,
        out_specs=[vmem] * 1,
        scratch_shapes=[
            pltpu.VMEM((FIELDS, width // LANES, rows + 2 * REACH, LANES), f32),
            pltpu.VMEM((4, width // LANES, (rows + 2 * REACH) >> (LEVELS - 1), LANES), f32),
        ],
        compiler_params=params,
        name="descend",
    )(own, lat_near, lat_far, west_halo, west_near, west_far, scales(REACH))[0]
    east_halo = lax.ppermute(edges, "lon", westward)
    packed, lat_rest = lax.optimization_barrier((packed, lat_rest))
    blocks = lax.all_to_all(packed, ("lat", "lon"), 0, 0, tiled=True)

    level_shapes = []
    for level in range(LEVELS):
        level_shapes += [jax.ShapeDtypeStruct((count >> level, TILE, width), f32)] * KEPT
    held_shapes = level_shapes + [jax.ShapeDtypeStruct((count, TILE, width), f32)]
    fine_scale = scales(HALO)
    held = pl.pallas_call(
        functools.partial(hold, lat_count),
        out_shape=held_shapes + [jax.ShapeDtypeStruct((FIELDS, count, TILE, LANES), f32)],
        in_specs=[vmem] * 8,
        out_specs=[vmem] * (1 + len(held_shapes)),
        scratch_shapes=[grid],
        compiler_params=params,
        name="hold",
    )(own, lat_near, lat_far, lat_rest, west_halo, west_near, west_far, fine_scale)
    held, raw = held[:-1], held[-1]
    held = pl.pallas_call(
        functools.partial(patch, lat_count),
        out_shape=held_shapes,
        in_specs=[vmem] * (3 + len(held_shapes)),
        out_specs=[vmem] * len(held_shapes),
        scratch_shapes=[pltpu.VMEM((FIELDS, height, LANES), f32)],
        compiler_params=params,
        name="patch",
    )(raw, east_halo, fine_scale, *held)

    return pl.pallas_call(
        functools.partial(ascend, lat_count, lon_count),
        out_shape=[jax.ShapeDtypeStruct((rows, cols), f32)] * 2,
        in_specs=[vmem] * (1 + len(held)),
        out_specs=[hbm] * 2,
        scratch_shapes=[
            pltpu.VMEM((lat_count * (rows >> LEVELS) + 4 * TILE, LANES), f32),
            pltpu.VMEM((2, cols // LANES, rows, LANES), f32),
            pltpu.SemaphoreType.DMA((2, cols // LANES)),
        ],
        compiler_params=params,
        name="ascend",
    )(blocks, *held)


def solution(mesh):
    body = functools.partial(on_device, mesh.shape["lat"], mesh.shape["lon"])
    return jax.shard_map(
        body,
        mesh=mesh,
        in_specs=(P("lat", "lon"),) * 4,
        out_specs=(P("lat", "lon"),) * 2,
        check_vma=False,
    )
```
